32 devices in a mesh: rows: 8 (over y, x, core), ang: 4 (over z).
Axes of the slice: x: 2, y: 2, z: 4, core: 2. Of those that a mesh axis runs over, the one named last changes fastest.
Arguments:
- delta_obj: float32 [1088, 2, 512], P('rows', None, 'ang'), may hold values from -4 to 4
- beta_obj: float32 [1088, 2, 512], P('rows', None, 'ang'), may hold values from 0 to 0.15
- layer_shifts: int32 [4, 2], replicated, may hold values from -8 to 8
- illumination_field: float32 [2, 128, 128], replicated, may hold values from -6 to 6
- amplitudes: float32 [4, 32, 128, 128], P('ang', 'rows'), may hold values from 0.2 to 3
- positions: int32 [4, 32, 2], P('ang', 'rows'), may hold values from 0 to 384, as said below
- scan_counts: int32 [4, 8], P('ang', 'rows'), may hold values from 1 to 4, as said below
Outputs:
- grad_delta: float32 [1088, 2, 512], P('rows', None, 'ang')
- grad_beta: float32 [1088, 2, 512], P('rows', None, 'ang')
The draws below stay inside these ranges and needn't reach their ends.
Inputs may be any that keep to these rules, and one draw needn't show every extreme that they name: `positions`: within each tile at each angle the slots come in order: a first group, at most 1 of them, has row offsets above 8; all later slots have row offsets of at most 8. Columns are at most 384. `scan_counts`: slots of a tile from this number on are not used.
All inputs are finite; a program needn't handle non-finite values.
Results may differ from the reference program's by a relative error of at most 0.0046.
Values may be sent and summed in bfloat16 or wider, within the bound.
No kernel may reach another device: no remote copies, remote signals or barrier semaphores. Data moves between devices by JAX's collectives and lax.ppermute only.
A program may use at most 64 MiB of HBM per device.

```python
import math
import jax
import jax.numpy as jnp
from jax import lax

PATTERN_PIXELS = 128
TH = 136
COLS_DEV = 128
LAYERS = 2
SHIFT = 8
SCAN_SLOT_LIMIT = 4
EDGE_CAP = 1
TILE_COUNT = 8
ANGLES = 4
HEIGHT = 1088
WIDTH = 512
SCANS = 32
N_ANG = 4


def scan_plan(key):
    keys = jax.random.split(jax.random.fold_in(key, 11), 9)
    grid_shape = (ANGLES, TILE_COUNT)
    rare = jax.random.randint(keys[0], grid_shape, 0, 8) == 0
    heavy = jax.random.randint(keys[1], grid_shape, SCAN_SLOT_LIMIT // 2, SCAN_SLOT_LIMIT + 1)
    light = jax.random.randint(keys[2], grid_shape, 1, SCAN_SLOT_LIMIT // 2 + 1)
    scan_totals = jnp.where(rare, heavy, light)
    pick_angle = jax.random.randint(keys[3], (), 0, ANGLES)
    pick_tile = jax.random.randint(keys[4], (), 0, TILE_COUNT)
    chosen = (jnp.arange(ANGLES)[:, None] == pick_angle) & (jnp.arange(TILE_COUNT)[None, :] == pick_tile)
    scan_totals = jnp.where(chosen, SCAN_SLOT_LIMIT, scan_totals)
    edges = jnp.minimum(jax.random.randint(keys[5], grid_shape, 0, EDGE_CAP + 1), scan_totals)
    edges = jnp.where(chosen, EDGE_CAP, edges)
    return (scan_totals.astype(jnp.int32), edges.astype(jnp.int32), chosen, keys)


def draw_scan_counts(key, part):
    scan_totals, edges, chosen, keys = scan_plan(key)
    return scan_totals


def draw_positions(key, part):
    scan_totals, edges, chosen, keys = scan_plan(key)
    slot_ids = jnp.arange(SCAN_SLOT_LIMIT)
    full_shape = (ANGLES, TILE_COUNT, SCAN_SLOT_LIMIT)
    is_edge = slot_ids[None, None, :] < edges[:, :, None]
    inner = jax.random.randint(keys[6], full_shape, 0, TH - PATTERN_PIXELS + 1)
    outer = jax.random.randint(keys[7], full_shape, TH - PATTERN_PIXELS + 1, TH)
    row_off = jnp.where(is_edge, outer, inner)
    col_off = jax.random.randint(keys[8], full_shape, 0, WIDTH - PATTERN_PIXELS + 1)
    first = chosen[:, :, None] & (slot_ids == 0)[None, None, :]
    row_off = jnp.where(first, TH - 1, row_off)
    col_off = jnp.where(first, WIDTH - PATTERN_PIXELS, col_off)
    return jnp.stack([row_off, col_off], -1).reshape(ANGLES, SCANS, 2).astype(jnp.int32)


def draw_layer_shifts(key, part):
    shifts = jax.random.randint(jax.random.fold_in(key, 23), (ANGLES, LAYERS), -SHIFT, SHIFT + 1)
    shifts = shifts.at[0, 0].set(SHIFT)
    shifts = shifts.at[0, 1].set(-SHIFT)
    return shifts.astype(jnp.int32)


def level_of(own_key, dims, cuts, least, largest):
    def one(dim, parts):
        heights = jax.random.uniform(jax.random.fold_in(jax.random.fold_in(own_key, 6), dim), (parts,), jnp.float32, least / len(cuts), largest / len(cuts))
        return jnp.repeat(jnp.exp(heights), dims[dim] // parts).reshape((-1,) + (1,) * (len(dims) - dim - 1))

    level = one(*cuts[0])
    for cut in cuts[1:]:
        level = level * one(*cut)
    return level


def gaussian(rng, extent, width, bound, cuts=(), held_as=jnp.bfloat16):
    loudness = level_of(rng, extent, cuts, -0.22, 0.18) if cuts else 1.0
    entries = jax.random.normal(rng, extent, jnp.float32) * width * loudness
    return jnp.minimum(jnp.maximum(entries, -bound), bound).astype(held_as)


def setup_inputs(seed: int = 0) -> dict:
    key_list = jax.random.split(jax.random.key(seed), 8)
    delta_obj = gaussian(key_list[0], (HEIGHT, LAYERS, WIDTH), 0.3, 4.0, ((0, 8), (2, 4)), jnp.float32)
    beta_obj = jnp.clip(0.15 * jax.random.uniform(key_list[1], (HEIGHT, LAYERS, WIDTH), jnp.float32) ** level_of(key_list[1], (HEIGHT, LAYERS, WIDTH), ((0, 8), (2, 4)), -0.2, 0.2), 0.0, 0.15)
    layer_shifts = draw_layer_shifts(jax.random.fold_in(key_list[7], 71), 0)
    illumination_field = gaussian(key_list[3], (2, PATTERN_PIXELS, PATTERN_PIXELS), 1.0, 6.0, (), jnp.float32)
    amplitudes = jnp.clip(jnp.exp(math.log(3.0) - 2.7080502 * jax.random.uniform(key_list[4], (ANGLES, SCANS, PATTERN_PIXELS, PATTERN_PIXELS), jnp.float32) ** level_of(key_list[4], (ANGLES, SCANS, PATTERN_PIXELS, PATTERN_PIXELS), ((0, 4), (1, 8)), -0.2, 0.2)), 0.2, 3.0)
    positions = draw_positions(jax.random.fold_in(key_list[7], 71), 0)
    scan_counts = draw_scan_counts(jax.random.fold_in(key_list[7], 71), 0)
    return dict(delta_obj=delta_obj, beta_obj=beta_obj, layer_shifts=layer_shifts, illumination_field=illumination_field, amplitudes=amplitudes, positions=positions, scan_counts=scan_counts)


best_prec = lax.Precision.HIGHEST
amp_floor = 0.1

def dft_tables():
    counter = jnp.arange(PATTERN_PIXELS, dtype=jnp.int32)
    product = counter[:, None] * counter[None, :] % PATTERN_PIXELS
    angle_table = product.astype(jnp.float32) * (2.0 * math.pi / PATTERN_PIXELS)
    factor = 1.0 / math.sqrt(PATTERN_PIXELS)
    return (jnp.cos(angle_table) * factor, -jnp.sin(angle_table) * factor)

def transform(real_in, imag_in, fourier_real, fourier_imaginary):
    left_re = jnp.matmul(fourier_real, real_in, precision=best_prec) - jnp.matmul(fourier_imaginary, imag_in, precision=best_prec)
    left_im = jnp.matmul(fourier_real, imag_in, precision=best_prec) + jnp.matmul(fourier_imaginary, real_in, precision=best_prec)
    out_re = jnp.matmul(left_re, fourier_real, precision=best_prec) - jnp.matmul(left_im, fourier_imaginary, precision=best_prec)
    out_im = jnp.matmul(left_re, fourier_imaginary, precision=best_prec) + jnp.matmul(left_im, fourier_real, precision=best_prec)
    return (out_re, out_im)

def scan_gradients(object_patches, illumination_field, measured_patterns, misfit_weight, fourier_real, fourier_imaginary):
    probe_re = illumination_field[0]
    probe_im = illumination_field[1]
    patch_re = object_patches[:, 0]
    patch_im = object_patches[:, 1]
    exit_re = probe_re * patch_re - probe_im * patch_im
    exit_im = probe_re * patch_im + probe_im * patch_re
    far_re, far_im = transform(exit_re, exit_im, fourier_real, fourier_imaginary)
    modulus = jnp.sqrt(far_re * far_re + far_im * far_im)
    factor = (1.0 - measured_patterns / jnp.maximum(modulus, amp_floor)) * misfit_weight[:, None, None]
    back_re, back_im = transform(far_re * factor, far_im * factor, fourier_real, -fourier_imaginary)
    return jnp.stack([probe_re * back_re + probe_im * back_im, probe_re * back_im - probe_im * back_re], axis=1)

def transmit(phase_in, absorb_in):
    damping = jnp.exp(-absorb_in)
    return (damping * jnp.cos(phase_in), damping * jnp.sin(phase_in))

def chain_back(trans_re, trans_im, grad_re, grad_im):
    return (trans_re * grad_im - trans_im * grad_re, -(trans_re * grad_re + trans_im * grad_im))

def assemble(windows, columns, margin):
    leading = windows.shape[:2]
    groups = windows.shape[2]
    full_width = groups * columns
    main_part = windows[..., :columns].reshape(leading + (full_width,))
    tail_part = jnp.pad(windows[..., columns:], ((0, 0), (0, 0), (0, 0), (0, columns - 2 * margin)))
    tail_part = tail_part.reshape(leading + (full_width,))
    padding = jnp.zeros(leading + (columns,), windows.dtype)
    extended = jnp.concatenate([main_part, padding], -1) + jnp.concatenate([padding, tail_part], -1)
    result = extended[..., margin:margin + full_width]
    result = result.at[..., full_width - margin:].add(extended[..., :margin])
    result = result.at[..., :columns - margin].add(extended[..., full_width + margin:])
    return result

def cut_windows(gradient, columns, margin):
    leading = gradient.shape[:2]
    full_width = gradient.shape[2]
    groups = full_width // columns
    extended = jnp.concatenate([gradient[..., full_width - margin:], gradient, gradient[..., :columns - margin]], -1)
    main_part = extended[..., :full_width].reshape(leading + (groups, columns))
    tail_part = extended[..., columns:full_width + columns].reshape(leading + (groups, columns))[..., :2 * margin]
    return jnp.concatenate([main_part, tail_part], -1)

def scan_angle(transmission, measured_patterns, spot_list, scan_totals, illumination_field, fourier_real, fourier_imaginary):
    tile_measured = measured_patterns.reshape(TILE_COUNT, SCAN_SLOT_LIMIT, PATTERN_PIXELS, PATTERN_PIXELS)
    tile_positions = spot_list.reshape(TILE_COUNT, SCAN_SLOT_LIMIT, 2)

    def tile_update(grad_trans, input_bundle):
        tile_index, measured_tile, position_tile, active_count = input_bundle
        row_start = tile_index * TH + position_tile[:, 0]
        col_start = position_tile[:, 1]
        object_patches = jax.vmap(lambda r_pos, c_pos: lax.dynamic_slice(transmission, (jnp.int32(0), r_pos, c_pos), (2, PATTERN_PIXELS, PATTERN_PIXELS)))(row_start, col_start)
        misfit_weight = (jnp.arange(SCAN_SLOT_LIMIT, dtype=jnp.int32) < active_count).astype(jnp.float32)
        patch_gradient = scan_gradients(object_patches, illumination_field, measured_tile, misfit_weight, fourier_real, fourier_imaginary)

        def add_one(slot_idx, total):
            anchor = (jnp.int32(0), row_start[slot_idx], col_start[slot_idx])
            current = lax.dynamic_slice(total, anchor, (2, PATTERN_PIXELS, PATTERN_PIXELS))
            return lax.dynamic_update_slice(total, current + patch_gradient[slot_idx], anchor)
        return (lax.fori_loop(0, SCAN_SLOT_LIMIT, add_one, grad_trans), None)
    tile_numbers = jnp.arange(TILE_COUNT, dtype=jnp.int32)
    return lax.scan(tile_update, jnp.zeros_like(transmission), (tile_numbers, tile_measured, tile_positions, scan_totals))[0]

def reference(delta_obj, beta_obj, layer_shifts, illumination_field, amplitudes, positions, scan_counts):
    height, layers, full_width = delta_obj.shape
    window_len = COLS_DEV + 2 * SHIFT
    blocks = jnp.stack([delta_obj, beta_obj]).reshape(2, height, layers, N_ANG, COLS_DEV)
    blocks = jnp.pad(blocks, ((0, 0), (0, 0), (0, 0), (0, 0), (2 * SHIFT, 2 * SHIFT)))
    fourier_real, fourier_imaginary = dft_tables()

    def angle_step(grad_obj, input_bundle):
        shift_row, measured_patterns, spot_list, scan_totals = input_bundle

        def add_layer(layer_idx, total):
            layer_slab = lax.dynamic_index_in_dim(blocks, layer_idx, 2, keepdims=False)
            return total + lax.dynamic_slice_in_dim(layer_slab, SHIFT + shift_row[layer_idx], window_len, 3)
        windows = lax.fori_loop(0, layers, add_layer, jnp.zeros((2, height, N_ANG, window_len), jnp.float32))
        windows = lax.optimization_barrier(windows.astype(jnp.bfloat16)).astype(jnp.float32)
        projection = assemble(windows, COLS_DEV, SHIFT)
        extended = jnp.pad(projection, ((0, 0), (0, PATTERN_PIXELS), (0, 0)))
        trans_re, trans_im = transmit(extended[0], extended[1])
        grad_trans = scan_angle(jnp.stack([trans_re, trans_im]), measured_patterns, spot_list, scan_totals, illumination_field, fourier_real, fourier_imaginary)
        grad_phase, grad_absorb = chain_back(trans_re, trans_im, grad_trans[0], grad_trans[1])
        grad_proj = jnp.stack([grad_phase, grad_absorb])[:, :height]
        grad_win = cut_windows(grad_proj, COLS_DEV, SHIFT)
        grad_win = lax.optimization_barrier(grad_win.astype(jnp.bfloat16)).astype(jnp.float32)

        def back_layer(layer_idx, total):
            layer_part = lax.dynamic_slice_in_dim(grad_win, SHIFT - shift_row[layer_idx], COLS_DEV, 3)
            layer_part = layer_part.reshape(2, height, full_width)
            current = lax.dynamic_index_in_dim(total, layer_idx, 2, keepdims=False)
            return lax.dynamic_update_index_in_dim(total, current + layer_part, layer_idx, 2)
        return (lax.fori_loop(0, layers, back_layer, grad_obj), None)
    start_grad = jnp.zeros((2, height, layers, full_width), jnp.float32)
    grad_obj = lax.scan(angle_step, start_grad, (layer_shifts, amplitudes, positions, scan_counts))[0]
    return (grad_obj[0], grad_obj[1])
```

```python
import functools
import math

import jax
import jax.numpy as jnp
import ml_dtypes
import numpy as np
from jax import lax
from jax.experimental import pallas as pl
from jax.experimental.pallas import tpu as pltpu
from jax.sharding import PartitionSpec as P

N = 128
SHIFT = 8
AMP_FLOOR = 0.1
PACK_ROWS = 48
EDGE_ROWS = 8

f32, bf16, i32 = jnp.float32, jnp.bfloat16, jnp.int32
SMEM = pl.BlockSpec(memory_space=pltpu.SMEM)
VMEM = pl.BlockSpec(memory_space=pltpu.VMEM)


def fourier_tables():
    counter = np.arange(N)
    angle = (counter[:, None] * counter[None, :] % N) * (2.0 * math.pi / N)
    re, im = np.cos(angle) / math.sqrt(N), -np.sin(angle) / math.sqrt(N)
    right = np.block([[re, im], [-im, re]])
    tables = []
    for table in (right, right.T):
        high = table.astype(ml_dtypes.bfloat16)
        tables += [high, (table - high.astype(np.float64)).astype(ml_dtypes.bfloat16)]
    return np.stack(tables)


def lane_iota(rows):
    return lax.broadcasted_iota(i32, (rows, N), 1)


def roll_lanes(value, by):
    return pltpu.roll(value, by, 1)


def roll_left(value, by):
    return pltpu.roll(value, lax.rem(N - by, N), 1)


def groups_of(rows):
    return [(g, start, min(PACK_ROWS, rows - start)) for g, start in enumerate(range(0, rows, PACK_ROWS))]


def packed_message(main, margins, scratch):
    rows = main.shape[0]
    scratch[0:rows, :] = margins
    packed = None
    for g, start, _ in groups_of(rows):
        part = scratch[start : start + PACK_ROWS, :]
        part = roll_lanes(part, 16 * g) if g else part
        packed = part if packed is None else packed + part
    return jnp.concatenate([main, packed], 0).astype(bf16)


def margins_of(message, rows):
    packed = message[rows:, :]
    parts = []
    for g, _, size in groups_of(rows):
        part = roll_lanes(packed, N - 16 * g) if g else packed
        parts.append(part[:size])
    return jnp.concatenate(parts, 0)


def window_kernel(shifts, delta, beta, *refs):
    outs, scratch = refs[:-1], refs[-1]
    angles = len(outs)
    tile = delta.shape[0] // 2
    scratch[2 * tile :, :] = jnp.zeros((scratch.shape[0] - 2 * tile, N), f32)
    me = lax.axis_index("ang")
    lane = lane_iota(tile)
    for d, out in enumerate(outs):
        angle = lax.rem(me + d, angles)
        mains, margins = [], []
        for ref in (delta, beta):
            main = margin = None
            for z in range(2):
                s = shifts[angle, z]
                rolled = pltpu.roll(ref[pl.ds(z, tile, stride=2), :], lax.rem(N - s, N), 1)
                source = lane + s
                inside = (source >= 0) & (source < N)
                kept, out_of = jnp.where(inside, rolled, 0.0), jnp.where(inside, 0.0, rolled)
                main = kept if z == 0 else main + kept
                margin = out_of if z == 0 else margin + out_of
            mains.append(main)
            margins.append(margin)
        out[...] = packed_message(jnp.concatenate(mains, 0), jnp.concatenate(margins, 0), scratch)


def assemble_kernel(previous, *refs):
    proj, halo, margins = refs[-3:]
    received = refs[:-3]
    blocks = len(received)
    tile = proj.shape[2]
    me = lax.axis_index("ang")
    for d, ref in enumerate(received):
        block = lax.rem(me + (blocks - d), blocks)
        message = ref[...].astype(f32)
        proj[0, block] = message[:tile]
        proj[1, block] = message[tile : 2 * tile]
        margins[block] = margins_of(message, 2 * tile)
    lane = lane_iota(tile)
    for block in range(blocks):
        before, after = (block - 1) % blocks, (block + 1) % blocks
        for c in range(2):
            part = slice(c * tile, (c + 1) * tile)
            extra = jnp.where(lane < SHIFT, margins[before, part], 0.0)
            extra += jnp.where(lane >= N - SHIFT, margins[after, part], 0.0)
            proj[c, block] += extra
    column = previous[0, 1]
    first, offset = column // N, lax.rem(column, N)
    second = jnp.minimum(first + 1, blocks - 1)
    lane = lane_iota(N)
    for c in range(2):
        left = roll_left(proj[c, first, 0:N, :], offset)
        right = roll_left(proj[c, second, 0:N, :], offset)
        halo[c * N : (c + 1) * N, :] = jnp.where(lane < N - offset, left, right).astype(bf16)


def transmit(phase, absorb):
    turns = jnp.round(phase * (2.0 / math.pi))
    r = phase - turns * 1.5703125
    r = r - turns * 4.837512969970703125e-4
    r = r - turns * 7.54978995489188e-8
    z = r * r
    sine = r + r * z * (-1.6666654611e-1 + z * (8.3321608736e-3 - z * 1.9515295891e-4))
    cosine = 1.0 - 0.5 * z + z * z * (4.166664568298827e-2 + z * (-1.388731625493765e-3 + z * 2.443315711809948e-5))
    quarter = turns.astype(i32)
    odd = (quarter & 1) == 1
    damping = jnp.exp(-absorb)
    out_cos = jnp.where(odd, sine, cosine)
    out_sin = jnp.where(odd, cosine, sine)
    out_cos = jnp.where(((quarter + 1) & 2) == 2, -out_cos, out_cos)
    out_sin = jnp.where((quarter & 2) == 2, -out_sin, out_sin)
    return damping * out_cos, damping * out_sin


def split(value):
    high = value.astype(bf16)
    return high, (value - high.astype(f32)).astype(bf16)


def dot(a, b):
    return jnp.dot(a, b, preferred_element_type=f32)


def times_right(value, high, low):
    vh, vl = split(value)
    return dot(vh, high) + (dot(vl, high) + dot(vh, low))


def times_left(high, low, value):
    vh, vl = split(value)
    return dot(high, vh) + (dot(high, vl) + dot(low, vh))


def scan_gradients(patches, measured, weights, probe, tables):
    probe_re, probe_im = probe[0], probe[1]
    right_high, right_low, left_high, left_low = (tables[t] for t in range(4))
    rows = [
        jnp.concatenate([probe_re * re - probe_im * im, probe_re * im + probe_im * re], 1)
        for re, im in patches
    ]
    half = times_right(jnp.concatenate(rows, 0), right_high, right_low)
    count = len(patches)
    stacked = jnp.concatenate(
        [
            jnp.concatenate([half[j * N : (j + 1) * N, part * N : (part + 1) * N] for j in range(count)], 1)
            for part in range(2)
        ],
        0,
    )
    far = times_left(left_high, left_low, stacked)
    far_re, far_im = far[:N], far[N:]
    squared = far_re * far_re + far_im * far_im
    inverse = lax.rsqrt(jnp.maximum(squared, AMP_FLOOR * AMP_FLOOR))
    amplitude = jnp.concatenate([m for m in measured], 1)
    factor = 1.0 - amplitude * inverse
    factor = jnp.concatenate(
        [factor[:, j * N : (j + 1) * N] * weights[j] for j in range(count)], 1
    )
    residual = jnp.concatenate([far_re * factor, far_im * factor], 0)
    half = times_left(right_high, right_low, residual)
    rows = [
        jnp.concatenate([half[:N, j * N : (j + 1) * N], half[N:, j * N : (j + 1) * N]], 1)
        for j in range(count)
    ]
    back = times_right(jnp.concatenate(rows, 0), left_high, left_low)
    grads = []
    for j in range(count):
        re, im = back[j * N : (j + 1) * N, :N], back[j * N : (j + 1) * N, N:]
        grads.append((probe_re * re + probe_im * im, probe_re * im - probe_im * re))
    return grads


def column_of(spots, slot, blocks):
    column = spots[slot, 1]
    first, offset = column // N, lax.rem(column, N)
    return first, jnp.minimum(first + 1, blocks - 1), offset


def inner_kernel(spots, counts, proj, probe, measured, tables, trans, grad, frame):
    blocks, tile = proj.shape[1], proj.shape[2]
    for block in range(blocks):
        re, im = transmit(proj[0, block], proj[1, block])
        trans[0, block] = re
        trans[1, block] = im
    grad[...] = jnp.zeros(grad.shape, f32)
    frame[0:SHIFT, :] = jnp.zeros((SHIFT, N), f32)
    frame[SHIFT + N :, :] = jnp.zeros((SHIFT, N), f32)
    slots = measured.shape[0]
    lane = lane_iota(N)
    patches, weights = [], []
    for slot in range(1, slots):
        row = jnp.minimum(spots[slot, 0], EDGE_ROWS)
        first, second, offset = column_of(spots, slot, blocks)
        pair = []
        for c in range(2):
            left = roll_left(trans[c, first, pl.ds(row, N), :], offset)
            right = roll_left(trans[c, second, pl.ds(row, N), :], offset)
            pair.append(jnp.where(lane < N - offset, left, right))
        patches.append(pair)
        weights.append(jnp.where(slot < counts[0, 0], 1.0, 0.0).astype(f32))
    grads = scan_gradients(patches, [measured[slot] for slot in range(1, slots)], weights, probe, tables)
    lane = lane_iota(tile)
    for slot in range(1, slots):
        row = jnp.minimum(spots[slot, 0], EDGE_ROWS)
        first, second, offset = column_of(spots, slot, blocks)
        for c in range(2):
            frame[SHIFT : SHIFT + N, :] = grads[slot - 1][c]
            placed = roll_lanes(frame[pl.ds(SHIFT - row, tile), :], offset)
            grad[c, first] += jnp.where(lane >= offset, placed, 0.0)
            grad[c, second] += jnp.where(lane < offset, placed, 0.0)


def edge_kernel(spots, counts, halo, trans, probe, measured, tables, own, sent, patch, frame):
    blocks, tile = trans.shape[1], trans.shape[2]
    first, second, offset = column_of(spots, 0, blocks)
    row = spots[0, 0]
    last = lax.axis_index("rows") == lax.axis_size("rows") - 1
    lane = lane_iota(tile)
    for c in range(2):
        left = roll_left(trans[c, first], offset)
        right = roll_left(trans[c, second], offset)
        patch[c, 0:tile, :] = jnp.where(lane < N - offset, left, right)
    below = jnp.where(last, 0.0, halo[...].astype(f32))
    re, im = transmit(below[:N], below[N:])
    patch[0, tile:, :] = re
    patch[1, tile:, :] = im
    pair = [patch[c, pl.ds(row, N), :] for c in range(2)]
    weight = jnp.where(0 < counts[0, 0], 1.0, 0.0).astype(f32)
    grads = scan_gradients([pair], [measured[0]], [weight], probe, tables)[0]
    for c in range(2):
        frame[c, 0:tile, :] = jnp.zeros((tile, N), f32)
        frame[c, tile : tile + N, :] = grads[c]
        frame[c, tile + N :, :] = jnp.zeros((tile, N), f32)
    for c in range(2):
        own[c] = frame[c, pl.ds(tile - row, tile), :]
        sent[c * N : (c + 1) * N, :] = frame[c, pl.ds(2 * tile - row, N), :].astype(bf16)


def cut_kernel(spots, previous, trans, inner, own, above, *refs):
    outs, total, scratch = refs[:-2], refs[-2], refs[-1]
    blocks, tile = trans.shape[1], trans.shape[2]
    scratch[2 * tile :, :] = jnp.zeros((scratch.shape[0] - 2 * tile, N), f32)
    total[...] = inner[...]
    first, second, offset = column_of(spots, 0, blocks)
    lane = lane_iota(tile)
    for c in range(2):
        placed = roll_lanes(own[c], offset)
        total[c, first] += jnp.where(lane >= offset, placed, 0.0)
        total[c, second] += jnp.where(lane < offset, placed, 0.0)
    first, second, offset = column_of(previous, 0, blocks)
    top = lax.axis_index("rows") == 0
    received = jnp.where(top, 0.0, above[...].astype(f32))
    lane = lane_iota(N)
    for c in range(2):
        placed = roll_lanes(received[c * N : (c + 1) * N], offset)
        total[c, first, 0:N, :] += jnp.where(lane >= offset, placed, 0.0)
        total[c, second, 0:N, :] += jnp.where(lane < offset, placed, 0.0)
    for block in range(blocks):
        tr, ti = trans[0, block], trans[1, block]
        gr, gi = total[0, block], total[1, block]
        total[0, block] = tr * gi - ti * gr
        total[1, block] = -(tr * gr + ti * gi)
    me = lax.axis_index("ang")
    lane = lane_iota(tile)
    for d, out in enumerate(outs):
        block = lax.rem(me + d, blocks)
        before, after = lax.rem(block + (blocks - 1), blocks), lax.rem(block + 1, blocks)
        mains, margins = [], []
        for c in range(2):
            mains.append(total[c, block])
            margin = jnp.where(lane < SHIFT, total[c, after], 0.0)
            margins.append(jnp.where(lane >= N - SHIFT, total[c, before], margin))
        out[...] = packed_message(jnp.concatenate(mains, 0), jnp.concatenate(margins, 0), scratch)


def slab_kernel(shifts, *refs):
    outs, received = refs[-2:], refs[:-2]
    angles = len(received)
    tile = outs[0].shape[0] // 2
    me = lax.axis_index("ang")
    lane = lane_iota(tile)
    sums = [[None, None], [None, None]]
    for d, ref in enumerate(received):
        angle = lax.rem(me + (angles - d), angles)
        message = ref[...].astype(f32)
        margins = margins_of(message, 2 * tile)
        for z in range(2):
            s = shifts[angle, z]
            target = lane + s
            inside = (target >= 0) & (target < N)
            for c in range(2):
                part = slice(c * tile, (c + 1) * tile)
                value = jnp.where(inside, message[part], margins[part])
                value = pltpu.roll(value, lax.rem(s + N, N), 1)
                sums[c][z] = value if sums[c][z] is None else sums[c][z] + value
    for c in range(2):
        for z in range(2):
            outs[c][pl.ds(z, tile, stride=2), :] = sums[c][z]


def call(kernel, ins, outs, scratch=(), flops=0, bytes_accessed=0):
    return pl.pallas_call(
        kernel,
        in_specs=ins,
        out_specs=[VMEM] * len(outs),
        out_shape=[jax.ShapeDtypeStruct(shape, dtype) for shape, dtype in outs],
        scratch_shapes=[pltpu.VMEM(shape, f32) for shape in scratch],
        compiler_params=pltpu.CompilerParams(vmem_limit_bytes=32 * 1024 * 1024),
        cost_estimate=pl.CostEstimate(flops=flops, bytes_accessed=bytes_accessed, transcendentals=0),
    )


def exchange(messages):
    count = lax.axis_size("ang")
    received = [messages[0]]
    for d in range(1, count):
        received.append(lax.ppermute(messages[d], "ang", [(i, (i + d) % count) for i in range(count)]))
    return received


def shift_rows(value, steps):
    count = lax.axis_size("rows")
    return lax.ppermute(value, "rows", [(i, (i + steps) % count) for i in range(count)])


def on_device(delta_obj, beta_obj, layer_shifts, illumination_field, amplitudes, positions, scan_counts):
    tile = delta_obj.shape[0]
    angles = lax.axis_size("ang")
    message = ((2 * tile + PACK_ROWS, N), bf16)
    padded = len(groups_of(2 * tile)) * PACK_ROWS
    field = ((2, angles, tile, N), f32)
    measured, spots = amplitudes[0], positions[0]
    tables = jnp.asarray(fourier_tables())
    previous = shift_rows(spots, 1)

    windows = call(window_kernel, [SMEM] + [VMEM] * 2, [message] * angles, [(padded, N)])(
        layer_shifts, delta_obj.reshape(2 * tile, N), beta_obj.reshape(2 * tile, N)
    )
    received = exchange(windows)
    proj, halo = call(
        assemble_kernel,
        [SMEM] + [VMEM] * angles,
        [field, ((2 * N, N), bf16)],
        [(angles, 2 * tile, N)],
    )(previous, *received)
    below = shift_rows(halo, -1)
    trans, inner = call(
        inner_kernel,
        [SMEM] * 2 + [VMEM] * 4,
        [field, field],
        [(N + 2 * SHIFT, N)],
        flops=3 * 10**9,
        bytes_accessed=3 * 10**6,
    )(spots, scan_counts, proj, illumination_field, measured, tables)
    own, sent = call(
        edge_kernel,
        [SMEM] * 2 + [VMEM] * 5,
        [((2, tile, N), f32), ((2 * N, N), bf16)],
        [(2, tile + N, N), (2, 2 * tile + N, N)],
    )(spots, scan_counts, below, trans, illumination_field, measured, tables)
    above = shift_rows(sent, 1)
    outgoing = call(
        cut_kernel,
        [SMEM] * 2 + [VMEM] * 4,
        [message] * angles,
        [field[0], (padded, N)],
    )(spots, previous, trans, inner, own, above)
    grad_delta, grad_beta = call(slab_kernel, [SMEM] + [VMEM] * angles, [((2 * tile, N), f32)] * 2)(
        layer_shifts, *exchange(outgoing)
    )
    return grad_delta.reshape(tile, 2, N), grad_beta.reshape(tile, 2, N)


def solution(mesh):
    placed = (
        P("rows", None, "ang"),
        P("rows", None, "ang"),
        P(),
        P(),
        P("ang", "rows", None, None),
        P("ang", "rows", None),
        P("ang", "rows"),
    )
    return jax.shard_map(
        on_device,
        mesh=mesh,
        in_specs=placed,
        out_specs=(P("rows", None, "ang"), P("rows", None, "ang")),
        check_vma=False,
    )
```

```python
import functools
import math

import jax
import jax.numpy as jnp
import ml_dtypes
import numpy as np
from jax import lax
from jax.experimental import pallas as pl
from jax.experimental.pallas import tpu as pltpu
from jax.sharding import PartitionSpec as P

N = 128
SHIFT = 8
AMP_FLOOR = 0.1
PACK_ROWS = 48
EDGE_ROWS = 8

f32, bf16, i32 = jnp.float32, jnp.bfloat16, jnp.int32
SMEM = pl.BlockSpec(memory_space=pltpu.SMEM)
VMEM = pl.BlockSpec(memory_space=pltpu.VMEM)
HBM = pl.BlockSpec(memory_space=pltpu.HBM)


def fourier_tables():
    counter = np.arange(N)
    angle = (counter[:, None] * counter[None, :] % N) * (2.0 * math.pi / N)
    re, im = np.cos(angle) / math.sqrt(N), -np.sin(angle) / math.sqrt(N)
    right = np.block([[re, im], [-im, re]])
    tables = []
    for table in (right, right.T):
        high = table.astype(ml_dtypes.bfloat16)
        tables += [high, (table - high.astype(np.float64)).astype(ml_dtypes.bfloat16)]
    return np.stack(tables)


def lane_iota(rows):
    return lax.broadcasted_iota(i32, (rows, N), 1)


def roll_lanes(value, by):
    return pltpu.roll(value, by, 1)


def roll_left(value, by):
    return pltpu.roll(value, lax.rem(N - by, N), 1)


def groups_of(rows):
    return [(g, start, min(PACK_ROWS, rows - start)) for g, start in enumerate(range(0, rows, PACK_ROWS))]


def packed_message(main, margins, scratch):
    rows = main.shape[0]
    scratch[0:rows, :] = margins
    packed = None
    for g, start, _ in groups_of(rows):
        part = scratch[start : start + PACK_ROWS, :]
        part = roll_lanes(part, 16 * g) if g else part
        packed = part if packed is None else packed + part
    return jnp.concatenate([main, packed], 0).astype(bf16)


def margins_of(message, rows):
    packed = message[rows:, :]
    parts = []
    for g, _, size in groups_of(rows):
        part = roll_lanes(packed, N - 16 * g) if g else packed
        parts.append(part[:size])
    return jnp.concatenate(parts, 0)


def window_kernel(shifts, spots, counts, delta, beta, probe_in, measured_in, *refs):
    outs = refs[:-8]
    slot, probe, measured, slab_delta, slab_beta, scratch, near, far = refs[-8:]
    copies = [
        pltpu.make_async_copy(source, target, near.at[k])
        for k, (source, target) in enumerate([(delta, slab_delta), (beta, slab_beta)])
    ]
    others = [
        pltpu.make_async_copy(source, target, far.at[k])
        for k, (source, target) in enumerate([(measured_in, measured), (probe_in, probe)])
    ]
    for copy in copies + others:
        copy.start()
    angles = len(outs)
    tile = delta.shape[0] // 2
    scratch[2 * tile :, :] = jnp.zeros((scratch.shape[0] - 2 * tile, N), f32)
    me = lax.axis_index("ang")
    lane = lane_iota(tile)
    for copy in copies:
        copy.wait()
    for d in [*range(1, angles), 0]:
        angle = lax.rem(me + d, angles)
        mains, margins = [], []
        for ref in (slab_delta, slab_beta):
            main = margin = None
            for z in range(2):
                s = shifts[z, angle]
                rolled = pltpu.roll(ref[pl.ds(z, tile, stride=2), :], lax.rem(N - s, N), 1)
                source = lane + s
                inside = (source >= 0) & (source < N)
                kept, out_of = jnp.where(inside, rolled, 0.0), jnp.where(inside, 0.0, rolled)
                main = kept if z == 0 else main + kept
                margin = out_of if z == 0 else margin + out_of
            mains.append(main)
            margins.append(margin)
        outs[d][...] = packed_message(jnp.concatenate(mains, 0), jnp.concatenate(margins, 0), scratch)
    for copy in others:
        copy.wait()
    slot[0:N, :] = measured[0]
    row = jnp.where(counts[0, 0] > 0, spots[0, 0], 0)
    slot[N : N + 8, :] = jnp.full((8, N), row, i32).astype(f32)
    slot[N + 8 :, :] = jnp.full((8, N), spots[1, 0], i32).astype(f32)


def slot_position(slot):
    return slot[N, 0].astype(i32), slot[N + 8, 0].astype(i32)


def block_of(column, blocks):
    first, offset = column // N, lax.rem(column, N)
    return first, jnp.minimum(first + 1, blocks - 1), offset


def is_even():
    return lax.rem(lax.axis_index("rows"), 2) == 0


def assemble_kernel(spots, slot, *refs):
    proj, core, cross, margins = refs[-4:]
    received = refs[:-4]
    blocks = len(received)
    tile = proj.shape[2]
    me = lax.axis_index("ang")
    for d, ref in enumerate(received):
        block = lax.rem(me + (blocks - d), blocks)
        message = ref[...].astype(f32)
        proj[0, block] = message[:tile]
        proj[1, block] = message[tile : 2 * tile]
        margins[block] = margins_of(message, 2 * tile)
    lane = lane_iota(tile)
    for block in range(blocks):
        before, after = (block - 1) % blocks, (block + 1) % blocks
        for c in range(2):
            part = slice(c * tile, (c + 1) * tile)
            extra = jnp.where(lane < SHIFT, margins[before, part], 0.0)
            extra += jnp.where(lane >= N - SHIFT, margins[after, part], 0.0)
            proj[c, block] += extra
    _, previous = slot_position(slot)
    lane = lane_iota(N)
    even = is_even()
    for upper in (True, False):
        first, second, offset = block_of(spots[1, 0] if upper else previous, blocks)
        start = EDGE_ROWS if upper else 0
        for c in range(2):
            left = roll_left(proj[c, first, start : start + N, :], offset)
            right = roll_left(proj[c, second, start : start + N, :], offset)
            value = jnp.where(lane < N - offset, left, right).astype(bf16)
            part = slice(c * N, (c + 1) * N)

            @pl.when(even == upper)
            def _():
                core[part, :] = value

            @pl.when(even != upper)
            def _():
                cross[part, :] = value


def transmit(phase, absorb):
    turns = jnp.round(phase * (2.0 / math.pi))
    r = phase - turns * 1.5703125
    r = r - turns * 4.837512969970703125e-4
    r = r - turns * 7.54978995489188e-8
    z = r * r
    sine = r + r * z * (-1.6666654611e-1 + z * (8.3321608736e-3 - z * 1.9515295891e-4))
    cosine = 1.0 - 0.5 * z + z * z * (4.166664568298827e-2 + z * (-1.388731625493765e-3 + z * 2.443315711809948e-5))
    quarter = turns.astype(i32)
    odd = (quarter & 1) == 1
    damping = jnp.exp(-absorb)
    out_cos = jnp.where(odd, sine, cosine)
    out_sin = jnp.where(odd, cosine, sine)
    out_cos = jnp.where(((quarter + 1) & 2) == 2, -out_cos, out_cos)
    out_sin = jnp.where((quarter & 2) == 2, -out_sin, out_sin)
    return damping * out_cos, damping * out_sin


def split(value):
    high = value.astype(bf16)
    return high, (value - high.astype(f32)).astype(bf16)


def dot(a, b):
    return jnp.dot(a, b, preferred_element_type=f32)


def times_right(value, high, low):
    vh, vl = split(value)
    return dot(vh, high) + (dot(vl, high) + dot(vh, low))


def times_left(high, low, value):
    vh, vl = split(value)
    return dot(high, vh) + (dot(high, vl) + dot(low, vh))


def scan_gradients(patches, measured, weights, probe, tables):
    probe_re, probe_im = probe[0], probe[1]
    right_high, right_low, left_high, left_low = (tables[t] for t in range(4))
    rows = [
        jnp.concatenate([probe_re * re - probe_im * im, probe_re * im + probe_im * re], 1)
        for re, im in patches
    ]
    half = times_right(jnp.concatenate(rows, 0), right_high, right_low)
    count = len(patches)
    stacked = jnp.concatenate(
        [
            jnp.concatenate([half[j * N : (j + 1) * N, part * N : (part + 1) * N] for j in range(count)], 1)
            for part in range(2)
        ],
        0,
    )
    far = times_left(left_high, left_low, stacked)
    far_re, far_im = far[:N], far[N:]
    squared = far_re * far_re + far_im * far_im
    inverse = lax.rsqrt(jnp.maximum(squared, AMP_FLOOR * AMP_FLOOR))
    amplitude = jnp.concatenate([m for m in measured], 1)
    factor = 1.0 - amplitude * inverse
    factor = jnp.concatenate(
        [factor[:, j * N : (j + 1) * N] * weights[j] for j in range(count)], 1
    )
    residual = jnp.concatenate([far_re * factor, far_im * factor], 0)
    half = times_left(right_high, right_low, residual)
    rows = [
        jnp.concatenate([half[:N, j * N : (j + 1) * N], half[N:, j * N : (j + 1) * N]], 1)
        for j in range(count)
    ]
    back = times_right(jnp.concatenate(rows, 0), left_high, left_low)
    grads = []
    for j in range(count):
        re, im = back[j * N : (j + 1) * N, :N], back[j * N : (j + 1) * N, N:]
        grads.append((probe_re * re + probe_im * im, probe_re * im - probe_im * re))
    return grads


def patch_of(values, lane, offset, first, second, rows):
    pair = []
    for c in range(2):
        left = roll_left(values[c, first, rows, :], offset)
        right = roll_left(values[c, second, rows, :], offset)
        pair.append(jnp.where(lane < N - offset, left, right))
    return pair


def add_patch(total, c, rows, value, lane, offset, first, second):
    placed = roll_lanes(value, offset)
    total[c, first, rows, :] += jnp.where(lane >= offset, placed, 0.0)
    total[c, second, rows, :] += jnp.where(lane < offset, placed, 0.0)


def inner_kernel(spots, counts, proj, probe, measured, tables, trans, grad, frame):
    blocks, tile = proj.shape[1], proj.shape[2]
    for block in range(blocks):
        re, im = transmit(proj[0, block], proj[1, block])
        trans[0, block] = re
        trans[1, block] = im
    grad[...] = jnp.zeros(grad.shape, f32)
    frame[0:SHIFT, :] = jnp.zeros((SHIFT, N), f32)
    frame[SHIFT + N :, :] = jnp.zeros((SHIFT, N), f32)
    slots = measured.shape[0]
    lane = lane_iota(N)
    patches, weights = [], []
    for slot in range(1, slots):
        row = jnp.minimum(spots[0, slot], EDGE_ROWS)
        first, second, offset = block_of(spots[1, slot], blocks)
        patches.append(patch_of(trans, lane, offset, first, second, pl.ds(row, N)))
        weights.append(jnp.where(slot < counts[0, 0], 1.0, 0.0).astype(f32))
    grads = scan_gradients(patches, [measured[slot] for slot in range(1, slots)], weights, probe, tables)
    lane = lane_iota(tile)
    for slot in range(1, slots):
        row = jnp.minimum(spots[0, slot], EDGE_ROWS)
        first, second, offset = block_of(spots[1, slot], blocks)
        for c in range(2):
            frame[SHIFT : SHIFT + N, :] = grads[slot - 1][c]
            add_patch(grad, c, slice(None), frame[pl.ds(SHIFT - row, tile), :], lane, offset, first, second)


def edge_kernel(spots, counts, slot, core, cross, trans, inner, probe, measured, tables, *refs):
    outs, (total, patch, frame, scratch) = refs[:-4], refs[-4:]
    blocks, tile = trans.shape[1], trans.shape[2]
    scratch[2 * tile :, :] = jnp.zeros((scratch.shape[0] - 2 * tile, N), f32)
    even = is_even()
    own_row, own_column = spots[0, 0], spots[1, 0]
    prev_row, prev_column = slot_position(slot)
    own_block, prev_block = block_of(own_column, blocks), block_of(prev_column, blocks)
    last = lax.axis_index("rows") == lax.axis_size("rows") - 1
    near, away = core[...].astype(f32), cross[...].astype(f32)
    below = jnp.where(last, 0.0, jnp.where(even, near, away))
    above = jnp.where(even, away, near)
    re, im = transmit(below[:N], below[N:])
    patch[0, 0, tile:, :] = re
    patch[0, 1, tile:, :] = im
    re, im = transmit(above[:N], above[N:])
    patch[1, 0, EDGE_ROWS:tile, :] = re
    patch[1, 1, EDGE_ROWS:tile, :] = im
    first, second, offset = own_block
    pair = patch_of(trans, lane_iota(tile), offset, first, second, slice(None))
    for c in range(2):
        patch[0, c, 0:tile, :] = pair[c]
    first, second, offset = prev_block
    pair = patch_of(trans, lane_iota(N), offset, first, second, slice(0, N))
    for c in range(2):
        patch[1, c, tile:, :] = pair[c]
    reaches = (prev_row > EDGE_ROWS) & (lax.axis_index("rows") > 0)
    start = jnp.maximum(prev_row, EDGE_ROWS)
    patches = [
        [patch[0, c, pl.ds(own_row, N), :] for c in range(2)],
        [patch[1, c, pl.ds(start, N), :] for c in range(2)],
    ]
    weights = [jnp.where(flag, 1.0, 0.0).astype(f32) for flag in (counts[0, 0] > 0, reaches)]
    grads = scan_gradients(patches, [measured[0], slot[0:N, :]], weights, probe, tables)
    total[...] = inner[...]
    for c in range(2):
        frame[c, 0:tile, :] = jnp.zeros((tile, N), f32)
        frame[c, tile : tile + N, :] = grads[0][c]
        frame[c, tile + N :, :] = jnp.zeros((frame.shape[1] - tile - N, N), f32)
    for c in range(2):
        add_patch(total, c, slice(None), frame[c, pl.ds(tile - own_row, tile), :], lane_iota(tile), offset=own_block[2], first=own_block[0], second=own_block[1])
    for c in range(2):
        frame[c, 0:N, :] = grads[1][c]
        frame[c, N : 2 * N, :] = jnp.zeros((N, N), f32)
    for c in range(2):
        add_patch(total, c, slice(0, N), frame[c, pl.ds(tile - start, N), :], lane_iota(N), offset=prev_block[2], first=prev_block[0], second=prev_block[1])
    for block in range(blocks):
        tr, ti = trans[0, block], trans[1, block]
        gr, gi = total[0, block], total[1, block]
        total[0, block] = tr * gi - ti * gr
        total[1, block] = -(tr * gr + ti * gi)
    me = lax.axis_index("ang")
    lane = lane_iota(tile)
    for d, out in enumerate(outs):
        block = lax.rem(me + d, blocks)
        before, after = lax.rem(block + (blocks - 1), blocks), lax.rem(block + 1, blocks)
        mains, margins = [], []
        for c in range(2):
            mains.append(total[c, block])
            margin = jnp.where(lane < SHIFT, total[c, after], 0.0)
            margins.append(jnp.where(lane >= N - SHIFT, total[c, before], margin))
        out[...] = packed_message(jnp.concatenate(mains, 0), jnp.concatenate(margins, 0), scratch)


def slab_kernel(shifts, *refs):
    outs, received = refs[-2:], refs[:-2]
    angles = len(received)
    tile = outs[0].shape[0] // 2
    me = lax.axis_index("ang")
    lane = lane_iota(tile)
    sums = [[None, None], [None, None]]
    for d, ref in enumerate(received):
        angle = lax.rem(me + (angles - d), angles)
        message = ref[...].astype(f32)
        margins = margins_of(message, 2 * tile)
        for z in range(2):
            s = shifts[z, angle]
            target = lane + s
            inside = (target >= 0) & (target < N)
            for c in range(2):
                part = slice(c * tile, (c + 1) * tile)
                value = jnp.where(inside, message[part], margins[part])
                value = pltpu.roll(value, lax.rem(s + N, N), 1)
                sums[c][z] = value if sums[c][z] is None else sums[c][z] + value
    for c in range(2):
        for z in range(2):
            outs[c][pl.ds(z, tile, stride=2), :] = sums[c][z]


def call(kernel, ins, outs, scratch=(), flops=0, bytes_accessed=0):
    scratch = [pltpu.VMEM(item, f32) if isinstance(item, tuple) else item for item in scratch]
    return pl.pallas_call(
        kernel,
        in_specs=ins,
        out_specs=[VMEM] * len(outs),
        out_shape=[jax.ShapeDtypeStruct(shape, dtype) for shape, dtype in outs],
        scratch_shapes=scratch,
        compiler_params=pltpu.CompilerParams(vmem_limit_bytes=32 * 1024 * 1024),
        cost_estimate=pl.CostEstimate(flops=flops, bytes_accessed=bytes_accessed, transcendentals=0),
    )


def exchange(messages):
    count = lax.axis_size("ang")
    received = [messages[0]]
    for d in range(1, count):
        received.append(lax.ppermute(messages[d], "ang", [(i, (i + d) % count) for i in range(count)]))
    return received


def on_rows(value, target):
    count = lax.axis_size("rows")
    return lax.ppermute(value, "rows", [(i, target(i) % count) for i in range(count)])


def on_device(delta_obj, beta_obj, layer_shifts, illumination_field, amplitudes, positions, scan_counts):
    tile = delta_obj.shape[0]
    angles = lax.axis_size("ang")
    message = ((2 * tile + PACK_ROWS, N), bf16)
    padded = (len(groups_of(2 * tile)) * PACK_ROWS, N)
    field = ((2, angles, tile, N), f32)
    slab = (2 * tile, N)
    halo = ((2 * N, N), bf16)
    shifts, spots = layer_shifts.T, positions[0].T
    tables = jnp.asarray(fourier_tables())

    *windows, slot, probe, measured = call(
        window_kernel,
        [SMEM] * 3 + [HBM] * 4,
        [message] * angles + [((N + 16, N), f32), (illumination_field.shape, f32), (amplitudes.shape[1:], f32)],
        [slab, slab, padded, pltpu.SemaphoreType.DMA((2,)), pltpu.SemaphoreType.DMA((2,))],
    )(
        shifts,
        spots,
        scan_counts,
        *(
            pltpu.with_memory_space_constraint(value, pltpu.HBM)
            for value in (delta_obj.reshape(slab), beta_obj.reshape(slab), illumination_field, amplitudes[0])
        ),
    )
    received = exchange(windows)
    previous = on_rows(slot, lambda i: i + 1)
    proj, core, cross = call(
        assemble_kernel,
        [SMEM] + [VMEM] * (angles + 1),
        [field, halo, halo],
        [(angles, 2 * tile, N)],
    )(spots, previous, *received)
    core = on_rows(core, lambda i: i ^ 1)
    cross = on_rows(cross, lambda i: i + 1 if i % 2 else i - 1)
    trans, inner = call(
        inner_kernel,
        [SMEM] * 2 + [VMEM] * 4,
        [field, field],
        [(N + 2 * SHIFT, N)],
        flops=3 * 10**9,
        bytes_accessed=3 * 10**6,
    )(spots, scan_counts, proj, probe, measured, tables)
    outgoing = call(
        edge_kernel,
        [SMEM] * 2 + [VMEM] * 8,
        [message] * angles,
        [field[0], (2, 2, tile + N, N), (2, 2 * tile + 8, N), padded],
    )(spots, scan_counts, previous, core, cross, trans, inner, probe, measured, tables)
    grad_delta, grad_beta = call(slab_kernel, [SMEM] + [VMEM] * angles, [(slab, f32)] * 2)(
        shifts, *exchange(outgoing)
    )
    return grad_delta.reshape(tile, 2, N), grad_beta.reshape(tile, 2, N)


def solution(mesh):
    placed = (
        P("rows", None, "ang"),
        P("rows", None, "ang"),
        P(),
        P(),
        P("ang", "rows", None, None),
        P("ang", "rows", None),
        P("ang", "rows"),
    )
    return jax.shard_map(
        on_device,
        mesh=mesh,
        in_specs=placed,
        out_specs=(P("rows", None, "ang"), P("rows", None, "ang")),
        check_vma=False,
    )
```

```python
import functools
import math

import jax
import jax.numpy as jnp
import ml_dtypes
import numpy as np
from jax import lax
from jax.experimental import pallas as pl
from jax.experimental.pallas import tpu as pltpu
from jax.sharding import PartitionSpec as P

N = 128
SHIFT = 8
AMP_FLOOR = 0.1
PACK_ROWS = 48
EDGE_ROWS = 8

f32, bf16, i32 = jnp.float32, jnp.bfloat16, jnp.int32
VMEM = pl.BlockSpec(memory_space=pltpu.VMEM)
SMEM = pl.BlockSpec(memory_space=pltpu.SMEM)
HBM = pl.BlockSpec(memory_space=pltpu.HBM)


def fourier_tables():
    counter = np.arange(N)
    angle = (counter[:, None] * counter[None, :] % N) * (2.0 * math.pi / N)
    re, im = np.cos(angle) / math.sqrt(N), -np.sin(angle) / math.sqrt(N)
    right = np.block([[re, im], [-im, re]])
    tables = []
    for table in (right, right.T):
        high = table.astype(ml_dtypes.bfloat16)
        tables += [high, (table - high.astype(np.float64)).astype(ml_dtypes.bfloat16)]
    return np.stack(tables)


def lane_iota(rows):
    return lax.broadcasted_iota(i32, (rows, N), 1)


def roll_lanes(value, by):
    return pltpu.roll(value, by, 1)


def roll_left(value, by):
    return pltpu.roll(value, lax.rem(N - by, N), 1)


def groups_of(rows):
    return [(g, start, min(PACK_ROWS, rows - start)) for g, start in enumerate(range(0, rows, PACK_ROWS))]


def packed_message(main, margins, scratch):
    rows = main.shape[0]
    scratch[0:rows, :] = margins
    packed = None
    for g, start, _ in groups_of(rows):
        part = scratch[start : start + PACK_ROWS, :]
        part = roll_lanes(part, 16 * g) if g else part
        packed = part if packed is None else packed + part
    return jnp.concatenate([main, packed], 0).astype(bf16)


def margins_of(message, rows):
    packed = message[rows:, :]
    parts = []
    for g, _, size in groups_of(rows):
        part = roll_lanes(packed, N - 16 * g) if g else packed
        parts.append(part[:size])
    return jnp.concatenate(parts, 0)


def window_message(d, shifts, slab_delta, slab_beta, scratch):
    tile = slab_delta.shape[0] // 2
    lane = lane_iota(tile)
    mains, margins = [], []
    for ref in (slab_delta, slab_beta):
        main = margin = None
        for z in range(2):
            s = shifts[2 * d + z, 0]
            rolled = pltpu.roll(ref[pl.ds(z, tile, stride=2), :], lax.rem(N - s, N), 1)
            source = lane + s
            inside = (source >= 0) & (source < N)
            kept, out_of = jnp.where(inside, rolled, 0.0), jnp.where(inside, 0.0, rolled)
            main = kept if z == 0 else main + kept
            margin = out_of if z == 0 else margin + out_of
        mains.append(main)
        margins.append(margin)
    scratch[2 * tile :, :] = jnp.zeros((scratch.shape[0] - 2 * tile, N), f32)
    return packed_message(jnp.concatenate(mains, 0), jnp.concatenate(margins, 0), scratch)


def first_kernel(angles, counts, *refs):
    sources, targets = refs[:6], refs[6:11]
    shifts, out, slot, scalar_shifts, scalar_spots, scratch, first_sems, second_sems = refs[11:]
    spots, slab_delta, slab_beta, _, measured = targets
    first = [
        pltpu.make_async_copy(source, target, first_sems.at[k])
        for k, (source, target) in enumerate(
            [*zip(sources[:4], (scalar_shifts, scalar_spots, slab_delta, slab_beta))]
        )
    ]
    second = [
        pltpu.make_async_copy(source, target, second_sems.at[k])
        for k, (source, target) in enumerate([(sources[1], spots), *zip(sources[4:], targets[3:])])
    ]
    for copy in first + second:
        copy.start()
    for copy in first:
        copy.wait()
    me = lax.axis_index("ang")
    for d in range(angles):
        angle = lax.rem(me + d, angles)
        for z in range(2):
            shifts[2 * d + z : 2 * d + z + 1, :] = jnp.full((1, N), scalar_shifts[z, angle], i32)
    out[...] = window_message(1, shifts, slab_delta, slab_beta, scratch)
    for copy in second:
        copy.wait()
    slot[0:N, :] = measured[0]
    row = jnp.where(counts[0, 0] > 0, scalar_spots[0, 0], 0)
    slot[N : N + 8, :] = jnp.full((8, N), row, i32).astype(f32)
    slot[N + 8 :, :] = jnp.full((8, N), scalar_spots[1, 0], i32).astype(f32)


def window_kernel(shifts, slab_delta, slab_beta, *refs):
    outs, scratch = refs[:-1], refs[-1]
    angles = len(outs) + 1
    for out, d in zip(outs, [*range(2, angles), 0]):
        out[...] = window_message(d, shifts, slab_delta, slab_beta, scratch)


def slot_position(slot):
    return slot[N, 0].astype(i32), slot[N + 8, 0].astype(i32)


def block_of(column, blocks):
    first, offset = column // N, lax.rem(column, N)
    return first, jnp.minimum(first + 1, blocks - 1), offset


def is_even():
    return lax.rem(lax.axis_index("rows"), 2) == 0


def assemble_kernel(spots, slot, *refs):
    proj, core, cross, margins = refs[-4:]
    received = refs[:-4]
    blocks = len(received)
    tile = proj.shape[2]
    me = lax.axis_index("ang")
    for d, ref in enumerate(received):
        block = lax.rem(me + (blocks - d), blocks)
        message = ref[...].astype(f32)
        proj[0, block] = message[:tile]
        proj[1, block] = message[tile : 2 * tile]
        margins[block] = margins_of(message, 2 * tile)
    lane = lane_iota(tile)
    for block in range(blocks):
        before, after = (block - 1) % blocks, (block + 1) % blocks
        for c in range(2):
            part = slice(c * tile, (c + 1) * tile)
            extra = jnp.where(lane < SHIFT, margins[before, part], 0.0)
            extra += jnp.where(lane >= N - SHIFT, margins[after, part], 0.0)
            proj[c, block] += extra
    _, previous = slot_position(slot)
    lane = lane_iota(N)
    even = is_even()
    for upper in (True, False):
        first, second, offset = block_of(spots[1, 0] if upper else previous, blocks)
        start = EDGE_ROWS if upper else 0
        for c in range(2):
            left = roll_left(proj[c, first, start : start + N, :], offset)
            right = roll_left(proj[c, second, start : start + N, :], offset)
            value = jnp.where(lane < N - offset, left, right).astype(bf16)
            part = slice(c * N, (c + 1) * N)

            @pl.when(even == upper)
            def _():
                core[part, :] = value

            @pl.when(even != upper)
            def _():
                cross[part, :] = value


def transmit(phase, absorb):
    turns = jnp.round(phase * (2.0 / math.pi))
    r = phase - turns * 1.5703125
    r = r - turns * 4.837512969970703125e-4
    r = r - turns * 7.54978995489188e-8
    z = r * r
    sine = r + r * z * (-1.6666654611e-1 + z * (8.3321608736e-3 - z * 1.9515295891e-4))
    cosine = 1.0 - 0.5 * z + z * z * (4.166664568298827e-2 + z * (-1.388731625493765e-3 + z * 2.443315711809948e-5))
    quarter = turns.astype(i32)
    odd = (quarter & 1) == 1
    damping = jnp.exp(-absorb)
    out_cos = jnp.where(odd, sine, cosine)
    out_sin = jnp.where(odd, cosine, sine)
    out_cos = jnp.where(((quarter + 1) & 2) == 2, -out_cos, out_cos)
    out_sin = jnp.where((quarter & 2) == 2, -out_sin, out_sin)
    return damping * out_cos, damping * out_sin


def split(value):
    high = value.astype(bf16)
    return high, (value - high.astype(f32)).astype(bf16)


def dot(a, b):
    return jnp.dot(a, b, preferred_element_type=f32)


def times_right(value, high, low):
    vh, vl = split(value)
    return dot(vh, high) + (dot(vl, high) + dot(vh, low))


def times_left(high, low, value):
    vh, vl = split(value)
    return dot(high, vh) + (dot(high, vl) + dot(low, vh))


def scan_gradients(patches, measured, weights, probe, tables):
    probe_re, probe_im = probe[0], probe[1]
    right_high, right_low, left_high, left_low = (tables[t] for t in range(4))
    rows = [
        jnp.concatenate([probe_re * re - probe_im * im, probe_re * im + probe_im * re], 1)
        for re, im in patches
    ]
    half = times_right(jnp.concatenate(rows, 0), right_high, right_low)
    count = len(patches)
    stacked = jnp.concatenate(
        [
            jnp.concatenate([half[j * N : (j + 1) * N, part * N : (part + 1) * N] for j in range(count)], 1)
            for part in range(2)
        ],
        0,
    )
    far = times_left(left_high, left_low, stacked)
    far_re, far_im = far[:N], far[N:]
    squared = far_re * far_re + far_im * far_im
    inverse = lax.rsqrt(jnp.maximum(squared, AMP_FLOOR * AMP_FLOOR))
    amplitude = jnp.concatenate([m for m in measured], 1)
    factor = 1.0 - amplitude * inverse
    factor = jnp.concatenate(
        [factor[:, j * N : (j + 1) * N] * weights[j] for j in range(count)], 1
    )
    residual = jnp.concatenate([far_re * factor, far_im * factor], 0)
    half = times_left(right_high, right_low, residual)
    rows = [
        jnp.concatenate([half[:N, j * N : (j + 1) * N], half[N:, j * N : (j + 1) * N]], 1)
        for j in range(count)
    ]
    back = times_right(jnp.concatenate(rows, 0), left_high, left_low)
    grads = []
    for j in range(count):
        re, im = back[j * N : (j + 1) * N, :N], back[j * N : (j + 1) * N, N:]
        grads.append((probe_re * re + probe_im * im, probe_re * im - probe_im * re))
    return grads


def patch_of(values, lane, offset, first, second, rows):
    pair = []
    for c in range(2):
        left = roll_left(values[c, first, rows, :], offset)
        right = roll_left(values[c, second, rows, :], offset)
        pair.append(jnp.where(lane < N - offset, left, right))
    return pair


def add_patch(total, c, rows, value, lane, offset, first, second):
    placed = roll_lanes(value, offset)
    total[c, first, rows, :] += jnp.where(lane >= offset, placed, 0.0)
    total[c, second, rows, :] += jnp.where(lane < offset, placed, 0.0)


def inner_kernel(spots, counts, proj, probe, measured, tables, trans, grad, frame):
    blocks, tile = proj.shape[1], proj.shape[2]
    for block in range(blocks):
        re, im = transmit(proj[0, block], proj[1, block])
        trans[0, block] = re
        trans[1, block] = im
    grad[...] = jnp.zeros(grad.shape, f32)
    frame[0:SHIFT, :] = jnp.zeros((SHIFT, N), f32)
    frame[SHIFT + N :, :] = jnp.zeros((SHIFT, N), f32)
    slots = measured.shape[0]
    lane = lane_iota(N)
    patches, weights = [], []
    for slot in range(1, slots):
        row = jnp.minimum(spots[0, slot], EDGE_ROWS)
        first, second, offset = block_of(spots[1, slot], blocks)
        patches.append(patch_of(trans, lane, offset, first, second, pl.ds(row, N)))
        weights.append(jnp.where(slot < counts[0, 0], 1.0, 0.0).astype(f32))
    grads = scan_gradients(patches, [measured[slot] for slot in range(1, slots)], weights, probe, tables)
    lane = lane_iota(tile)
    for slot in range(1, slots):
        row = jnp.minimum(spots[0, slot], EDGE_ROWS)
        first, second, offset = block_of(spots[1, slot], blocks)
        for c in range(2):
            frame[SHIFT : SHIFT + N, :] = grads[slot - 1][c]
            add_patch(grad, c, slice(None), frame[pl.ds(SHIFT - row, tile), :], lane, offset, first, second)


def edge_kernel(spots, counts, slot, core, cross, trans, inner, probe, measured, tables, *refs):
    outs, (total, patch, frame, scratch) = refs[:-4], refs[-4:]
    blocks, tile = trans.shape[1], trans.shape[2]
    scratch[2 * tile :, :] = jnp.zeros((scratch.shape[0] - 2 * tile, N), f32)
    even = is_even()
    own_row, own_column = spots[0, 0], spots[1, 0]
    prev_row, prev_column = slot_position(slot)
    own_block, prev_block = block_of(own_column, blocks), block_of(prev_column, blocks)
    last = lax.axis_index("rows") == lax.axis_size("rows") - 1
    near, away = core[...].astype(f32), cross[...].astype(f32)
    below = jnp.where(last, 0.0, jnp.where(even, near, away))
    above = jnp.where(even, away, near)
    re, im = transmit(below[:N], below[N:])
    patch[0, 0, tile:, :] = re
    patch[0, 1, tile:, :] = im
    re, im = transmit(above[:N], above[N:])
    patch[1, 0, EDGE_ROWS:tile, :] = re
    patch[1, 1, EDGE_ROWS:tile, :] = im
    first, second, offset = own_block
    pair = patch_of(trans, lane_iota(tile), offset, first, second, slice(None))
    for c in range(2):
        patch[0, c, 0:tile, :] = pair[c]
    first, second, offset = prev_block
    pair = patch_of(trans, lane_iota(N), offset, first, second, slice(0, N))
    for c in range(2):
        patch[1, c, tile:, :] = pair[c]
    reaches = (prev_row > EDGE_ROWS) & (lax.axis_index("rows") > 0)
    start = jnp.maximum(prev_row, EDGE_ROWS)
    patches = [
        [patch[0, c, pl.ds(own_row, N), :] for c in range(2)],
        [patch[1, c, pl.ds(start, N), :] for c in range(2)],
    ]
    weights = [jnp.where(flag, 1.0, 0.0).astype(f32) for flag in (counts[0, 0] > 0, reaches)]
    grads = scan_gradients(patches, [measured[0], slot[0:N, :]], weights, probe, tables)
    total[...] = inner[...]
    for c in range(2):
        frame[c, 0:tile, :] = jnp.zeros((tile, N), f32)
        frame[c, tile : tile + N, :] = grads[0][c]
        frame[c, tile + N :, :] = jnp.zeros((frame.shape[1] - tile - N, N), f32)
    for c in range(2):
        add_patch(total, c, slice(None), frame[c, pl.ds(tile - own_row, tile), :], lane_iota(tile), offset=own_block[2], first=own_block[0], second=own_block[1])
    for c in range(2):
        frame[c, 0:N, :] = grads[1][c]
        frame[c, N : 2 * N, :] = jnp.zeros((N, N), f32)
    for c in range(2):
        add_patch(total, c, slice(0, N), frame[c, pl.ds(tile - start, N), :], lane_iota(N), offset=prev_block[2], first=prev_block[0], second=prev_block[1])
    for block in range(blocks):
        tr, ti = trans[0, block], trans[1, block]
        gr, gi = total[0, block], total[1, block]
        total[0, block] = tr * gi - ti * gr
        total[1, block] = -(tr * gr + ti * gi)
    me = lax.axis_index("ang")
    lane = lane_iota(tile)
    for d, out in enumerate(outs):
        block = lax.rem(me + d, blocks)
        before, after = lax.rem(block + (blocks - 1), blocks), lax.rem(block + 1, blocks)
        mains, margins = [], []
        for c in range(2):
            mains.append(total[c, block])
            margin = jnp.where(lane < SHIFT, total[c, after], 0.0)
            margins.append(jnp.where(lane >= N - SHIFT, total[c, before], margin))
        out[...] = packed_message(jnp.concatenate(mains, 0), jnp.concatenate(margins, 0), scratch)


def slab_kernel(angles, steps, last, shifts, *refs):
    refs, outs = (refs[:-2], refs[-2:]) if last else (refs[:-1], refs[-1:])
    received, before = refs[: len(steps)], refs[len(steps) :]
    tile = (received[0].shape[0] - PACK_ROWS) // 2
    lane = lane_iota(tile)
    sums = [[before[0][c, z] if before else None for z in range(2)] for c in range(2)]
    for d, ref in zip(steps, received):
        message = ref[...].astype(f32)
        margins = margins_of(message, 2 * tile)
        for z in range(2):
            s = shifts[2 * ((angles - d) % angles) + z, 0]
            target = lane + s
            inside = (target >= 0) & (target < N)
            for c in range(2):
                part = slice(c * tile, (c + 1) * tile)
                value = jnp.where(inside, message[part], margins[part])
                value = pltpu.roll(value, lax.rem(s + N, N), 1)
                sums[c][z] = value if sums[c][z] is None else sums[c][z] + value
    for c in range(2):
        for z in range(2):
            if last:
                outs[c][pl.ds(z, tile, stride=2), :] = sums[c][z]
            else:
                outs[0][c, z] = sums[c][z]


def call(kernel, ins, outs, scratch=(), flops=0, bytes_accessed=0):
    scratch = [pltpu.VMEM(item, f32) if isinstance(item, tuple) else item for item in scratch]
    return pl.pallas_call(
        kernel,
        in_specs=ins,
        out_specs=[VMEM] * len(outs),
        out_shape=[jax.ShapeDtypeStruct(shape, dtype) for shape, dtype in outs],
        scratch_shapes=scratch,
        compiler_params=pltpu.CompilerParams(vmem_limit_bytes=32 * 1024 * 1024),
        cost_estimate=pl.CostEstimate(flops=flops, bytes_accessed=bytes_accessed, transcendentals=0),
    )


def exchange(messages):
    count = lax.axis_size("ang")
    received = [messages[0]]
    for d in range(1, count):
        received.append(lax.ppermute(messages[d], "ang", [(i, (i + d) % count) for i in range(count)]))
    return received


def on_rows(value, target):
    count = lax.axis_size("rows")
    return lax.ppermute(value, "rows", [(i, target(i) % count) for i in range(count)])


def on_device(delta_obj, beta_obj, layer_shifts, illumination_field, amplitudes, positions, scan_counts):
    tile = delta_obj.shape[0]
    angles = lax.axis_size("ang")
    message = ((2 * tile + PACK_ROWS, N), bf16)
    padded = (len(groups_of(2 * tile)) * PACK_ROWS, N)
    field = ((2, angles, tile, N), f32)
    slab = (2 * tile, N)
    halo = ((2 * N, N), bf16)
    shifts, spots = layer_shifts.T, positions[0].T
    tables = jnp.asarray(fourier_tables())

    arguments = [
        pltpu.with_memory_space_constraint(value, pltpu.HBM)
        for value in (
            shifts,
            spots,
            delta_obj.reshape(slab),
            beta_obj.reshape(slab),
            illumination_field,
            amplitudes[0],
        )
    ]
    spots, slab_delta, slab_beta, probe, measured, shifts, following, slot = call(
        functools.partial(first_kernel, angles),
        [SMEM] + [HBM] * len(arguments),
        [
            *((value.shape, value.dtype) for value in arguments[1:]),
            ((2 * angles, N), i32),
            message,
            ((N + 16, N), f32),
        ],
        [
            *(pltpu.SMEM(value.shape, i32) for value in arguments[:2]),
            padded,
            pltpu.SemaphoreType.DMA((4,)),
            pltpu.SemaphoreType.DMA((4,)),
        ],
    )(scan_counts, *arguments)
    *others, own = call(window_kernel, [VMEM] * 3, [message] * (angles - 1), [padded])(shifts, slab_delta, slab_beta)
    windows = [own, following, *others]
    received = exchange(windows)
    previous = on_rows(slot, lambda i: i + 1)
    proj, core, cross = call(
        assemble_kernel,
        [VMEM] * (angles + 2),
        [field, halo, halo],
        [(angles, 2 * tile, N)],
    )(spots, previous, *received)
    core = on_rows(core, lambda i: i ^ 1)
    cross = on_rows(cross, lambda i: i + 1 if i % 2 else i - 1)
    trans, inner = call(
        inner_kernel,
        [VMEM, SMEM] + [VMEM] * 4,
        [field, field],
        [(N + 2 * SHIFT, N)],
        flops=3 * 10**9,
        bytes_accessed=3 * 10**6,
    )(spots, scan_counts, proj, probe, measured, tables)
    outgoing = call(
        edge_kernel,
        [VMEM, SMEM] + [VMEM] * 8,
        [message] * angles,
        [field[0], (2, 2, tile + N, N), (2, 2 * tile + 8, N), padded],
    )(spots, scan_counts, previous, core, cross, trans, inner, probe, measured, tables)
    received = exchange(outgoing)
    early = list(range(angles - 1))
    sums = call(
        functools.partial(slab_kernel, angles, early, False),
        [VMEM] * angles,
        [((2, 2, tile, N), f32)],
        flops=10**9,
        bytes_accessed=10**6,
    )(shifts, *received[:-1])[0]
    grad_delta, grad_beta = call(
        functools.partial(slab_kernel, angles, [angles - 1], True), [VMEM] * 3, [(slab, f32)] * 2
    )(shifts, received[-1], sums)
    return grad_delta.reshape(tile, 2, N), grad_beta.reshape(tile, 2, N)


def solution(mesh):
    placed = (
        P("rows", None, "ang"),
        P("rows", None, "ang"),
        P(),
        P(),
        P("ang", "rows", None, None),
        P("ang", "rows", None),
        P("ang", "rows"),
    )
    return jax.shard_map(
        on_device,
        mesh=mesh,
        in_specs=placed,
        out_specs=(P("rows", None, "ang"), P("rows", None, "ang")),
        check_vma=False,
    )
```

```python
import functools
import math

import jax
import jax.numpy as jnp
import ml_dtypes
import numpy as np
from jax import lax
from jax.experimental import pallas as pl
from jax.experimental.pallas import tpu as pltpu
from jax.sharding import PartitionSpec as P

N = 128
SHIFT = 8
AMP_FLOOR = 0.1
PACK_ROWS = 48
EDGE_ROWS = 8

f32, bf16, i32 = jnp.float32, jnp.bfloat16, jnp.int32
VMEM = pl.BlockSpec(memory_space=pltpu.VMEM)
SMEM = pl.BlockSpec(memory_space=pltpu.SMEM)
HBM = pl.BlockSpec(memory_space=pltpu.HBM)


def fourier_tables():
    counter = np.arange(N)
    angle = (counter[:, None] * counter[None, :] % N) * (2.0 * math.pi / N)
    re, im = np.cos(angle) / math.sqrt(N), -np.sin(angle) / math.sqrt(N)
    right = np.block([[re, im], [-im, re]])
    tables = []
    for table in (right, right.T):
        high = table.astype(ml_dtypes.bfloat16)
        tables += [high, (table - high.astype(np.float64)).astype(ml_dtypes.bfloat16)]
    return np.stack(tables)


def lane_iota(rows):
    return lax.broadcasted_iota(i32, (rows, N), 1)


def roll_lanes(value, by):
    return pltpu.roll(value, by, 1)


def roll_left(value, by):
    return pltpu.roll(value, lax.rem(N - by, N), 1)


def groups_of(rows):
    return [(g, start, min(PACK_ROWS, rows - start)) for g, start in enumerate(range(0, rows, PACK_ROWS))]


def packed_message(main, margins, scratch):
    rows = main.shape[0]
    scratch[0:rows, :] = margins
    packed = None
    for g, start, _ in groups_of(rows):
        part = scratch[start : start + PACK_ROWS, :]
        part = roll_lanes(part, 16 * g) if g else part
        packed = part if packed is None else packed + part
    return jnp.concatenate([main, packed], 0).astype(bf16)


def margins_of(message, rows):
    packed = message[rows:, :]
    parts = []
    for g, _, size in groups_of(rows):
        part = roll_lanes(packed, N - 16 * g) if g else packed
        parts.append(part[:size])
    return jnp.concatenate(parts, 0)


def window_message(shift_of, slab_delta, slab_beta, scratch):
    tile = slab_delta.shape[0] // 2
    lane = lane_iota(tile)
    mains, margins = [], []
    for ref in (slab_delta, slab_beta):
        main = margin = None
        for z in range(2):
            s = shift_of(z)
            rolled = pltpu.roll(ref[pl.ds(z, tile, stride=2), :], lax.rem(N - s, N), 1)
            source = lane + s
            inside = (source >= 0) & (source < N)
            kept, out_of = jnp.where(inside, rolled, 0.0), jnp.where(inside, 0.0, rolled)
            main = kept if z == 0 else main + kept
            margin = out_of if z == 0 else margin + out_of
        mains.append(main)
        margins.append(margin)
    scratch[2 * tile :, :] = jnp.zeros((scratch.shape[0] - 2 * tile, N), f32)
    return packed_message(jnp.concatenate(mains, 0), jnp.concatenate(margins, 0), scratch)


def first_kernel(angles, counts, *refs):
    sources, targets = refs[:6], refs[6:11]
    shifts, out, slot, scalar_shifts, scalar_spots, scratch, first_sems, second_sems = refs[11:]
    spots, slab_delta, slab_beta, _, measured = targets
    first = [
        pltpu.make_async_copy(source, target, first_sems.at[k])
        for k, (source, target) in enumerate(
            [*zip(sources[:4], (scalar_shifts, scalar_spots, slab_delta, slab_beta))]
        )
    ]
    second = [
        pltpu.make_async_copy(source, target, second_sems.at[k])
        for k, (source, target) in enumerate([(sources[1], spots), *zip(sources[4:], targets[3:])])
    ]
    for copy in first + second:
        copy.start()
    for copy in first:
        copy.wait()
    me = lax.axis_index("ang")
    first_angle = lax.rem(me + 1, angles)
    out[...] = window_message(lambda z: scalar_shifts[z, first_angle], slab_delta, slab_beta, scratch)
    for d in range(angles):
        angle = lax.rem(me + d, angles)
        for z in range(2):
            shifts[2 * d + z : 2 * d + z + 1, :] = jnp.full((1, N), scalar_shifts[z, angle], i32)
    for copy in second:
        copy.wait()
    slot[0:N, :] = measured[0]
    row = jnp.where(counts[0, 0] > 0, scalar_spots[0, 0], 0)
    slot[N : N + 8, :] = jnp.full((8, N), row, i32).astype(f32)
    slot[N + 8 :, :] = jnp.full((8, N), scalar_spots[1, 0], i32).astype(f32)


def window_kernel(shifts, slab_delta, slab_beta, *refs):
    outs, scratch = refs[:-1], refs[-1]
    angles = len(outs) + 1
    for out, d in zip(outs, [*range(2, angles), 0]):
        out[...] = window_message(lambda z: shifts[2 * d + z, 0], slab_delta, slab_beta, scratch)


def slot_position(slot):
    return slot[N, 0].astype(i32), slot[N + 8, 0].astype(i32)


def block_of(column, blocks):
    first, offset = column // N, lax.rem(column, N)
    return first, jnp.minimum(first + 1, blocks - 1), offset


def is_even():
    return lax.rem(lax.axis_index("rows"), 2) == 0


def unpack_kernel(blocks, steps, *refs):
    received, (proj, margins) = refs[: len(steps)], refs[-2:]
    tile = proj.shape[2]
    me = lax.axis_index("ang")
    for d, ref in zip(steps, received):
        block = lax.rem(me + (blocks - d), blocks)
        message = ref[...].astype(f32)
        proj[0, block] = message[:tile]
        proj[1, block] = message[tile : 2 * tile]
        margins[block] = margins_of(message, 2 * tile)


def assemble_kernel(spots, slot, message, proj_in, margins_in, core, cross, proj, margins):
    blocks, tile = proj.shape[1], proj.shape[2]
    unpack_kernel(blocks, [blocks - 1], message, proj, margins)
    lane = lane_iota(tile)
    for block in range(blocks):
        before, after = (block - 1) % blocks, (block + 1) % blocks
        for c in range(2):
            part = slice(c * tile, (c + 1) * tile)
            extra = jnp.where(lane < SHIFT, margins[before, part], 0.0)
            extra += jnp.where(lane >= N - SHIFT, margins[after, part], 0.0)
            proj[c, block] += extra
    _, previous = slot_position(slot)
    lane = lane_iota(N)
    even = is_even()
    for upper in (True, False):
        first, second, offset = block_of(spots[1, 0] if upper else previous, blocks)
        start = EDGE_ROWS if upper else 0
        for c in range(2):
            left = roll_left(proj[c, first, start : start + N, :], offset)
            right = roll_left(proj[c, second, start : start + N, :], offset)
            value = jnp.where(lane < N - offset, left, right).astype(bf16)
            part = slice(c * N, (c + 1) * N)

            @pl.when(even == upper)
            def _():
                core[part, :] = value

            @pl.when(even != upper)
            def _():
                cross[part, :] = value


def transmit(phase, absorb):
    turns = jnp.round(phase * (2.0 / math.pi))
    r = phase - turns * 1.5703125
    r = r - turns * 4.837512969970703125e-4
    r = r - turns * 7.54978995489188e-8
    z = r * r
    sine = r + r * z * (-1.6666654611e-1 + z * (8.3321608736e-3 - z * 1.9515295891e-4))
    cosine = 1.0 - 0.5 * z + z * z * (4.166664568298827e-2 + z * (-1.388731625493765e-3 + z * 2.443315711809948e-5))
    quarter = turns.astype(i32)
    odd = (quarter & 1) == 1
    damping = jnp.exp(-absorb)
    out_cos = jnp.where(odd, sine, cosine)
    out_sin = jnp.where(odd, cosine, sine)
    out_cos = jnp.where(((quarter + 1) & 2) == 2, -out_cos, out_cos)
    out_sin = jnp.where((quarter & 2) == 2, -out_sin, out_sin)
    return damping * out_cos, damping * out_sin


def split(value):
    high = value.astype(bf16)
    return high, (value - high.astype(f32)).astype(bf16)


def dot(a, b):
    return jnp.dot(a, b, preferred_element_type=f32)


def times_right(value, high, low):
    vh, vl = split(value)
    return dot(vh, high) + (dot(vl, high) + dot(vh, low))


def times_left(high, low, value):
    vh, vl = split(value)
    return dot(high, vh) + (dot(high, vl) + dot(low, vh))


def scan_gradients(patches, measured, weights, probe, tables):
    probe_re, probe_im = probe[0], probe[1]
    right_high, right_low, left_high, left_low = (tables[t] for t in range(4))
    rows = [
        jnp.concatenate([probe_re * re - probe_im * im, probe_re * im + probe_im * re], 1)
        for re, im in patches
    ]
    half = times_right(jnp.concatenate(rows, 0), right_high, right_low)
    count = len(patches)
    stacked = jnp.concatenate(
        [
            jnp.concatenate([half[j * N : (j + 1) * N, part * N : (part + 1) * N] for j in range(count)], 1)
            for part in range(2)
        ],
        0,
    )
    far = times_left(left_high, left_low, stacked)
    far_re, far_im = far[:N], far[N:]
    squared = far_re * far_re + far_im * far_im
    inverse = lax.rsqrt(jnp.maximum(squared, AMP_FLOOR * AMP_FLOOR))
    amplitude = jnp.concatenate([m for m in measured], 1)
    factor = 1.0 - amplitude * inverse
    factor = jnp.concatenate(
        [factor[:, j * N : (j + 1) * N] * weights[j] for j in range(count)], 1
    )
    residual = jnp.concatenate([far_re * factor, far_im * factor], 0)
    half = times_left(right_high, right_low, residual)
    rows = [
        jnp.concatenate([half[:N, j * N : (j + 1) * N], half[N:, j * N : (j + 1) * N]], 1)
        for j in range(count)
    ]
    back = times_right(jnp.concatenate(rows, 0), left_high, left_low)
    grads = []
    for j in range(count):
        re, im = back[j * N : (j + 1) * N, :N], back[j * N : (j + 1) * N, N:]
        grads.append((probe_re * re + probe_im * im, probe_re * im - probe_im * re))
    return grads


def patch_of(values, lane, offset, first, second, rows):
    pair = []
    for c in range(2):
        left = roll_left(values[c, first, rows, :], offset)
        right = roll_left(values[c, second, rows, :], offset)
        pair.append(jnp.where(lane < N - offset, left, right))
    return pair


def chain_back(patch, grad):
    (tr, ti), (gr, gi) = patch, grad
    return tr * gi - ti * gr, -(tr * gr + ti * gi)


def add_patch(total, c, rows, value, lane, offset, first, second):
    placed = roll_lanes(value, offset)
    total[c, first, rows, :] += jnp.where(lane >= offset, placed, 0.0)
    total[c, second, rows, :] += jnp.where(lane < offset, placed, 0.0)


def inner_kernel(spots, counts, proj, probe, measured, tables, trans, grad, frame):
    blocks, tile = proj.shape[1], proj.shape[2]
    for block in range(blocks):
        re, im = transmit(proj[0, block], proj[1, block])
        trans[0, block] = re
        trans[1, block] = im
    grad[...] = jnp.zeros(grad.shape, f32)
    frame[0:SHIFT, :] = jnp.zeros((SHIFT, N), f32)
    frame[SHIFT + N :, :] = jnp.zeros((SHIFT, N), f32)
    slots = measured.shape[0]
    lane = lane_iota(N)
    patches, weights = [], []
    for slot in range(1, slots):
        row = jnp.minimum(spots[0, slot], EDGE_ROWS)
        first, second, offset = block_of(spots[1, slot], blocks)
        patches.append(patch_of(trans, lane, offset, first, second, pl.ds(row, N)))
        weights.append(jnp.where(slot < counts[0, 0], 1.0, 0.0).astype(f32))
    grads = scan_gradients(patches, [measured[slot] for slot in range(1, slots)], weights, probe, tables)
    lane = lane_iota(tile)
    for slot in range(1, slots):
        row = jnp.minimum(spots[0, slot], EDGE_ROWS)
        first, second, offset = block_of(spots[1, slot], blocks)
        chained = chain_back(patches[slot - 1], grads[slot - 1])
        for c in range(2):
            frame[SHIFT : SHIFT + N, :] = chained[c]
            add_patch(grad, c, slice(None), frame[pl.ds(SHIFT - row, tile), :], lane, offset, first, second)


def gradient_message(block, total, scratch):
    blocks, tile = total.shape[1], total.shape[2]
    scratch[2 * tile :, :] = jnp.zeros((scratch.shape[0] - 2 * tile, N), f32)
    lane = lane_iota(tile)
    before, after = lax.rem(block + (blocks - 1), blocks), lax.rem(block + 1, blocks)
    mains, margins = [], []
    for c in range(2):
        mains.append(total[c, block])
        margin = jnp.where(lane < SHIFT, total[c, after], 0.0)
        margins.append(jnp.where(lane >= N - SHIFT, total[c, before], margin))
    return packed_message(jnp.concatenate(mains, 0), jnp.concatenate(margins, 0), scratch)


def cut_kernel(total, *refs):
    outs, scratch = refs[:-1], refs[-1]
    blocks = total.shape[1]
    me = lax.axis_index("ang")
    for out, d in zip(outs, [*range(2, blocks), 0]):
        out[...] = gradient_message(lax.rem(me + d, blocks), total, scratch)


def edge_kernel(spots, counts, slot, core, cross, trans, inner, probe, measured, tables, out, total, patch, frame, scratch):
    blocks, tile = trans.shape[1], trans.shape[2]
    even = is_even()
    own_row, own_column = spots[0, 0], spots[1, 0]
    prev_row, prev_column = slot_position(slot)
    own_block, prev_block = block_of(own_column, blocks), block_of(prev_column, blocks)
    last = lax.axis_index("rows") == lax.axis_size("rows") - 1
    near, away = core[...].astype(f32), cross[...].astype(f32)
    below = jnp.where(last, 0.0, jnp.where(even, near, away))
    above = jnp.where(even, away, near)
    re, im = transmit(below[:N], below[N:])
    patch[0, 0, tile:, :] = re
    patch[0, 1, tile:, :] = im
    re, im = transmit(above[:N], above[N:])
    patch[1, 0, EDGE_ROWS:tile, :] = re
    patch[1, 1, EDGE_ROWS:tile, :] = im
    first, second, offset = own_block
    pair = patch_of(trans, lane_iota(tile), offset, first, second, slice(None))
    for c in range(2):
        patch[0, c, 0:tile, :] = pair[c]
    first, second, offset = prev_block
    pair = patch_of(trans, lane_iota(N), offset, first, second, slice(0, N))
    for c in range(2):
        patch[1, c, tile:, :] = pair[c]
    reaches = (prev_row > EDGE_ROWS) & (lax.axis_index("rows") > 0)
    start = jnp.maximum(prev_row, EDGE_ROWS)
    patches = [
        [patch[0, c, pl.ds(own_row, N), :] for c in range(2)],
        [patch[1, c, pl.ds(start, N), :] for c in range(2)],
    ]
    weights = [jnp.where(flag, 1.0, 0.0).astype(f32) for flag in (counts[0, 0] > 0, reaches)]
    grads = scan_gradients(patches, [measured[0], slot[0:N, :]], weights, probe, tables)
    chained = [chain_back(pair, grad) for pair, grad in zip(patches, grads)]
    first, second, offset = own_block
    for c in range(2):
        frame[c, 0:tile, :] = jnp.zeros((tile, N), f32)
        frame[c, tile : tile + N, :] = chained[0][c]
        frame[c, tile + N :, :] = jnp.zeros((frame.shape[1] - tile - N, N), f32)
        rows = frame[c, pl.ds(tile - own_row, tile), :]
        add_patch(total, c, slice(None), rows, lane_iota(tile), offset, first, second)
    first, second, offset = prev_block
    for c in range(2):
        frame[c, 0:N, :] = chained[1][c]
        frame[c, N : 2 * N, :] = jnp.zeros((N, N), f32)
        rows = frame[c, pl.ds(tile - start, N), :]
        add_patch(total, c, slice(0, N), rows, lane_iota(N), offset, first, second)
    out[...] = gradient_message(lax.rem(lax.axis_index("ang") + 1, blocks), total, scratch)


def slab_kernel(angles, steps, last, shifts, *refs):
    refs, outs = (refs[:-2], refs[-2:]) if last else (refs[:-1], refs[-1:])
    received, before = refs[: len(steps)], refs[len(steps) :]
    tile = (received[0].shape[0] - PACK_ROWS) // 2
    lane = lane_iota(tile)
    sums = [[before[0][c, z] if before else None for z in range(2)] for c in range(2)]
    for d, ref in zip(steps, received):
        message = ref[...].astype(f32)
        margins = margins_of(message, 2 * tile)
        for z in range(2):
            s = shifts[2 * ((angles - d) % angles) + z, 0]
            target = lane + s
            inside = (target >= 0) & (target < N)
            for c in range(2):
                part = slice(c * tile, (c + 1) * tile)
                value = jnp.where(inside, message[part], margins[part])
                value = pltpu.roll(value, lax.rem(s + N, N), 1)
                sums[c][z] = value if sums[c][z] is None else sums[c][z] + value
    for c in range(2):
        for z in range(2):
            if last:
                outs[c][pl.ds(z, tile, stride=2), :] = sums[c][z]
            else:
                outs[0][c, z] = sums[c][z]


def call(kernel, ins, outs, scratch=(), flops=0, bytes_accessed=0, aliases=()):
    scratch = [pltpu.VMEM(item, f32) if isinstance(item, tuple) else item for item in scratch]
    return pl.pallas_call(
        kernel,
        in_specs=ins,
        out_specs=[VMEM] * len(outs),
        out_shape=[jax.ShapeDtypeStruct(shape, dtype) for shape, dtype in outs],
        scratch_shapes=scratch,
        input_output_aliases=dict(aliases),
        compiler_params=pltpu.CompilerParams(vmem_limit_bytes=32 * 1024 * 1024),
        cost_estimate=pl.CostEstimate(flops=flops, bytes_accessed=bytes_accessed, transcendentals=0),
    )


def exchange(messages):
    count = lax.axis_size("ang")
    received = [messages[0]]
    for d in range(1, count):
        received.append(lax.ppermute(messages[d], "ang", [(i, (i + d) % count) for i in range(count)]))
    return received


def on_rows(value, target):
    count = lax.axis_size("rows")
    return lax.ppermute(value, "rows", [(i, target(i) % count) for i in range(count)])


def on_device(delta_obj, beta_obj, layer_shifts, illumination_field, amplitudes, positions, scan_counts):
    tile = delta_obj.shape[0]
    angles = lax.axis_size("ang")
    message = ((2 * tile + PACK_ROWS, N), bf16)
    padded = (len(groups_of(2 * tile)) * PACK_ROWS, N)
    field = ((2, angles, tile, N), f32)
    slab = (2 * tile, N)
    halo = ((2 * N, N), bf16)
    shifts, spots = layer_shifts.T, positions[0].T
    tables = jnp.asarray(fourier_tables())

    arguments = [
        pltpu.with_memory_space_constraint(value, pltpu.HBM)
        for value in (
            shifts,
            spots,
            delta_obj.reshape(slab),
            beta_obj.reshape(slab),
            illumination_field,
            amplitudes[0],
        )
    ]
    spots, slab_delta, slab_beta, probe, measured, shifts, following, slot = call(
        functools.partial(first_kernel, angles),
        [SMEM] + [HBM] * len(arguments),
        [
            *((value.shape, value.dtype) for value in arguments[1:]),
            ((2 * angles, N), i32),
            message,
            ((N + 16, N), f32),
        ],
        [
            *(pltpu.SMEM(value.shape, i32) for value in arguments[:2]),
            padded,
            pltpu.SemaphoreType.DMA((4,)),
            pltpu.SemaphoreType.DMA((4,)),
        ],
    )(scan_counts, *arguments)
    *others, own = call(window_kernel, [VMEM] * 3, [message] * (angles - 1), [padded])(shifts, slab_delta, slab_beta)
    windows = [own, following, *others]
    received = exchange(windows)
    previous = on_rows(slot, lambda i: i + 1)
    rows = ((angles, 2 * tile, N), f32)
    early = list(range(angles - 1))
    partly = call(
        functools.partial(unpack_kernel, angles, early),
        [VMEM] * (angles - 1),
        [field, rows],
        flops=10**9,
        bytes_accessed=10**6,
    )(*received[:-1])
    core, cross, proj, _ = call(
        assemble_kernel, [VMEM] * 5, [halo, halo, field, rows], aliases={3: 2, 4: 3}
    )(spots, previous, received[-1], *partly)
    core = on_rows(core, lambda i: i ^ 1)
    cross = on_rows(cross, lambda i: i + 1 if i % 2 else i - 1)
    trans, inner = call(
        inner_kernel,
        [VMEM, SMEM] + [VMEM] * 4,
        [field, field],
        [(N + 2 * SHIFT, N)],
        flops=3 * 10**9,
        bytes_accessed=3 * 10**6,
    )(spots, scan_counts, proj, probe, measured, tables)
    following, total = call(
        edge_kernel,
        [VMEM, SMEM] + [VMEM] * 8,
        [message, field],
        [(2, 2, tile + N, N), (2, 2 * tile + 8, N), padded],
        aliases={6: 1},
    )(spots, scan_counts, previous, core, cross, trans, inner, probe, measured, tables)
    *others, own = call(cut_kernel, [VMEM], [message] * (angles - 1), [padded])(total)
    received = exchange([own, following, *others])
    sums = call(
        functools.partial(slab_kernel, angles, early, False),
        [VMEM] * angles,
        [((2, 2, tile, N), f32)],
        flops=10**9,
        bytes_accessed=10**6,
    )(shifts, *received[:-1])[0]
    grad_delta, grad_beta = call(
        functools.partial(slab_kernel, angles, [angles - 1], True), [VMEM] * 3, [(slab, f32)] * 2
    )(shifts, received[-1], sums)
    return grad_delta.reshape(tile, 2, N), grad_beta.reshape(tile, 2, N)


def solution(mesh):
    placed = (
        P("rows", None, "ang"),
        P("rows", None, "ang"),
        P(),
        P(),
        P("ang", "rows", None, None),
        P("ang", "rows", None),
        P("ang", "rows"),
    )
    return jax.shard_map(
        on_device,
        mesh=mesh,
        in_specs=placed,
        out_specs=(P("rows", None, "ang"), P("rows", None, "ang")),
        check_vma=False,
    )
```

```python
import functools
import math

import jax
import jax.numpy as jnp
import ml_dtypes
import numpy as np
from jax import lax
from jax.experimental import pallas as pl
from jax.experimental.pallas import tpu as pltpu
from jax.sharding import PartitionSpec as P

N = 128
SHIFT = 8
AMP_FLOOR = 0.1
PACK_ROWS = 40
EDGE_ROWS = 8

f32, bf16, i32 = jnp.float32, jnp.bfloat16, jnp.int32
VMEM = pl.BlockSpec(memory_space=pltpu.VMEM)
SMEM = pl.BlockSpec(memory_space=pltpu.SMEM)
HBM = pl.BlockSpec(memory_space=pltpu.HBM)


def fourier_tables():
    counter = np.arange(N)
    angle = (counter[:, None] * counter[None, :] % N) * (2.0 * math.pi / N)
    re, im = np.cos(angle) / math.sqrt(N), -np.sin(angle) / math.sqrt(N)
    right = np.block([[re, im], [-im, re]])
    tables = []
    for table in (right, right.T):
        high = table.astype(ml_dtypes.bfloat16)
        tables += [high, (table - high.astype(np.float64)).astype(ml_dtypes.bfloat16)]
    return np.stack(tables)


def lane_iota(rows):
    return lax.broadcasted_iota(i32, (rows, N), 1)


def roll_lanes(value, by):
    return pltpu.roll(value, by, 1)


def roll_left(value, by):
    return pltpu.roll(value, lax.rem(N - by, N), 1)


def groups_of(rows):
    return [(g, start, min(PACK_ROWS, rows - start)) for g, start in enumerate(range(0, rows, PACK_ROWS))]


def packed_message(main, margins, scratch):
    rows = main.shape[0]
    scratch[0:rows, :] = margins
    packed = None
    for g, start, _ in groups_of(rows):
        part = scratch[start : start + PACK_ROWS, :]
        part = roll_lanes(part, 16 * g) if g else part
        packed = part if packed is None else packed + part
    return jnp.concatenate([main, packed], 0).astype(bf16)


def margins_of(message, rows):
    packed = message[rows:, :]
    parts = []
    for g, _, size in groups_of(rows):
        part = roll_lanes(packed, N - 16 * g) if g else packed
        parts.append(part[:size])
    return jnp.concatenate(parts, 0)


def window_message(shift_of, slab_delta, slab_beta, scratch):
    tile = slab_delta.shape[0] // 2
    lane = lane_iota(tile)
    mains, margins = [], []
    for ref in (slab_delta, slab_beta):
        main = margin = None
        for z in range(2):
            s = shift_of(z)
            rolled = pltpu.roll(ref[pl.ds(z, tile, stride=2), :], lax.rem(N - s, N), 1)
            source = lane + s
            inside = (source >= 0) & (source < N)
            kept, out_of = jnp.where(inside, rolled, 0.0), jnp.where(inside, 0.0, rolled)
            main = kept if z == 0 else main + kept
            margin = out_of if z == 0 else margin + out_of
        mains.append(main)
        margins.append(margin)
    scratch[2 * tile :, :] = jnp.zeros((scratch.shape[0] - 2 * tile, N), f32)
    return packed_message(jnp.concatenate(mains, 0), jnp.concatenate(margins, 0), scratch)


def first_kernel(
    angles, shifts_in, spots_in, delta, beta, measured_in,
    slab_delta, slab_beta, shifts, out, slot, scalar_shifts, scalar_spots, scratch, sems,
):
    copies = [
        pltpu.make_async_copy(source, target, sems.at[k])
        for k, (source, target) in enumerate(
            [
                (shifts_in, scalar_shifts),
                (spots_in, scalar_spots),
                (delta, slab_delta),
                (beta, slab_beta),
                (measured_in.at[0], slot.at[0:N]),
            ]
        )
    ]
    for copy in copies:
        copy.start()
    me = lax.axis_index("ang")
    for copy in copies[:2]:
        copy.wait()
    for d in range(angles):
        angle = lax.rem(me + d, angles)
        for z in range(2):
            shifts[2 * d + z : 2 * d + z + 1, :] = jnp.full((1, N), scalar_shifts[z, angle], i32)
    slot[N : N + 8, :] = jnp.full((8, N), scalar_spots[0, 0], i32).astype(f32)
    slot[N + 8 :, :] = jnp.full((8, N), scalar_spots[1, 0], i32).astype(f32)
    following = lax.rem(me + 1, angles)
    for copy in copies[2:]:
        copy.wait()
    out[...] = window_message(lambda z: scalar_shifts[z, following], slab_delta, slab_beta, scratch)


def window_kernel(shifts, slab_delta, slab_beta, *refs):
    outs, scratch = refs[:-1], refs[-1]
    for k, out in enumerate(outs):
        d = k + 2
        out[...] = window_message(lambda z: shifts[2 * d + z, 0], slab_delta, slab_beta, scratch)


def load_kernel(
    counts_in, shifts, slab_delta, slab_beta, _, spots_in, probe_in, measured_in,
    own, counts, spots, probe, measured, scratch, sems,
):
    copies = [
        pltpu.make_async_copy(source, target, sems.at[k])
        for k, (source, target) in enumerate([(spots_in, spots), (probe_in, probe), (measured_in, measured)])
    ]
    for copy in copies:
        copy.start()
    own[...] = window_message(lambda z: shifts[z, 0], slab_delta, slab_beta, scratch)
    counts[...] = jnp.full(counts.shape, counts_in[0, 0], i32)
    for copy in copies:
        copy.wait()


def slot_position(slot):
    return slot[N, 0].astype(i32), slot[N + 8, 0].astype(i32)


def block_of(column, blocks):
    first, offset = column // N, lax.rem(column, N)
    return first, jnp.minimum(first + 1, blocks - 1), offset


def is_even():
    return lax.rem(lax.axis_index("rows"), 2) == 0


def unpack_kernel(blocks, steps, *refs):
    received, (proj, margins) = refs[: len(steps)], refs[-2:]
    tile = proj.shape[2]
    me = lax.axis_index("ang")
    for d, ref in zip(steps, received):
        block = lax.rem(me + (blocks - d), blocks)
        message = ref[...].astype(f32)
        proj[0, block] = message[:tile]
        proj[1, block] = message[tile : 2 * tile]
        margins[block] = margins_of(message, 2 * tile)


def assemble_kernel(spots, slot, message, proj_in, margins_in, core, cross, proj, margins):
    blocks, tile = proj.shape[1], proj.shape[2]
    unpack_kernel(blocks, [blocks - 1], message, proj, margins)
    lane = lane_iota(tile)
    for block in range(blocks):
        before, after = (block - 1) % blocks, (block + 1) % blocks
        for c in range(2):
            part = slice(c * tile, (c + 1) * tile)
            extra = jnp.where(lane < SHIFT, margins[before, part], 0.0)
            extra += jnp.where(lane >= N - SHIFT, margins[after, part], 0.0)
            proj[c, block] += extra
    _, previous = slot_position(slot)
    own = spots[1, 0]
    lane = lane_iota(N)
    even = is_even()
    for out, upper in ((core, even), (cross, jnp.logical_not(even))):
        first, second, offset = block_of(jnp.where(upper, own, previous), blocks)
        rows = pl.ds(pl.multiple_of(jnp.where(upper, EDGE_ROWS, 0), 8), N)
        pair = patch_of(proj, lane, offset, first, second, rows)
        out[...] = jnp.concatenate(pair, 0).astype(bf16)


def transmit(phase, absorb):
    turns = jnp.round(phase * (2.0 / math.pi))
    r = phase - turns * 1.5703125
    r = r - turns * 4.837512969970703125e-4
    r = r - turns * 7.54978995489188e-8
    z = r * r
    sine = r + r * z * (-1.6666654611e-1 + z * (8.3321608736e-3 - z * 1.9515295891e-4))
    cosine = 1.0 - 0.5 * z + z * z * (4.166664568298827e-2 + z * (-1.388731625493765e-3 + z * 2.443315711809948e-5))
    quarter = turns.astype(i32)
    odd = (quarter & 1) == 1
    damping = jnp.exp(-absorb)
    out_cos = jnp.where(odd, sine, cosine)
    out_sin = jnp.where(odd, cosine, sine)
    out_cos = jnp.where(((quarter + 1) & 2) == 2, -out_cos, out_cos)
    out_sin = jnp.where((quarter & 2) == 2, -out_sin, out_sin)
    return damping * out_cos, damping * out_sin


def split(value):
    high = value.astype(bf16)
    return high, (value - high.astype(f32)).astype(bf16)


def dot(a, b):
    return jnp.dot(a, b, preferred_element_type=f32)


def times_right(value, high, low):
    vh, vl = split(value)
    return dot(vh, high) + (dot(vl, high) + dot(vh, low))


def times_left(high, low, value):
    vh, vl = split(value)
    return dot(high, vh) + (dot(high, vl) + dot(low, vh))


def scan_gradients(patches, measured, weights, probe, tables):
    probe_re, probe_im = probe[0], probe[1]
    right_high, right_low, left_high, left_low = (tables[t] for t in range(4))
    rows = [
        jnp.concatenate([probe_re * re - probe_im * im, probe_re * im + probe_im * re], 1)
        for re, im in patches
    ]
    half = times_right(jnp.concatenate(rows, 0), right_high, right_low)
    count = len(patches)
    stacked = jnp.concatenate(
        [
            jnp.concatenate([half[j * N : (j + 1) * N, part * N : (part + 1) * N] for j in range(count)], 1)
            for part in range(2)
        ],
        0,
    )
    far = times_left(left_high, left_low, stacked)
    far_re, far_im = far[:N], far[N:]
    squared = far_re * far_re + far_im * far_im
    inverse = lax.rsqrt(jnp.maximum(squared, AMP_FLOOR * AMP_FLOOR))
    amplitude = jnp.concatenate([m for m in measured], 1)
    factor = 1.0 - amplitude * inverse
    factor = jnp.concatenate(
        [factor[:, j * N : (j + 1) * N] * weights[j] for j in range(count)], 1
    )
    residual = jnp.concatenate([far_re * factor, far_im * factor], 0)
    half = times_left(right_high, right_low, residual)
    rows = [
        jnp.concatenate([half[:N, j * N : (j + 1) * N], half[N:, j * N : (j + 1) * N]], 1)
        for j in range(count)
    ]
    back = times_right(jnp.concatenate(rows, 0), left_high, left_low)
    grads = []
    for j in range(count):
        re, im = back[j * N : (j + 1) * N, :N], back[j * N : (j + 1) * N, N:]
        grads.append((probe_re * re + probe_im * im, probe_re * im - probe_im * re))
    return grads


def patch_of(values, lane, offset, first, second, rows):
    pair = []
    for c in range(2):
        left = roll_left(values[c, first, rows, :], offset)
        right = roll_left(values[c, second, rows, :], offset)
        pair.append(jnp.where(lane < N - offset, left, right))
    return pair


def chain_back(patch, grad):
    (tr, ti), (gr, gi) = patch, grad
    return tr * gi - ti * gr, -(tr * gr + ti * gi)


def add_patch(total, c, rows, value, lane, offset, first, second):
    placed = roll_lanes(value, offset)
    total[c, first, rows, :] += jnp.where(lane >= offset, placed, 0.0)
    total[c, second, rows, :] += jnp.where(lane < offset, placed, 0.0)


def inner_kernel(spots, counts, proj, probe, measured, tables, trans, grad, frame):
    blocks, tile = proj.shape[1], proj.shape[2]
    for block in range(blocks):
        re, im = transmit(proj[0, block], proj[1, block])
        trans[0, block] = re
        trans[1, block] = im
    grad[...] = jnp.zeros(grad.shape, f32)
    frame[0:SHIFT, :] = jnp.zeros((SHIFT, N), f32)
    frame[SHIFT + N :, :] = jnp.zeros((SHIFT, N), f32)
    slots = measured.shape[0]
    lane = lane_iota(N)
    patches, weights = [], []
    for slot in range(1, slots):
        row = jnp.minimum(spots[0, slot], EDGE_ROWS)
        first, second, offset = block_of(spots[1, slot], blocks)
        patches.append(patch_of(trans, lane, offset, first, second, pl.ds(row, N)))
        weights.append(jnp.where(slot < counts[0, 0], 1.0, 0.0).astype(f32))
    grads = scan_gradients(patches, [measured[slot] for slot in range(1, slots)], weights, probe, tables)
    lane = lane_iota(tile)
    for slot in range(1, slots):
        row = jnp.minimum(spots[0, slot], EDGE_ROWS)
        first, second, offset = block_of(spots[1, slot], blocks)
        chained = chain_back(patches[slot - 1], grads[slot - 1])
        for c in range(2):
            frame[SHIFT : SHIFT + N, :] = chained[c]
            add_patch(grad, c, slice(None), frame[pl.ds(SHIFT - row, tile), :], lane, offset, first, second)


def gradient_message(block, total, scratch):
    blocks, tile = total.shape[1], total.shape[2]
    scratch[2 * tile :, :] = jnp.zeros((scratch.shape[0] - 2 * tile, N), f32)
    lane = lane_iota(tile)
    before, after = lax.rem(block + (blocks - 1), blocks), lax.rem(block + 1, blocks)
    mains, margins = [], []
    for c in range(2):
        mains.append(total[c, block])
        margin = jnp.where(lane < SHIFT, total[c, after], 0.0)
        margins.append(jnp.where(lane >= N - SHIFT, total[c, before], margin))
    return packed_message(jnp.concatenate(mains, 0), jnp.concatenate(margins, 0), scratch)


def edge_kernel(spots, counts, slot, core, cross, trans, inner, probe, measured, tables, *refs):
    outs, (total, patch, frame, scratch) = refs[:-4], refs[-4:]
    blocks, tile = trans.shape[1], trans.shape[2]
    even = is_even()
    own_row, own_column = spots[0, 0], spots[1, 0]
    prev_row, prev_column = slot_position(slot)
    own_block, prev_block = block_of(own_column, blocks), block_of(prev_column, blocks)
    last = lax.axis_index("rows") == lax.axis_size("rows") - 1
    near, away = core[...].astype(f32), cross[...].astype(f32)
    below = jnp.where(last, 0.0, jnp.where(even, near, away))
    above = jnp.where(even, away, near)
    re, im = transmit(below[:N], below[N:])
    patch[0, 0, tile:, :] = re
    patch[0, 1, tile:, :] = im
    re, im = transmit(above[:N], above[N:])
    patch[1, 0, EDGE_ROWS:tile, :] = re
    patch[1, 1, EDGE_ROWS:tile, :] = im
    first, second, offset = own_block
    pair = patch_of(trans, lane_iota(tile), offset, first, second, slice(None))
    for c in range(2):
        patch[0, c, 0:tile, :] = pair[c]
    first, second, offset = prev_block
    pair = patch_of(trans, lane_iota(N), offset, first, second, slice(0, N))
    for c in range(2):
        patch[1, c, tile:, :] = pair[c]
    reaches = (prev_row > EDGE_ROWS) & (lax.axis_index("rows") > 0)
    start = jnp.maximum(prev_row, EDGE_ROWS)
    patches = [
        [patch[0, c, pl.ds(own_row, N), :] for c in range(2)],
        [patch[1, c, pl.ds(start, N), :] for c in range(2)],
    ]
    weights = [jnp.where(flag, 1.0, 0.0).astype(f32) for flag in (counts[0, 0] > 0, reaches)]
    grads = scan_gradients(patches, [measured[0], slot[0:N, :]], weights, probe, tables)
    chained = [chain_back(pair, grad) for pair, grad in zip(patches, grads)]
    first, second, offset = own_block
    for c in range(2):
        frame[c, 0:tile, :] = jnp.zeros((tile, N), f32)
        frame[c, tile : tile + N, :] = chained[0][c]
        frame[c, tile + N :, :] = jnp.zeros((frame.shape[1] - tile - N, N), f32)
        rows = frame[c, pl.ds(tile - own_row, tile), :]
        add_patch(total, c, slice(None), rows, lane_iota(tile), offset, first, second)
    first, second, offset = prev_block
    for c in range(2):
        frame[c, 0:N, :] = chained[1][c]
        frame[c, N : 2 * N, :] = jnp.zeros((N, N), f32)
        rows = frame[c, pl.ds(tile - start, N), :]
        add_patch(total, c, slice(0, N), rows, lane_iota(N), offset, first, second)
    me = lax.axis_index("ang")
    for d, out in enumerate(outs):
        out[...] = gradient_message(lax.rem(me + d, blocks), total, scratch)


def slab_kernel(angles, steps, last, shifts, *refs):
    refs, outs = (refs[:-2], refs[-2:]) if last else (refs[:-1], refs[-1:])
    received, before = refs[: len(steps)], refs[len(steps) :]
    tile = (received[0].shape[0] - PACK_ROWS) // 2
    lane = lane_iota(tile)
    sums = [[before[0][c, z] if before else None for z in range(2)] for c in range(2)]
    for d, ref in zip(steps, received):
        message = ref[...].astype(f32)
        margins = margins_of(message, 2 * tile)
        for z in range(2):
            s = shifts[2 * ((angles - d) % angles) + z, 0]
            target = lane + s
            inside = (target >= 0) & (target < N)
            for c in range(2):
                part = slice(c * tile, (c + 1) * tile)
                value = jnp.where(inside, message[part], margins[part])
                value = pltpu.roll(value, lax.rem(s + N, N), 1)
                sums[c][z] = value if sums[c][z] is None else sums[c][z] + value
    for c in range(2):
        for z in range(2):
            if last:
                outs[c][pl.ds(z, tile, stride=2), :] = sums[c][z]
            else:
                outs[0][c, z] = sums[c][z]


def call(kernel, ins, outs, scratch=(), flops=0, bytes_accessed=0, aliases=()):
    scratch = [pltpu.VMEM(item, f32) if isinstance(item, tuple) else item for item in scratch]
    return pl.pallas_call(
        kernel,
        in_specs=ins,
        out_specs=[VMEM] * len(outs),
        out_shape=[jax.ShapeDtypeStruct(shape, dtype) for shape, dtype in outs],
        scratch_shapes=scratch,
        input_output_aliases=dict(aliases),
        compiler_params=pltpu.CompilerParams(vmem_limit_bytes=32 * 1024 * 1024),
        cost_estimate=pl.CostEstimate(flops=flops, bytes_accessed=bytes_accessed, transcendentals=0),
    )


def exchange(messages):
    count = lax.axis_size("ang")
    received = [messages[0]]
    for d in range(1, count):
        received.append(lax.ppermute(messages[d], "ang", [(i, (i + d) % count) for i in range(count)]))
    return received


def on_rows(value, target):
    count = lax.axis_size("rows")
    return lax.ppermute(value, "rows", [(i, target(i) % count) for i in range(count)])


def on_device(delta_obj, beta_obj, layer_shifts, illumination_field, amplitudes, positions, scan_counts):
    tile = delta_obj.shape[0]
    angles = lax.axis_size("ang")
    message = ((2 * tile + PACK_ROWS, N), bf16)
    padded = (len(groups_of(2 * tile)) * PACK_ROWS, N)
    field = ((2, angles, tile, N), f32)
    slab = (2 * tile, N)
    halo = ((2 * N, N), bf16)
    tables = jnp.asarray(fourier_tables())

    in_hbm = functools.partial(pltpu.with_memory_space_constraint, memory_space=pltpu.HBM)
    shifts, spots, probe, measured = (
        in_hbm(value) for value in (layer_shifts.T, positions[0].T, illumination_field, amplitudes[0])
    )
    slab_delta, slab_beta, shifts, following, slot = call(
        functools.partial(first_kernel, angles),
        [HBM] * 5,
        [(slab, f32), (slab, f32), ((2 * angles, N), i32), message, ((N + 16, N), f32)],
        [pltpu.SMEM(shifts.shape, i32), pltpu.SMEM(spots.shape, i32), padded, pltpu.SemaphoreType.DMA((5,))],
    )(shifts, spots, in_hbm(delta_obj.reshape(slab)), in_hbm(beta_obj.reshape(slab)), measured)
    others = call(window_kernel, [VMEM] * 3, [message] * (angles - 2), [padded])(shifts, slab_delta, slab_beta)
    own, counts, spots, probe, measured = call(
        load_kernel,
        [SMEM] + [VMEM] * 4 + [HBM] * 3,
        [message, ((8, N), i32)] + [(value.shape, value.dtype) for value in (spots, probe, measured)],
        [padded, pltpu.SemaphoreType.DMA((3,))],
        flops=10**9,
        bytes_accessed=10**6,
    )(scan_counts, shifts, slab_delta, slab_beta, others[-1], spots, probe, measured)
    windows = [own, following, *others]
    received = exchange(windows)
    previous = on_rows(slot, lambda i: i + 1)
    rows = ((angles, 2 * tile, N), f32)
    early = list(range(angles - 1))
    partly = call(
        functools.partial(unpack_kernel, angles, early),
        [VMEM] * (angles - 1),
        [field, rows],
        flops=10**9,
        bytes_accessed=10**6,
    )(*received[:-1])
    core, cross, proj, _ = call(
        assemble_kernel, [VMEM] * 5, [halo, halo, field, rows], aliases={3: 2, 4: 3}
    )(spots, previous, received[-1], *partly)
    core = on_rows(core, lambda i: i ^ 1)
    cross = on_rows(cross, lambda i: i + 1 if i % 2 else i - 1)
    trans, inner = call(
        inner_kernel,
        [VMEM] * 6,
        [field, field],
        [(N + 2 * SHIFT, N)],
        flops=3 * 10**9,
        bytes_accessed=3 * 10**6,
    )(spots, counts, proj, probe, measured, tables)
    *outgoing, _ = call(
        edge_kernel,
        [VMEM] * 10,
        [message] * angles + [field],
        [(2, 2, tile + N, N), (2, 2 * tile + 8, N), padded],
        aliases={6: angles},
    )(spots, counts, previous, core, cross, trans, inner, probe, measured, tables)
    received = exchange(outgoing)
    early = list(range(angles - 1))
    sums = call(
        functools.partial(slab_kernel, angles, early, False),
        [VMEM] * angles,
        [((2, 2, tile, N), f32)],
        flops=10**9,
        bytes_accessed=10**6,
    )(shifts, *received[:-1])[0]
    grad_delta, grad_beta = call(
        functools.partial(slab_kernel, angles, [angles - 1], True), [VMEM] * 3, [(slab, f32)] * 2
    )(shifts, received[-1], sums)
    return grad_delta.reshape(tile, 2, N), grad_beta.reshape(tile, 2, N)


def solution(mesh):
    placed = (
        P("rows", None, "ang"),
        P("rows", None, "ang"),
        P(),
        P(),
        P("ang", "rows", None, None),
        P("ang", "rows", None),
        P("ang", "rows"),
    )
    return jax.shard_map(
        on_device,
        mesh=mesh,
        in_specs=placed,
        out_specs=(P("rows", None, "ang"), P("rows", None, "ang")),
        check_vma=False,
    )
```

```python
import functools
import math

import jax
import jax.numpy as jnp
import ml_dtypes
import numpy as np
from jax import lax
from jax.experimental import pallas as pl
from jax.experimental.pallas import tpu as pltpu
from jax.sharding import PartitionSpec as P

N = 128
SHIFT = 8
AMP_FLOOR = 0.1
PACK_ROWS = 40
EDGE_ROWS = 8

f32, bf16, i32 = jnp.float32, jnp.bfloat16, jnp.int32
VMEM = pl.BlockSpec(memory_space=pltpu.VMEM)
SMEM = pl.BlockSpec(memory_space=pltpu.SMEM)
HBM = pl.BlockSpec(memory_space=pltpu.HBM)


def fourier_tables():
    counter = np.arange(N)
    angle = (counter[:, None] * counter[None, :] % N) * (2.0 * math.pi / N)
    re, im = np.cos(angle) / math.sqrt(N), -np.sin(angle) / math.sqrt(N)
    right = np.block([[re, im], [-im, re]])
    tables = []
    for table in (right, right.T):
        high = table.astype(ml_dtypes.bfloat16)
        tables += [high, (table - high.astype(np.float64)).astype(ml_dtypes.bfloat16)]
    return np.stack(tables)


def lane_iota(rows):
    return lax.broadcasted_iota(i32, (rows, N), 1)


def roll_lanes(value, by):
    return pltpu.roll(value, by, 1)


def roll_left(value, by):
    return pltpu.roll(value, lax.rem(N - by, N), 1)


def groups_of(rows):
    return [(g, start, min(PACK_ROWS, rows - start)) for g, start in enumerate(range(0, rows, PACK_ROWS))]


def packed_message(main, margins, scratch):
    rows = main.shape[0]
    scratch[0:rows, :] = margins
    packed = None
    for g, start, _ in groups_of(rows):
        part = scratch[start : start + PACK_ROWS, :]
        part = roll_lanes(part, 16 * g) if g else part
        packed = part if packed is None else packed + part
    return jnp.concatenate([main, packed], 0).astype(bf16)


def margins_of(message, rows):
    packed = message[rows:, :]
    parts = []
    for g, _, size in groups_of(rows):
        part = roll_lanes(packed, N - 16 * g) if g else packed
        parts.append(part[:size])
    return jnp.concatenate(parts, 0)


def window_message(shift_of, slab_delta, slab_beta, scratch):
    tile = slab_delta.shape[0] // 2
    lane = lane_iota(tile)
    mains, margins = [], []
    for ref in (slab_delta, slab_beta):
        main = margin = None
        for z in range(2):
            s = shift_of(z)
            rolled = pltpu.roll(ref[pl.ds(z, tile, stride=2), :], lax.rem(N - s, N), 1)
            source = lane + s
            inside = (source >= 0) & (source < N)
            kept, out_of = jnp.where(inside, rolled, 0.0), jnp.where(inside, 0.0, rolled)
            main = kept if z == 0 else main + kept
            margin = out_of if z == 0 else margin + out_of
        mains.append(main)
        margins.append(margin)
    scratch[2 * tile :, :] = jnp.zeros((scratch.shape[0] - 2 * tile, N), f32)
    return packed_message(jnp.concatenate(mains, 0), jnp.concatenate(margins, 0), scratch)


def first_kernel(
    angles, shifts_in, spots_in, delta, beta, measured_in,
    slab_delta, slab_beta, shifts, out, slot, scalar_shifts, scalar_spots, scratch, sems,
):
    copies = [
        pltpu.make_async_copy(source, target, sems.at[k])
        for k, (source, target) in enumerate(
            [
                (shifts_in, scalar_shifts),
                (spots_in, scalar_spots),
                (delta, slab_delta),
                (beta, slab_beta),
                (measured_in.at[0], slot.at[0:N]),
            ]
        )
    ]
    for copy in copies:
        copy.start()
    me = lax.axis_index("ang")
    for copy in copies[:2]:
        copy.wait()
    for d in range(angles):
        angle = lax.rem(me + d, angles)
        for z in range(2):
            shifts[2 * d + z : 2 * d + z + 1, :] = jnp.full((1, N), scalar_shifts[z, angle], i32)
    slot[N : N + 8, :] = jnp.full((8, N), scalar_spots[0, 0], i32).astype(f32)
    slot[N + 8 :, :] = jnp.full((8, N), scalar_spots[1, 0], i32).astype(f32)
    following = lax.rem(me + 1, angles)
    for copy in copies[2:]:
        copy.wait()
    out[...] = window_message(lambda z: scalar_shifts[z, following], slab_delta, slab_beta, scratch)


def window_kernel(shifts, slab_delta, slab_beta, _, *refs):
    outs, slot, scratch = refs[:-2], refs[-2], refs[-1]
    slot[N:, :] = slot[N:, :] + 0.0
    for k, out in enumerate(outs):
        d = k + 2
        out[...] = window_message(lambda z: shifts[2 * d + z, 0], slab_delta, slab_beta, scratch)


def load_kernel(
    counts_in, shifts, slab_delta, slab_beta, _, spots_in, probe_in, measured_in,
    own, counts, spots, probe, measured, scratch, sems,
):
    copies = [
        pltpu.make_async_copy(source, target, sems.at[k])
        for k, (source, target) in enumerate([(spots_in, spots), (probe_in, probe), (measured_in, measured)])
    ]
    for copy in copies:
        copy.start()
    own[...] = window_message(lambda z: shifts[z, 0], slab_delta, slab_beta, scratch)
    counts[...] = jnp.full(counts.shape, counts_in[0, 0], i32)
    for copy in copies:
        copy.wait()


def slot_position(slot):
    return slot[N, 0].astype(i32), slot[N + 8, 0].astype(i32)


def block_of(column, blocks):
    first, offset = column // N, lax.rem(column, N)
    return first, jnp.minimum(first + 1, blocks - 1), offset


def is_even():
    return lax.rem(lax.axis_index("rows"), 2) == 0


def unpack_kernel(blocks, steps, *refs):
    received, (proj, margins) = refs[: len(steps)], refs[-2:]
    tile = proj.shape[2]
    me = lax.axis_index("ang")
    for d, ref in zip(steps, received):
        block = lax.rem(me + (blocks - d), blocks)
        message = ref[...].astype(f32)
        proj[0, block] = message[:tile]
        proj[1, block] = message[tile : 2 * tile]
        margins[block] = margins_of(message, 2 * tile)


def assemble_kernel(spots, slot, message, proj_in, margins_in, core, cross, proj, margins):
    blocks, tile = proj.shape[1], proj.shape[2]
    unpack_kernel(blocks, [blocks - 1], message, proj, margins)
    lane = lane_iota(tile)
    for block in range(blocks):
        before, after = (block - 1) % blocks, (block + 1) % blocks
        for c in range(2):
            part = slice(c * tile, (c + 1) * tile)
            extra = jnp.where(lane < SHIFT, margins[before, part], 0.0)
            extra += jnp.where(lane >= N - SHIFT, margins[after, part], 0.0)
            proj[c, block] += extra
    _, previous = slot_position(slot)
    own = spots[1, 0]
    lane = lane_iota(N)
    even = is_even()
    for out, upper in ((core, even), (cross, jnp.logical_not(even))):
        first, second, offset = block_of(jnp.where(upper, own, previous), blocks)
        rows = pl.ds(pl.multiple_of(jnp.where(upper, EDGE_ROWS, 0), 8), N)
        pair = patch_of(proj, lane, offset, first, second, rows)
        out[...] = jnp.concatenate(pair, 0).astype(bf16)


def transmit(phase, absorb):
    turns = jnp.round(phase * (2.0 / math.pi))
    r = phase - turns * 1.5703125
    r = r - turns * 4.837512969970703125e-4
    r = r - turns * 7.54978995489188e-8
    z = r * r
    sine = r + r * z * (-1.6666654611e-1 + z * (8.3321608736e-3 - z * 1.9515295891e-4))
    cosine = 1.0 - 0.5 * z + z * z * (4.166664568298827e-2 + z * (-1.388731625493765e-3 + z * 2.443315711809948e-5))
    quarter = turns.astype(i32)
    odd = (quarter & 1) == 1
    damping = jnp.exp(-absorb)
    out_cos = jnp.where(odd, sine, cosine)
    out_sin = jnp.where(odd, cosine, sine)
    out_cos = jnp.where(((quarter + 1) & 2) == 2, -out_cos, out_cos)
    out_sin = jnp.where((quarter & 2) == 2, -out_sin, out_sin)
    return damping * out_cos, damping * out_sin


def split(value):
    high = value.astype(bf16)
    return high, (value - high.astype(f32)).astype(bf16)


def dot(a, b):
    return jnp.dot(a, b, preferred_element_type=f32)


def times_right(value, high, low):
    vh, vl = split(value)
    return dot(vh, high) + (dot(vl, high) + dot(vh, low))


def times_left(high, low, value):
    vh, vl = split(value)
    return dot(high, vh) + (dot(high, vl) + dot(low, vh))


def scan_gradients(patches, measured, weights, probe, tables):
    probe_re, probe_im = probe[0], probe[1]
    right_high, right_low, left_high, left_low = (tables[t] for t in range(4))
    rows = [
        jnp.concatenate([probe_re * re - probe_im * im, probe_re * im + probe_im * re], 1)
        for re, im in patches
    ]
    half = times_right(jnp.concatenate(rows, 0), right_high, right_low)
    count = len(patches)
    stacked = jnp.concatenate(
        [
            jnp.concatenate([half[j * N : (j + 1) * N, part * N : (part + 1) * N] for j in range(count)], 1)
            for part in range(2)
        ],
        0,
    )
    far = times_left(left_high, left_low, stacked)
    far_re, far_im = far[:N], far[N:]
    squared = far_re * far_re + far_im * far_im
    inverse = lax.rsqrt(jnp.maximum(squared, AMP_FLOOR * AMP_FLOOR))
    amplitude = jnp.concatenate([m for m in measured], 1)
    factor = 1.0 - amplitude * inverse
    factor = jnp.concatenate(
        [factor[:, j * N : (j + 1) * N] * weights[j] for j in range(count)], 1
    )
    residual = jnp.concatenate([far_re * factor, far_im * factor], 0)
    half = times_left(right_high, right_low, residual)
    rows = [
        jnp.concatenate([half[:N, j * N : (j + 1) * N], half[N:, j * N : (j + 1) * N]], 1)
        for j in range(count)
    ]
    back = times_right(jnp.concatenate(rows, 0), left_high, left_low)
    grads = []
    for j in range(count):
        re, im = back[j * N : (j + 1) * N, :N], back[j * N : (j + 1) * N, N:]
        grads.append((probe_re * re + probe_im * im, probe_re * im - probe_im * re))
    return grads


def patch_of(values, lane, offset, first, second, rows):
    pair = []
    for c in range(2):
        left = roll_left(values[c, first, rows, :], offset)
        right = roll_left(values[c, second, rows, :], offset)
        pair.append(jnp.where(lane < N - offset, left, right))
    return pair


def chain_back(patch, grad):
    (tr, ti), (gr, gi) = patch, grad
    return tr * gi - ti * gr, -(tr * gr + ti * gi)


def add_patch(total, c, rows, value, lane, offset, first, second):
    placed = roll_lanes(value, offset)
    total[c, first, rows, :] += jnp.where(lane >= offset, placed, 0.0)
    total[c, second, rows, :] += jnp.where(lane < offset, placed, 0.0)


def edge_patch(is_own, spots, slot, halo, trans, patch):
    blocks, tile = trans.shape[1], trans.shape[2]
    prev_row, prev_column = slot_position(slot)
    columns = block_of(jnp.where(is_own, spots[1, 0], prev_column), blocks)
    start = jnp.where(is_own, spots[0, 0], jnp.maximum(prev_row, EDGE_ROWS))
    first, second, offset = columns
    here = pl.ds(pl.multiple_of(jnp.where(is_own, 0, tile), 8), tile)
    there = pl.ds(pl.multiple_of(jnp.where(is_own, tile, EDGE_ROWS), 8), N)
    last = lax.axis_index("rows") == lax.axis_size("rows") - 1
    value = jnp.where(is_own & last, 0.0, halo[...].astype(f32))
    outside = transmit(value[:N], value[N:])
    inside = patch_of(trans, lane_iota(tile), offset, first, second, slice(None))
    for c in range(2):
        patch[c, here, :] = inside[c]
        patch[c, there, :] = outside[c]
    pair = [patch[c, pl.ds(start, N), :] for c in range(2)]
    return pair, columns, jnp.where(is_own, start, start - tile)


def edge_weight(is_own, counts, slot):
    prev_row, _ = slot_position(slot)
    reaches = (prev_row > EDGE_ROWS) & (lax.axis_index("rows") > 0)
    return jnp.where(jnp.where(is_own, counts[0, 0] > 0, reaches), 1.0, 0.0).astype(f32)


def add_edge(total, chained, columns, place, frame):
    tile = total.shape[2]
    first, second, offset = columns
    for c in range(2):
        frame[c, 0:tile, :] = jnp.zeros((tile, N), f32)
        frame[c, tile : tile + N, :] = chained[c]
        frame[c, tile + N :, :] = jnp.zeros((tile, N), f32)
        rows = frame[c, pl.ds(tile - place, tile), :]
        add_patch(total, c, slice(None), rows, lane_iota(tile), offset, first, second)


def inner_kernel(spots, counts, proj, slot0, core, probe, measured, tables, trans, grad, patch, frame, edge_frame):
    blocks, tile = proj.shape[1], proj.shape[2]
    for block in range(blocks):
        re, im = transmit(proj[0, block], proj[1, block])
        trans[0, block] = re
        trans[1, block] = im
    grad[...] = jnp.zeros(grad.shape, f32)
    frame[0:SHIFT, :] = jnp.zeros((SHIFT, N), f32)
    frame[SHIFT + N :, :] = jnp.zeros((SHIFT, N), f32)
    slots = measured.shape[0]
    lane = lane_iota(N)
    is_own = is_even()
    pair, columns, place = edge_patch(is_own, spots, slot0, core, trans, patch)
    patches, weights = [pair], [edge_weight(is_own, counts, slot0)]
    patterns = [jnp.where(is_own, measured[0], slot0[0:N, :])]
    for slot in range(1, slots):
        row = jnp.minimum(spots[0, slot], EDGE_ROWS)
        first, second, offset = block_of(spots[1, slot], blocks)
        patches.append(patch_of(trans, lane, offset, first, second, pl.ds(row, N)))
        weights.append(jnp.where(slot < counts[0, 0], 1.0, 0.0).astype(f32))
        patterns.append(measured[slot])
    grads = scan_gradients(patches, patterns, weights, probe, tables)
    add_edge(grad, chain_back(patches[0], grads[0]), columns, place, edge_frame)
    lane = lane_iota(tile)
    for slot in range(1, slots):
        row = jnp.minimum(spots[0, slot], EDGE_ROWS)
        first, second, offset = block_of(spots[1, slot], blocks)
        chained = chain_back(patches[slot], grads[slot])
        for c in range(2):
            frame[SHIFT : SHIFT + N, :] = chained[c]
            add_patch(grad, c, slice(None), frame[pl.ds(SHIFT - row, tile), :], lane, offset, first, second)


def gradient_message(block, total, scratch):
    blocks, tile = total.shape[1], total.shape[2]
    scratch[2 * tile :, :] = jnp.zeros((scratch.shape[0] - 2 * tile, N), f32)
    lane = lane_iota(tile)
    before, after = lax.rem(block + (blocks - 1), blocks), lax.rem(block + 1, blocks)
    mains, margins = [], []
    for c in range(2):
        mains.append(total[c, block])
        margin = jnp.where(lane < SHIFT, total[c, after], 0.0)
        margins.append(jnp.where(lane >= N - SHIFT, total[c, before], margin))
    return packed_message(jnp.concatenate(mains, 0), jnp.concatenate(margins, 0), scratch)


def edge_kernel(spots, counts, slot0, cross, trans, _, probe, measured, tables, *refs):
    outs, (total, patch, frame, scratch) = refs[:-4], refs[-4:]
    blocks = trans.shape[1]
    is_own = jnp.logical_not(is_even())
    pair, columns, place = edge_patch(is_own, spots, slot0, cross, trans, patch)
    pattern = jnp.where(is_own, measured[0], slot0[0:N, :])
    weight = edge_weight(is_own, counts, slot0)
    grads = scan_gradients([pair], [pattern], [weight], probe, tables)
    add_edge(total, chain_back(pair, grads[0]), columns, place, frame)
    me = lax.axis_index("ang")
    for k, out in enumerate(outs):
        out[...] = gradient_message(lax.rem(me + k + 1, blocks), total, scratch)


def own_kernel(total, _, out, scratch):
    out[...] = gradient_message(lax.axis_index("ang"), total, scratch)


def slab_kernel(angles, steps, last, shifts, *refs):
    refs, outs = (refs[:-2], refs[-2:]) if last else (refs[:-1], refs[-1:])
    received, before = refs[: len(steps)], refs[len(steps) :]
    tile = (received[0].shape[0] - PACK_ROWS) // 2
    lane = lane_iota(tile)
    sums = [[before[0][c, z] if before else None for z in range(2)] for c in range(2)]
    for d, ref in zip(steps, received):
        message = ref[...].astype(f32)
        margins = margins_of(message, 2 * tile)
        for z in range(2):
            s = shifts[2 * ((angles - d) % angles) + z, 0]
            target = lane + s
            inside = (target >= 0) & (target < N)
            for c in range(2):
                part = slice(c * tile, (c + 1) * tile)
                value = jnp.where(inside, message[part], margins[part])
                value = pltpu.roll(value, lax.rem(s + N, N), 1)
                sums[c][z] = value if sums[c][z] is None else sums[c][z] + value
    for c in range(2):
        for z in range(2):
            if last:
                outs[c][pl.ds(z, tile, stride=2), :] = sums[c][z]
            else:
                outs[0][c, z] = sums[c][z]


def call(kernel, ins, outs, scratch=(), flops=0, bytes_accessed=0, aliases=()):
    scratch = [pltpu.VMEM(item, f32) if isinstance(item, tuple) else item for item in scratch]
    return pl.pallas_call(
        kernel,
        in_specs=ins,
        out_specs=[VMEM] * len(outs),
        out_shape=[jax.ShapeDtypeStruct(shape, dtype) for shape, dtype in outs],
        scratch_shapes=scratch,
        input_output_aliases=dict(aliases),
        compiler_params=pltpu.CompilerParams(vmem_limit_bytes=32 * 1024 * 1024),
        cost_estimate=pl.CostEstimate(flops=flops, bytes_accessed=bytes_accessed, transcendentals=0),
    )


def exchange(messages):
    count = lax.axis_size("ang")
    received = [messages[0]]
    for d in range(1, count):
        received.append(lax.ppermute(messages[d], "ang", [(i, (i + d) % count) for i in range(count)]))
    return received


def on_rows(value, target):
    count = lax.axis_size("rows")
    return lax.ppermute(value, "rows", [(i, target(i) % count) for i in range(count)])


def on_device(delta_obj, beta_obj, layer_shifts, illumination_field, amplitudes, positions, scan_counts):
    tile = delta_obj.shape[0]
    angles = lax.axis_size("ang")
    message = ((2 * tile + PACK_ROWS, N), bf16)
    padded = (len(groups_of(2 * tile)) * PACK_ROWS, N)
    field = ((2, angles, tile, N), f32)
    slab = (2 * tile, N)
    halo = ((2 * N, N), bf16)
    tables = jnp.asarray(fourier_tables())

    in_hbm = functools.partial(pltpu.with_memory_space_constraint, memory_space=pltpu.HBM)
    shifts, spots, probe, measured = (
        in_hbm(value) for value in (layer_shifts.T, positions[0].T, illumination_field, amplitudes[0])
    )
    slab_delta, slab_beta, shifts, following, slot = call(
        functools.partial(first_kernel, angles),
        [HBM] * 5,
        [(slab, f32), (slab, f32), ((2 * angles, N), i32), message, ((N + 16, N), f32)],
        [pltpu.SMEM(shifts.shape, i32), pltpu.SMEM(spots.shape, i32), padded, pltpu.SemaphoreType.DMA((5,))],
    )(shifts, spots, in_hbm(delta_obj.reshape(slab)), in_hbm(beta_obj.reshape(slab)), measured)
    *others, slot = call(
        window_kernel, [VMEM] * 4, [message] * (angles - 2) + [((N + 16, N), f32)], [padded], aliases={3: angles - 2}
    )(shifts, slab_delta, slab_beta, slot)
    own, counts, spots, probe, measured = call(
        load_kernel,
        [SMEM] + [VMEM] * 4 + [HBM] * 3,
        [message, ((8, N), i32)] + [(value.shape, value.dtype) for value in (spots, probe, measured)],
        [padded, pltpu.SemaphoreType.DMA((3,))],
        flops=10**9,
        bytes_accessed=10**6,
    )(scan_counts, shifts, slab_delta, slab_beta, others[-1], spots, probe, measured)
    windows = [own, following, *others]
    received = exchange(windows)
    previous = on_rows(slot, lambda i: i + 1)
    rows = ((angles, 2 * tile, N), f32)
    early = list(range(angles - 1))
    partly = call(
        functools.partial(unpack_kernel, angles, early),
        [VMEM] * (angles - 1),
        [field, rows],
        flops=10**9,
        bytes_accessed=10**6,
    )(*received[:-1])
    core, cross, proj, _ = call(
        assemble_kernel, [VMEM] * 5, [halo, halo, field, rows], aliases={3: 2, 4: 3}
    )(spots, previous, received[-1], *partly)
    core = on_rows(core, lambda i: i ^ 1)
    cross = on_rows(cross, lambda i: i + 1 if i % 2 else i - 1)
    patch, frame = (2, 2 * tile, N), (2, 2 * tile + N, N)
    trans, inner = call(
        inner_kernel,
        [VMEM] * 8,
        [field, field],
        [patch, (N + 2 * SHIFT, N), frame],
        flops=3 * 10**9,
        bytes_accessed=3 * 10**6,
    )(spots, counts, proj, previous, core, probe, measured, tables)
    *outgoing, total = call(
        edge_kernel,
        [VMEM] * 9,
        [message] * (angles - 1) + [field],
        [patch, frame, padded],
        aliases={5: angles - 1},
    )(spots, counts, previous, cross, trans, inner, probe, measured, tables)
    own = call(own_kernel, [VMEM] * 2, [message], [padded])(total, outgoing[-1])[0]
    received = exchange([own, *outgoing])
    early = list(range(angles - 1))
    sums = call(
        functools.partial(slab_kernel, angles, early, False),
        [VMEM] * angles,
        [((2, 2, tile, N), f32)],
        flops=10**9,
        bytes_accessed=10**6,
    )(shifts, *received[:-1])[0]
    grad_delta, grad_beta = call(
        functools.partial(slab_kernel, angles, [angles - 1], True), [VMEM] * 3, [(slab, f32)] * 2
    )(shifts, received[-1], sums)
    return grad_delta.reshape(tile, 2, N), grad_beta.reshape(tile, 2, N)


def solution(mesh):
    placed = (
        P("rows", None, "ang"),
        P("rows", None, "ang"),
        P(),
        P(),
        P("ang", "rows", None, None),
        P("ang", "rows", None),
        P("ang", "rows"),
    )
    return jax.shard_map(
        on_device,
        mesh=mesh,
        in_specs=placed,
        out_specs=(P("rows", None, "ang"), P("rows", None, "ang")),
        check_vma=False,
    )
```

```python
import functools
import math

import jax
import jax.numpy as jnp
import ml_dtypes
import numpy as np
from jax import lax
from jax.experimental import pallas as pl
from jax.experimental.pallas import tpu as pltpu
from jax.sharding import PartitionSpec as P

N = 128
SHIFT = 8
AMP_FLOOR = 0.1
PACK_ROWS = 40
EDGE_ROWS = 8

f32, bf16, i32 = jnp.float32, jnp.bfloat16, jnp.int32
VMEM = pl.BlockSpec(memory_space=pltpu.VMEM)
SMEM = pl.BlockSpec(memory_space=pltpu.SMEM)
HBM = pl.BlockSpec(memory_space=pltpu.HBM)


def fourier_tables():
    counter = np.arange(N)
    angle = (counter[:, None] * counter[None, :] % N) * (2.0 * math.pi / N)
    re, im = np.cos(angle) / math.sqrt(N), -np.sin(angle) / math.sqrt(N)
    right = np.block([[re, im], [-im, re]])
    tables = []
    for table in (right, right.T):
        high = table.astype(ml_dtypes.bfloat16)
        tables += [high, (table - high.astype(np.float64)).astype(ml_dtypes.bfloat16)]
    return np.stack(tables)


def lane_iota(rows):
    return lax.broadcasted_iota(i32, (rows, N), 1)


def roll_lanes(value, by):
    return pltpu.roll(value, by, 1)


def roll_left(value, by):
    return pltpu.roll(value, lax.rem(N - by, N), 1)


def groups_of(rows):
    return [(g, start, min(PACK_ROWS, rows - start)) for g, start in enumerate(range(0, rows, PACK_ROWS))]


def packed_message(main, margins, scratch):
    rows = main.shape[0]
    scratch[0:rows, :] = margins
    packed = None
    for g, start, _ in groups_of(rows):
        part = scratch[start : start + PACK_ROWS, :]
        part = roll_lanes(part, 16 * g) if g else part
        packed = part if packed is None else packed + part
    return jnp.concatenate([main, packed], 0).astype(bf16)


def margins_of(message, rows):
    packed = message[rows:, :]
    parts = []
    for g, _, size in groups_of(rows):
        part = roll_lanes(packed, N - 16 * g) if g else packed
        parts.append(part[:size])
    return jnp.concatenate(parts, 0)


def window_message(shift_of, slab_delta, slab_beta, scratch):
    tile = slab_delta.shape[0] // 2
    lane = lane_iota(tile)
    mains, margins = [], []
    for ref in (slab_delta, slab_beta):
        main = margin = None
        for z in range(2):
            s = shift_of(z)
            rolled = pltpu.roll(ref[pl.ds(z, tile, stride=2), :], lax.rem(N - s, N), 1)
            source = lane + s
            inside = (source >= 0) & (source < N)
            kept, out_of = jnp.where(inside, rolled, 0.0), jnp.where(inside, 0.0, rolled)
            main = kept if z == 0 else main + kept
            margin = out_of if z == 0 else margin + out_of
        mains.append(main)
        margins.append(margin)
    scratch[2 * tile :, :] = jnp.zeros((scratch.shape[0] - 2 * tile, N), f32)
    return packed_message(jnp.concatenate(mains, 0), jnp.concatenate(margins, 0), scratch)


def first_kernel(
    angles, shifts_in, spots_in, delta, beta, measured_in,
    slab_delta, slab_beta, shifts, out, slot, scalar_shifts, scalar_spots, scratch, sems,
):
    copies = [
        pltpu.make_async_copy(source, target, sems.at[k])
        for k, (source, target) in enumerate(
            [
                (shifts_in, scalar_shifts),
                (spots_in, scalar_spots),
                (delta, slab_delta),
                (beta, slab_beta),
                (measured_in.at[0], slot.at[0:N]),
            ]
        )
    ]
    for copy in copies:
        copy.start()
    me = lax.axis_index("ang")
    for copy in copies[:2]:
        copy.wait()
    for d in range(angles):
        angle = lax.rem(me + d, angles)
        for z in range(2):
            shifts[2 * d + z : 2 * d + z + 1, :] = jnp.full((1, N), scalar_shifts[z, angle], i32)
    slot[N : N + 8, :] = jnp.full((8, N), scalar_spots[0, 0], i32).astype(f32)
    slot[N + 8 :, :] = jnp.full((8, N), scalar_spots[1, 0], i32).astype(f32)
    following = lax.rem(me + 1, angles)
    for copy in copies[2:]:
        copy.wait()
    out[...] = window_message(lambda z: scalar_shifts[z, following], slab_delta, slab_beta, scratch)


def window_kernel(shifts, slab_delta, slab_beta, _, *refs):
    outs, slot, scratch = refs[:-2], refs[-2], refs[-1]
    slot[N:, :] = slot[N:, :] + 0.0
    for k, out in enumerate(outs):
        d = k + 2
        out[...] = window_message(lambda z: shifts[2 * d + z, 0], slab_delta, slab_beta, scratch)


def load_kernel(
    counts_in, shifts, slab_delta, slab_beta, _, spots_in, probe_in, measured_in,
    own, counts, spots, probe, measured, scratch, sems,
):
    copies = [
        pltpu.make_async_copy(source, target, sems.at[k])
        for k, (source, target) in enumerate([(spots_in, spots), (probe_in, probe), (measured_in, measured)])
    ]
    for copy in copies:
        copy.start()
    own[...] = window_message(lambda z: shifts[z, 0], slab_delta, slab_beta, scratch)
    counts[...] = jnp.full(counts.shape, counts_in[0, 0], i32)
    for copy in copies:
        copy.wait()


def slot_position(slot):
    return slot[N, 0].astype(i32), slot[N + 8, 0].astype(i32)


def block_of(column, blocks):
    first, offset = column // N, lax.rem(column, N)
    return first, jnp.minimum(first + 1, blocks - 1), offset


def is_even():
    return lax.rem(lax.axis_index("rows"), 2) == 0


def unpack_kernel(blocks, steps, *refs):
    received, (proj, margins) = refs[: len(steps)], refs[-2:]
    tile = proj.shape[2]
    me = lax.axis_index("ang")
    for d, ref in zip(steps, received):
        block = lax.rem(me + (blocks - d), blocks)
        message = ref[...].astype(f32)
        proj[0, block] = message[:tile]
        proj[1, block] = message[tile : 2 * tile]
        margins[block] = margins_of(message, 2 * tile)


def assemble_kernel(spots, slot, message, proj_in, margins_in, core, cross, proj, margins):
    blocks, tile = proj.shape[1], proj.shape[2]
    unpack_kernel(blocks, [blocks - 1], message, proj, margins)
    lane = lane_iota(tile)
    for block in range(blocks):
        before, after = (block - 1) % blocks, (block + 1) % blocks
        for c in range(2):
            part = slice(c * tile, (c + 1) * tile)
            extra = jnp.where(lane < SHIFT, margins[before, part], 0.0)
            extra += jnp.where(lane >= N - SHIFT, margins[after, part], 0.0)
            proj[c, block] += extra
    _, previous = slot_position(slot)
    own = spots[1, 0]
    lane = lane_iota(N)
    even = is_even()
    for out, upper in ((core, even), (cross, jnp.logical_not(even))):
        first, second, offset = block_of(jnp.where(upper, own, previous), blocks)
        rows = pl.ds(pl.multiple_of(jnp.where(upper, EDGE_ROWS, 0), 8), N)
        pair = patch_of(proj, lane, offset, first, second, rows)
        out[...] = jnp.concatenate(pair, 0).astype(bf16)


def transmit(phase, absorb):
    turns = jnp.round(phase * (2.0 / math.pi))
    r = phase - turns * 1.5703125
    r = r - turns * 4.837512969970703125e-4
    r = r - turns * 7.54978995489188e-8
    z = r * r
    sine = r + r * z * (-1.6666654611e-1 + z * (8.3321608736e-3 - z * 1.9515295891e-4))
    cosine = 1.0 - 0.5 * z + z * z * (4.166664568298827e-2 + z * (-1.388731625493765e-3 + z * 2.443315711809948e-5))
    quarter = turns.astype(i32)
    odd = (quarter & 1) == 1
    damping = jnp.exp(-absorb)
    out_cos = jnp.where(odd, sine, cosine)
    out_sin = jnp.where(odd, cosine, sine)
    out_cos = jnp.where(((quarter + 1) & 2) == 2, -out_cos, out_cos)
    out_sin = jnp.where((quarter & 2) == 2, -out_sin, out_sin)
    return damping * out_cos, damping * out_sin


def split(value):
    high = value.astype(bf16)
    return high, (value - high.astype(f32)).astype(bf16)


def dot(a, b):
    return jnp.dot(a, b, preferred_element_type=f32)


def times_right(value, high, low):
    vh, vl = split(value)
    return dot(vh, high) + (dot(vl, high) + dot(vh, low))


def times_left(high, low, value):
    vh, vl = split(value)
    return dot(high, vh) + (dot(high, vl) + dot(low, vh))


def scan_gradients(patches, measured, weights, probe, tables):
    probe_re, probe_im = probe[0], probe[1]
    right_high, right_low, left_high, left_low = (tables[t] for t in range(4))
    rows = [
        jnp.concatenate([probe_re * re - probe_im * im, probe_re * im + probe_im * re], 1)
        for re, im in patches
    ]
    half = times_right(jnp.concatenate(rows, 0), right_high, right_low)
    count = len(patches)
    stacked = jnp.concatenate(
        [
            jnp.concatenate([half[j * N : (j + 1) * N, part * N : (part + 1) * N] for j in range(count)], 1)
            for part in range(2)
        ],
        0,
    )
    far = times_left(left_high, left_low, stacked)
    far_re, far_im = far[:N], far[N:]
    squared = far_re * far_re + far_im * far_im
    inverse = lax.rsqrt(jnp.maximum(squared, AMP_FLOOR * AMP_FLOOR))
    amplitude = jnp.concatenate([m for m in measured], 1)
    factor = 1.0 - amplitude * inverse
    factor = jnp.concatenate(
        [factor[:, j * N : (j + 1) * N] * weights[j] for j in range(count)], 1
    )
    residual = jnp.concatenate([far_re * factor, far_im * factor], 0)
    half = times_left(right_high, right_low, residual)
    rows = [
        jnp.concatenate([half[:N, j * N : (j + 1) * N], half[N:, j * N : (j + 1) * N]], 1)
        for j in range(count)
    ]
    back = times_right(jnp.concatenate(rows, 0), left_high, left_low)
    grads = []
    for j in range(count):
        re, im = back[j * N : (j + 1) * N, :N], back[j * N : (j + 1) * N, N:]
        grads.append((probe_re * re + probe_im * im, probe_re * im - probe_im * re))
    return grads


def patch_of(values, lane, offset, first, second, rows):
    pair = []
    for c in range(2):
        left = roll_left(values[c, first, rows, :], offset)
        right = roll_left(values[c, second, rows, :], offset)
        pair.append(jnp.where(lane < N - offset, left, right))
    return pair


def chain_back(patch, grad):
    (tr, ti), (gr, gi) = patch, grad
    return tr * gi - ti * gr, -(tr * gr + ti * gi)


def add_patch(total, c, rows, value, lane, offset, first, second):
    placed = roll_lanes(value, offset)
    total[c, first, rows, :] += jnp.where(lane >= offset, placed, 0.0)
    total[c, second, rows, :] += jnp.where(lane < offset, placed, 0.0)


def edge_patch(is_own, spots, slot, halo, trans, patch):
    blocks, tile = trans.shape[1], trans.shape[2]
    prev_row, prev_column = slot_position(slot)
    columns = block_of(jnp.where(is_own, spots[1, 0], prev_column), blocks)
    start = jnp.where(is_own, spots[0, 0], jnp.maximum(prev_row, EDGE_ROWS))
    first, second, offset = columns
    here = pl.ds(pl.multiple_of(jnp.where(is_own, 0, tile), 8), tile)
    there = pl.ds(pl.multiple_of(jnp.where(is_own, tile, EDGE_ROWS), 8), N)
    last = lax.axis_index("rows") == lax.axis_size("rows") - 1
    value = jnp.where(is_own & last, 0.0, halo[...].astype(f32))
    outside = transmit(value[:N], value[N:])
    inside = patch_of(trans, lane_iota(tile), offset, first, second, slice(None))
    for c in range(2):
        patch[c, here, :] = inside[c]
        patch[c, there, :] = outside[c]
    pair = [patch[c, pl.ds(start, N), :] for c in range(2)]
    return pair, columns, jnp.where(is_own, start, start - tile)


def edge_weight(is_own, counts, slot):
    prev_row, _ = slot_position(slot)
    reaches = (prev_row > EDGE_ROWS) & (lax.axis_index("rows") > 0)
    return jnp.where(jnp.where(is_own, counts[0, 0] > 0, reaches), 1.0, 0.0).astype(f32)


def add_edge(total, chained, columns, place, frame):
    tile = total.shape[2]
    first, second, offset = columns
    for c in range(2):
        frame[c, 0:tile, :] = jnp.zeros((tile, N), f32)
        frame[c, tile : tile + N, :] = chained[c]
        frame[c, tile + N :, :] = jnp.zeros((tile, N), f32)
        rows = frame[c, pl.ds(tile - place, tile), :]
        add_patch(total, c, slice(None), rows, lane_iota(tile), offset, first, second)


def inner_kernel(spots, counts, proj, slot0, core, probe, measured, tables, trans, grad, patch, frame, edge_frame):
    blocks, tile = proj.shape[1], proj.shape[2]
    for block in range(blocks):
        re, im = transmit(proj[0, block], proj[1, block])
        trans[0, block] = re
        trans[1, block] = im
    grad[...] = jnp.zeros(grad.shape, f32)
    frame[0:SHIFT, :] = jnp.zeros((SHIFT, N), f32)
    frame[SHIFT + N :, :] = jnp.zeros((SHIFT, N), f32)
    slots = measured.shape[0]
    lane = lane_iota(N)
    is_own = is_even()
    pair, columns, place = edge_patch(is_own, spots, slot0, core, trans, patch)
    patches, weights = [pair], [edge_weight(is_own, counts, slot0)]
    patterns = [jnp.where(is_own, measured[0], slot0[0:N, :])]
    for slot in range(1, slots):
        row = jnp.minimum(spots[0, slot], EDGE_ROWS)
        first, second, offset = block_of(spots[1, slot], blocks)
        patches.append(patch_of(trans, lane, offset, first, second, pl.ds(row, N)))
        weights.append(jnp.where(slot < counts[0, 0], 1.0, 0.0).astype(f32))
        patterns.append(measured[slot])
    grads = scan_gradients(patches, patterns, weights, probe, tables)
    add_edge(grad, chain_back(patches[0], grads[0]), columns, place, edge_frame)
    lane = lane_iota(tile)
    for slot in range(1, slots):
        row = jnp.minimum(spots[0, slot], EDGE_ROWS)
        first, second, offset = block_of(spots[1, slot], blocks)
        chained = chain_back(patches[slot], grads[slot])
        for c in range(2):
            frame[SHIFT : SHIFT + N, :] = chained[c]
            add_patch(grad, c, slice(None), frame[pl.ds(SHIFT - row, tile), :], lane, offset, first, second)


def gradient_message(block, total, scratch):
    blocks, tile = total.shape[1], total.shape[2]
    scratch[2 * tile :, :] = jnp.zeros((scratch.shape[0] - 2 * tile, N), f32)
    lane = lane_iota(tile)
    before, after = lax.rem(block + (blocks - 1), blocks), lax.rem(block + 1, blocks)
    mains, margins = [], []
    for c in range(2):
        mains.append(total[c, block])
        margin = jnp.where(lane < SHIFT, total[c, after], 0.0)
        margins.append(jnp.where(lane >= N - SHIFT, total[c, before], margin))
    return packed_message(jnp.concatenate(mains, 0), jnp.concatenate(margins, 0), scratch)


def edge_kernel(spots, counts, slot0, cross, trans, _, probe, measured, tables, *refs):
    outs, (total, patch, frame, scratch) = refs[:-4], refs[-4:]
    blocks = trans.shape[1]
    is_own = jnp.logical_not(is_even())
    pair, columns, place = edge_patch(is_own, spots, slot0, cross, trans, patch)
    pattern = jnp.where(is_own, measured[0], slot0[0:N, :])
    weight = edge_weight(is_own, counts, slot0)
    grads = scan_gradients([pair], [pattern], [weight], probe, tables)
    add_edge(total, chain_back(pair, grads[0]), columns, place, frame)
    me = lax.axis_index("ang")
    for k, out in enumerate(outs):
        out[...] = gradient_message(lax.rem(me + k + 1, blocks), total, scratch)


def own_kernel(total, _, out, scratch):
    out[...] = gradient_message(lax.axis_index("ang"), total, scratch)


def slab_kernel(angles, steps, last, shifts, *refs):
    refs, outs = (refs[:-2], refs[-2:]) if last else (refs[:-1], refs[-1:])
    received, before = refs[: len(steps)], refs[len(steps) :]
    tile = (received[0].shape[0] - PACK_ROWS) // 2
    lane = lane_iota(tile)
    sums = [[before[0][c, z] if before else None for z in range(2)] for c in range(2)]
    for d, ref in zip(steps, received):
        message = ref[...].astype(f32)
        margins = margins_of(message, 2 * tile)
        for z in range(2):
            s = shifts[2 * ((angles - d) % angles) + z, 0]
            target = lane + s
            inside = (target >= 0) & (target < N)
            for c in range(2):
                part = slice(c * tile, (c + 1) * tile)
                value = jnp.where(inside, message[part], margins[part])
                value = pltpu.roll(value, lax.rem(s + N, N), 1)
                sums[c][z] = value if sums[c][z] is None else sums[c][z] + value
    for c in range(2):
        for z in range(2):
            if last:
                outs[c][pl.ds(z, tile, stride=2), :] = sums[c][z]
            else:
                outs[0][c, z] = sums[c][z]


def call(kernel, ins, outs, scratch=(), flops=0, bytes_accessed=0, aliases=()):
    scratch = [pltpu.VMEM(item, f32) if isinstance(item, tuple) else item for item in scratch]
    return pl.pallas_call(
        kernel,
        in_specs=ins,
        out_specs=[VMEM] * len(outs),
        out_shape=[jax.ShapeDtypeStruct(shape, dtype) for shape, dtype in outs],
        scratch_shapes=scratch,
        input_output_aliases=dict(aliases),
        compiler_params=pltpu.CompilerParams(vmem_limit_bytes=32 * 1024 * 1024),
        cost_estimate=pl.CostEstimate(flops=flops, bytes_accessed=bytes_accessed, transcendentals=0),
    )


def exchange(messages):
    count = lax.axis_size("ang")
    received = [messages[0]]
    for d in range(1, count):
        received.append(lax.ppermute(messages[d], "ang", [(i, (i + d) % count) for i in range(count)]))
    return received


def on_rows(value, target):
    count = lax.axis_size("rows")
    return lax.ppermute(value, "rows", [(i, target(i) % count) for i in range(count)])


def across_chips(value):
    rows, angles = lax.axis_size("rows"), lax.axis_size("ang")
    pairs = []
    for i in range(rows):
        for a in range(angles):
            if i not in (0, rows - 1):
                target = (i + 1 if i % 2 else i - 1, a)
            elif angles % 2:
                target = (rows - 1 - i, a)
            else:
                target = (i, a ^ 1)
            pairs.append((i * angles + a, target[0] * angles + target[1]))
    return lax.ppermute(value, ("rows", "ang"), pairs)


def on_device(delta_obj, beta_obj, layer_shifts, illumination_field, amplitudes, positions, scan_counts):
    tile = delta_obj.shape[0]
    angles = lax.axis_size("ang")
    message = ((2 * tile + PACK_ROWS, N), bf16)
    padded = (len(groups_of(2 * tile)) * PACK_ROWS, N)
    field = ((2, angles, tile, N), f32)
    slab = (2 * tile, N)
    halo = ((2 * N, N), bf16)
    tables = jnp.asarray(fourier_tables())

    in_hbm = functools.partial(pltpu.with_memory_space_constraint, memory_space=pltpu.HBM)
    shifts, spots, probe, measured = (
        in_hbm(value) for value in (layer_shifts.T, positions[0].T, illumination_field, amplitudes[0])
    )
    slab_delta, slab_beta, shifts, following, slot = call(
        functools.partial(first_kernel, angles),
        [HBM] * 5,
        [(slab, f32), (slab, f32), ((2 * angles, N), i32), message, ((N + 16, N), f32)],
        [pltpu.SMEM(shifts.shape, i32), pltpu.SMEM(spots.shape, i32), padded, pltpu.SemaphoreType.DMA((5,))],
    )(shifts, spots, in_hbm(delta_obj.reshape(slab)), in_hbm(beta_obj.reshape(slab)), measured)
    *others, slot = call(
        window_kernel, [VMEM] * 4, [message] * (angles - 2) + [((N + 16, N), f32)], [padded], aliases={3: angles - 2}
    )(shifts, slab_delta, slab_beta, slot)
    own, counts, spots, probe, measured = call(
        load_kernel,
        [SMEM] + [VMEM] * 4 + [HBM] * 3,
        [message, ((8, N), i32)] + [(value.shape, value.dtype) for value in (spots, probe, measured)],
        [padded, pltpu.SemaphoreType.DMA((3,))],
        flops=10**9,
        bytes_accessed=10**6,
    )(scan_counts, shifts, slab_delta, slab_beta, others[-1], spots, probe, measured)
    windows = [own, following, *others]
    received = exchange(windows)
    previous = on_rows(slot, lambda i: i + 1)
    rows = ((angles, 2 * tile, N), f32)
    early = list(range(angles - 1))
    partly = call(
        functools.partial(unpack_kernel, angles, early),
        [VMEM] * (angles - 1),
        [field, rows],
        flops=10**9,
        bytes_accessed=10**6,
    )(*received[:-1])
    core, cross, proj, _ = call(
        assemble_kernel, [VMEM] * 5, [halo, halo, field, rows], aliases={3: 2, 4: 3}
    )(spots, previous, received[-1], *partly)
    core = on_rows(core, lambda i: i ^ 1)
    cross = across_chips(cross)
    patch, frame = (2, 2 * tile, N), (2, 2 * tile + N, N)
    trans, inner = call(
        inner_kernel,
        [VMEM] * 8,
        [field, field],
        [patch, (N + 2 * SHIFT, N), frame],
        flops=3 * 10**9,
        bytes_accessed=3 * 10**6,
    )(spots, counts, proj, previous, core, probe, measured, tables)
    *outgoing, total = call(
        edge_kernel,
        [VMEM] * 9,
        [message] * (angles - 1) + [field],
        [patch, frame, padded],
        aliases={5: angles - 1},
    )(spots, counts, previous, cross, trans, inner, probe, measured, tables)
    own = call(own_kernel, [VMEM] * 2, [message], [padded])(total, outgoing[-1])[0]
    received = exchange([own, *outgoing])
    early = list(range(angles - 1))
    sums = call(
        functools.partial(slab_kernel, angles, early, False),
        [VMEM] * angles,
        [((2, 2, tile, N), f32)],
        flops=10**9,
        bytes_accessed=10**6,
    )(shifts, *received[:-1])[0]
    grad_delta, grad_beta = call(
        functools.partial(slab_kernel, angles, [angles - 1], True), [VMEM] * 3, [(slab, f32)] * 2
    )(shifts, received[-1], sums)
    return grad_delta.reshape(tile, 2, N), grad_beta.reshape(tile, 2, N)


def solution(mesh):
    placed = (
        P("rows", None, "ang"),
        P("rows", None, "ang"),
        P(),
        P(),
        P("ang", "rows", None, None),
        P("ang", "rows", None),
        P("ang", "rows"),
    )
    return jax.shard_map(
        on_device,
        mesh=mesh,
        in_specs=placed,
        out_specs=(P("rows", None, "ang"), P("rows", None, "ang")),
        check_vma=False,
    )
```

```python
import functools
import math

import jax
import jax.numpy as jnp
import ml_dtypes
import numpy as np
from jax import lax
from jax.experimental import pallas as pl
from jax.experimental.pallas import tpu as pltpu
from jax.sharding import PartitionSpec as P

N = 128
SHIFT = 8
AMP_FLOOR = 0.1
PACK_ROWS = 40
EDGE_ROWS = 8

f32, bf16, i32 = jnp.float32, jnp.bfloat16, jnp.int32
VMEM = pl.BlockSpec(memory_space=pltpu.VMEM)
SMEM = pl.BlockSpec(memory_space=pltpu.SMEM)
HBM = pl.BlockSpec(memory_space=pltpu.HBM)


def fourier_tables():
    counter = np.arange(N)
    angle = (counter[:, None] * counter[None, :] % N) * (2.0 * math.pi / N)
    re, im = np.cos(angle) / math.sqrt(N), -np.sin(angle) / math.sqrt(N)
    right = np.block([[re, im], [-im, re]])
    tables = []
    for table in (right, right.T):
        high = table.astype(ml_dtypes.bfloat16)
        tables += [high, (table - high.astype(np.float64)).astype(ml_dtypes.bfloat16)]
    return np.stack(tables)


def lane_iota(rows):
    return lax.broadcasted_iota(i32, (rows, N), 1)


def roll_lanes(value, by):
    return pltpu.roll(value, by, 1)


def roll_left(value, by):
    return pltpu.roll(value, lax.rem(N - by, N), 1)


def groups_of(rows):
    return [(g, start, min(PACK_ROWS, rows - start)) for g, start in enumerate(range(0, rows, PACK_ROWS))]


def packed_message(main, margins, scratch):
    rows = main.shape[0]
    scratch[0:rows, :] = margins
    packed = None
    for g, start, _ in groups_of(rows):
        part = scratch[start : start + PACK_ROWS, :]
        part = roll_lanes(part, 16 * g) if g else part
        packed = part if packed is None else packed + part
    return jnp.concatenate([main, packed], 0).astype(bf16)


def margins_of(message, rows):
    packed = message[rows:, :]
    parts = []
    for g, _, size in groups_of(rows):
        part = roll_lanes(packed, N - 16 * g) if g else packed
        parts.append(part[:size])
    return jnp.concatenate(parts, 0)


def window_message(shift_of, slab_delta, slab_beta, scratch):
    tile = slab_delta.shape[0] // 2
    lane = lane_iota(tile)
    mains, margins = [], []
    for ref in (slab_delta, slab_beta):
        main = margin = None
        for z in range(2):
            s = shift_of(z)
            rolled = pltpu.roll(ref[pl.ds(z, tile, stride=2), :], lax.rem(N - s, N), 1)
            source = lane + s
            inside = (source >= 0) & (source < N)
            kept, out_of = jnp.where(inside, rolled, 0.0), jnp.where(inside, 0.0, rolled)
            main = kept if z == 0 else main + kept
            margin = out_of if z == 0 else margin + out_of
        mains.append(main)
        margins.append(margin)
    scratch[2 * tile :, :] = jnp.zeros((scratch.shape[0] - 2 * tile, N), f32)
    return packed_message(jnp.concatenate(mains, 0), jnp.concatenate(margins, 0), scratch)


def first_kernel(
    angles, shifts_in, spots_in, delta, beta, measured_in,
    slab_delta, slab_beta, shifts, out, slot, scalar_shifts, scalar_spots, scratch, sems,
):
    copies = [
        pltpu.make_async_copy(source, target, sems.at[k])
        for k, (source, target) in enumerate(
            [
                (shifts_in, scalar_shifts),
                (spots_in, scalar_spots),
                (delta, slab_delta),
                (beta, slab_beta),
                (measured_in.at[0], slot.at[0:N]),
            ]
        )
    ]
    for copy in copies:
        copy.start()
    me = lax.axis_index("ang")
    for copy in copies[:2]:
        copy.wait()
    for d in range(angles):
        angle = lax.rem(me + d, angles)
        for z in range(2):
            shifts[2 * d + z : 2 * d + z + 1, :] = jnp.full((1, N), scalar_shifts[z, angle], i32)
    slot[N : N + 8, :] = jnp.full((8, N), scalar_spots[0, 0], i32).astype(f32)
    slot[N + 8 :, :] = jnp.full((8, N), scalar_spots[1, 0], i32).astype(f32)
    following = lax.rem(me + 1, angles)
    for copy in copies[2:]:
        copy.wait()
    out[...] = window_message(lambda z: scalar_shifts[z, following], slab_delta, slab_beta, scratch)


def window_kernel(shifts, slab_delta, slab_beta, _, *refs):
    outs, slot, scratch = refs[:-2], refs[-2], refs[-1]
    slot[N:, :] = slot[N:, :] + 0.0
    for k, out in enumerate(outs):
        d = k + 2
        out[...] = window_message(lambda z: shifts[2 * d + z, 0], slab_delta, slab_beta, scratch)


def load_kernel(
    counts_in, shifts, slab_delta, slab_beta, _, spots_in, probe_in, measured_in,
    own, counts, spots, probe, measured, scratch, sems,
):
    copies = [
        pltpu.make_async_copy(source, target, sems.at[k])
        for k, (source, target) in enumerate([(spots_in, spots), (probe_in, probe), (measured_in, measured)])
    ]
    for copy in copies:
        copy.start()
    own[...] = window_message(lambda z: shifts[z, 0], slab_delta, slab_beta, scratch)
    counts[...] = jnp.full(counts.shape, counts_in[0, 0], i32)
    for copy in copies:
        copy.wait()


def slot_position(slot):
    return slot[N, 0].astype(i32), slot[N + 8, 0].astype(i32)


def block_of(column, blocks):
    first, offset = column // N, lax.rem(column, N)
    return first, jnp.minimum(first + 1, blocks - 1), offset


def is_even():
    return lax.rem(lax.axis_index("rows"), 2) == 0


def unpack_kernel(blocks, steps, *refs):
    received, (proj, margins) = refs[: len(steps)], refs[-2:]
    tile = proj.shape[2]
    me = lax.axis_index("ang")
    for d, ref in zip(steps, received):
        block = lax.rem(me + (blocks - d), blocks)
        message = ref[...].astype(f32)
        proj[0, block] = message[:tile]
        proj[1, block] = message[tile : 2 * tile]
        margins[block] = margins_of(message, 2 * tile)


def assemble_kernel(spots, slot, message, proj_in, margins_in, core, cross, proj, margins):
    blocks, tile = proj.shape[1], proj.shape[2]
    unpack_kernel(blocks, [blocks - 1], message, proj, margins)
    lane = lane_iota(tile)
    for block in range(blocks):
        before, after = (block - 1) % blocks, (block + 1) % blocks
        for c in range(2):
            part = slice(c * tile, (c + 1) * tile)
            extra = jnp.where(lane < SHIFT, margins[before, part], 0.0)
            extra += jnp.where(lane >= N - SHIFT, margins[after, part], 0.0)
            proj[c, block] += extra
    _, previous = slot_position(slot)
    own = spots[1, 0]
    lane = lane_iota(N)
    even = is_even()
    for out, upper in ((core, even), (cross, jnp.logical_not(even))):
        first, second, offset = block_of(jnp.where(upper, own, previous), blocks)
        rows = pl.ds(pl.multiple_of(jnp.where(upper, EDGE_ROWS, 0), 8), N)
        pair = patch_of(proj, lane, offset, first, second, rows)
        out[...] = jnp.concatenate(pair, 0).astype(bf16)


def transmit(phase, absorb):
    turns = jnp.round(phase * (1.0 / math.pi))
    r = (phase - turns * 3.140625) - turns * 9.67653589793e-4
    z = r * r
    sine = r + r * z * (-1.66666597e-1 + z * (8.33307858e-3 + z * (-1.98106050e-4 + z * 2.60541672e-6)))
    cosine = 1.0 + z * (
        -0.5 + z * (4.16666418e-2 + z * (-1.38883968e-3 + z * (2.47596343e-5 - z * 2.60512e-7)))
    )
    damping = jnp.exp(-absorb)
    damping = jnp.where((turns.astype(i32) & 1) == 1, -damping, damping)
    return damping * cosine, damping * sine


def split(value):
    high = value.astype(bf16)
    return high, (value - high.astype(f32)).astype(bf16)


def dot(a, b):
    return jnp.dot(a, b, preferred_element_type=f32)


def times_right(value, high, low):
    vh, vl = split(value)
    return dot(vh, high) + (dot(vl, high) + dot(vh, low))


def times_left(high, low, value):
    vh, vl = split(value)
    n = value.shape[1]
    both = dot(high, jnp.concatenate([vh, vl], 1))
    return both[:, :n] + (both[:, n:] + dot(low, vh))


def scan_gradients(patches, measured, weights, probe, tables):
    probe_re, probe_im = probe[0], probe[1]
    right_high, right_low, left_high, left_low = (tables[t] for t in range(4))
    rows = [
        jnp.concatenate([probe_re * re - probe_im * im, probe_re * im + probe_im * re], 1)
        for re, im in patches
    ]
    half = times_right(jnp.concatenate(rows, 0), right_high, right_low)
    count = len(patches)
    stacked = jnp.concatenate(
        [
            jnp.concatenate([half[j * N : (j + 1) * N, part * N : (part + 1) * N] for j in range(count)], 1)
            for part in range(2)
        ],
        0,
    )
    far = times_left(left_high, left_low, stacked)
    far_re, far_im = far[:N], far[N:]
    squared = far_re * far_re + far_im * far_im
    inverse = lax.rsqrt(jnp.maximum(squared, AMP_FLOOR * AMP_FLOOR))
    amplitude = jnp.concatenate([m for m in measured], 1)
    factor = 1.0 - amplitude * inverse
    factor = jnp.concatenate(
        [factor[:, j * N : (j + 1) * N] * weights[j] for j in range(count)], 1
    )
    residual = jnp.concatenate([far_re * factor, far_im * factor], 0)
    half = times_left(right_high, right_low, residual)
    rows = [
        jnp.concatenate([half[:N, j * N : (j + 1) * N], half[N:, j * N : (j + 1) * N]], 1)
        for j in range(count)
    ]
    back = times_right(jnp.concatenate(rows, 0), left_high, left_low)
    grads = []
    for j in range(count):
        re, im = back[j * N : (j + 1) * N, :N], back[j * N : (j + 1) * N, N:]
        grads.append((probe_re * re + probe_im * im, probe_re * im - probe_im * re))
    return grads


def patch_of(values, lane, offset, first, second, rows):
    pair = []
    for c in range(2):
        left = roll_left(values[c, first, rows, :], offset)
        right = roll_left(values[c, second, rows, :], offset)
        pair.append(jnp.where(lane < N - offset, left, right))
    return pair


def chain_back(patch, grad):
    (tr, ti), (gr, gi) = patch, grad
    return tr * gi - ti * gr, -(tr * gr + ti * gi)


def add_patch(total, c, rows, value, lane, offset, first, second):
    placed = roll_lanes(value, offset)
    total[c, first, rows, :] += jnp.where(lane >= offset, placed, 0.0)
    total[c, second, rows, :] += jnp.where(lane < offset, placed, 0.0)


def edge_patch(is_own, spots, slot, halo, trans, patch):
    blocks, tile = trans.shape[1], trans.shape[2]
    prev_row, prev_column = slot_position(slot)
    columns = block_of(jnp.where(is_own, spots[1, 0], prev_column), blocks)
    start = jnp.where(is_own, spots[0, 0], jnp.maximum(prev_row, EDGE_ROWS))
    first, second, offset = columns
    here = pl.ds(pl.multiple_of(jnp.where(is_own, 0, tile), 8), tile)
    there = pl.ds(pl.multiple_of(jnp.where(is_own, tile, EDGE_ROWS), 8), N)
    last = lax.axis_index("rows") == lax.axis_size("rows") - 1
    value = jnp.where(is_own & last, 0.0, halo[...].astype(f32))
    outside = transmit(value[:N], value[N:])
    inside = patch_of(trans, lane_iota(tile), offset, first, second, slice(None))
    for c in range(2):
        patch[c, here, :] = inside[c]
        patch[c, there, :] = outside[c]
    pair = [patch[c, pl.ds(start, N), :] for c in range(2)]
    return pair, columns, jnp.where(is_own, start, start - tile)


def edge_weight(is_own, counts, slot):
    prev_row, _ = slot_position(slot)
    reaches = (prev_row > EDGE_ROWS) & (lax.axis_index("rows") > 0)
    return jnp.where(jnp.where(is_own, counts[0, 0] > 0, reaches), 1.0, 0.0).astype(f32)


def add_edge(total, chained, columns, place, frame):
    tile = total.shape[2]
    first, second, offset = columns
    for c in range(2):
        frame[c, 0:tile, :] = jnp.zeros((tile, N), f32)
        frame[c, tile : tile + N, :] = chained[c]
        frame[c, tile + N :, :] = jnp.zeros((tile, N), f32)
        rows = frame[c, pl.ds(tile - place, tile), :]
        add_patch(total, c, slice(None), rows, lane_iota(tile), offset, first, second)


def inner_kernel(spots, counts, proj, slot0, core, probe, measured, tables, trans, grad, patch, frame, edge_frame):
    blocks, tile = proj.shape[1], proj.shape[2]
    for block in range(blocks):
        re, im = transmit(proj[0, block], proj[1, block])
        trans[0, block] = re
        trans[1, block] = im
    grad[...] = jnp.zeros(grad.shape, f32)
    frame[0:SHIFT, :] = jnp.zeros((SHIFT, N), f32)
    frame[SHIFT + N :, :] = jnp.zeros((SHIFT, N), f32)
    slots = measured.shape[0]
    lane = lane_iota(N)
    is_own = is_even()
    pair, columns, place = edge_patch(is_own, spots, slot0, core, trans, patch)
    patches, weights = [pair], [edge_weight(is_own, counts, slot0)]
    patterns = [jnp.where(is_own, measured[0], slot0[0:N, :])]
    for slot in range(1, slots):
        row = jnp.minimum(spots[0, slot], EDGE_ROWS)
        first, second, offset = block_of(spots[1, slot], blocks)
        patches.append(patch_of(trans, lane, offset, first, second, pl.ds(row, N)))
        weights.append(jnp.where(slot < counts[0, 0], 1.0, 0.0).astype(f32))
        patterns.append(measured[slot])
    grads = scan_gradients(patches, patterns, weights, probe, tables)
    add_edge(grad, chain_back(patches[0], grads[0]), columns, place, edge_frame)
    lane = lane_iota(tile)
    for slot in range(1, slots):
        row = jnp.minimum(spots[0, slot], EDGE_ROWS)
        first, second, offset = block_of(spots[1, slot], blocks)
        chained = chain_back(patches[slot], grads[slot])
        for c in range(2):
            frame[SHIFT : SHIFT + N, :] = chained[c]
            add_patch(grad, c, slice(None), frame[pl.ds(SHIFT - row, tile), :], lane, offset, first, second)


def gradient_message(block, total, scratch):
    blocks, tile = total.shape[1], total.shape[2]
    scratch[2 * tile :, :] = jnp.zeros((scratch.shape[0] - 2 * tile, N), f32)
    lane = lane_iota(tile)
    before, after = lax.rem(block + (blocks - 1), blocks), lax.rem(block + 1, blocks)
    mains, margins = [], []
    for c in range(2):
        mains.append(total[c, block])
        margin = jnp.where(lane < SHIFT, total[c, after], 0.0)
        margins.append(jnp.where(lane >= N - SHIFT, total[c, before], margin))
    return packed_message(jnp.concatenate(mains, 0), jnp.concatenate(margins, 0), scratch)


def edge_kernel(spots, counts, slot0, cross, trans, _, probe, measured, tables, *refs):
    outs, (total, patch, frame, scratch) = refs[:-4], refs[-4:]
    blocks = trans.shape[1]
    is_own = jnp.logical_not(is_even())
    pair, columns, place = edge_patch(is_own, spots, slot0, cross, trans, patch)
    pattern = jnp.where(is_own, measured[0], slot0[0:N, :])
    weight = edge_weight(is_own, counts, slot0)
    grads = scan_gradients([pair], [pattern], [weight], probe, tables)
    add_edge(total, chain_back(pair, grads[0]), columns, place, frame)
    me = lax.axis_index("ang")
    for k, out in enumerate(outs):
        out[...] = gradient_message(lax.rem(me + k + 1, blocks), total, scratch)


def own_kernel(total, _, out, scratch):
    out[...] = gradient_message(lax.axis_index("ang"), total, scratch)


def slab_kernel(angles, steps, last, shifts, *refs):
    refs, outs = (refs[:-2], refs[-2:]) if last else (refs[:-1], refs[-1:])
    received, before = refs[: len(steps)], refs[len(steps) :]
    tile = (received[0].shape[0] - PACK_ROWS) // 2
    lane = lane_iota(tile)
    sums = [[before[0][c, z] if before else None for z in range(2)] for c in range(2)]
    for d, ref in zip(steps, received):
        message = ref[...].astype(f32)
        margins = margins_of(message, 2 * tile)
        for z in range(2):
            s = shifts[2 * ((angles - d) % angles) + z, 0]
            target = lane + s
            inside = (target >= 0) & (target < N)
            for c in range(2):
                part = slice(c * tile, (c + 1) * tile)
                value = jnp.where(inside, message[part], margins[part])
                value = pltpu.roll(value, lax.rem(s + N, N), 1)
                sums[c][z] = value if sums[c][z] is None else sums[c][z] + value
    for c in range(2):
        for z in range(2):
            if last:
                outs[c][pl.ds(z, tile, stride=2), :] = sums[c][z]
            else:
                outs[0][c, z] = sums[c][z]


def call(kernel, ins, outs, scratch=(), flops=0, bytes_accessed=0, aliases=()):
    scratch = [pltpu.VMEM(item, f32) if isinstance(item, tuple) else item for item in scratch]
    return pl.pallas_call(
        kernel,
        in_specs=ins,
        out_specs=[VMEM] * len(outs),
        out_shape=[jax.ShapeDtypeStruct(shape, dtype) for shape, dtype in outs],
        scratch_shapes=scratch,
        input_output_aliases=dict(aliases),
        compiler_params=pltpu.CompilerParams(vmem_limit_bytes=32 * 1024 * 1024),
        cost_estimate=pl.CostEstimate(flops=flops, bytes_accessed=bytes_accessed, transcendentals=0),
    )


def exchange(messages):
    count = lax.axis_size("ang")
    received = [messages[0]]
    for d in range(1, count):
        received.append(lax.ppermute(messages[d], "ang", [(i, (i + d) % count) for i in range(count)]))
    return received


def on_rows(value, target):
    count = lax.axis_size("rows")
    return lax.ppermute(value, "rows", [(i, target(i) % count) for i in range(count)])


def across_chips(value):
    rows, angles = lax.axis_size("rows"), lax.axis_size("ang")
    pairs = []
    for i in range(rows):
        for a in range(angles):
            if i not in (0, rows - 1):
                target = (i + 1 if i % 2 else i - 1, a)
            elif angles % 2:
                target = (rows - 1 - i, a)
            else:
                target = (i, a ^ 1)
            pairs.append((i * angles + a, target[0] * angles + target[1]))
    return lax.ppermute(value, ("rows", "ang"), pairs)


def on_device(delta_obj, beta_obj, layer_shifts, illumination_field, amplitudes, positions, scan_counts):
    tile = delta_obj.shape[0]
    angles = lax.axis_size("ang")
    message = ((2 * tile + PACK_ROWS, N), bf16)
    padded = (len(groups_of(2 * tile)) * PACK_ROWS, N)
    field = ((2, angles, tile, N), f32)
    slab = (2 * tile, N)
    halo = ((2 * N, N), bf16)
    tables = jnp.asarray(fourier_tables())

    in_hbm = functools.partial(pltpu.with_memory_space_constraint, memory_space=pltpu.HBM)
    shifts, spots, probe, measured = (
        in_hbm(value) for value in (layer_shifts.T, positions[0].T, illumination_field, amplitudes[0])
    )
    slab_delta, slab_beta, shifts, following, slot = call(
        functools.partial(first_kernel, angles),
        [HBM] * 5,
        [(slab, f32), (slab, f32), ((2 * angles, N), i32), message, ((N + 16, N), f32)],
        [pltpu.SMEM(shifts.shape, i32), pltpu.SMEM(spots.shape, i32), padded, pltpu.SemaphoreType.DMA((5,))],
    )(shifts, spots, in_hbm(delta_obj.reshape(slab)), in_hbm(beta_obj.reshape(slab)), measured)
    *others, slot = call(
        window_kernel, [VMEM] * 4, [message] * (angles - 2) + [((N + 16, N), f32)], [padded], aliases={3: angles - 2}
    )(shifts, slab_delta, slab_beta, slot)
    own, counts, spots, probe, measured = call(
        load_kernel,
        [SMEM] + [VMEM] * 4 + [HBM] * 3,
        [message, ((8, N), i32)] + [(value.shape, value.dtype) for value in (spots, probe, measured)],
        [padded, pltpu.SemaphoreType.DMA((3,))],
        flops=10**9,
        bytes_accessed=10**6,
    )(scan_counts, shifts, slab_delta, slab_beta, others[-1], spots, probe, measured)
    windows = [own, following, *others]
    received = exchange(windows)
    previous = on_rows(slot, lambda i: i + 1)
    rows = ((angles, 2 * tile, N), f32)
    early = list(range(angles - 1))
    partly = call(
        functools.partial(unpack_kernel, angles, early),
        [VMEM] * (angles - 1),
        [field, rows],
        flops=10**9,
        bytes_accessed=10**6,
    )(*received[:-1])
    core, cross, proj, _ = call(
        assemble_kernel, [VMEM] * 5, [halo, halo, field, rows], aliases={3: 2, 4: 3}
    )(spots, previous, received[-1], *partly)
    core = on_rows(core, lambda i: i ^ 1)
    cross = across_chips(cross)
    patch, frame = (2, 2 * tile, N), (2, 2 * tile + N, N)
    trans, inner = call(
        inner_kernel,
        [VMEM] * 8,
        [field, field],
        [patch, (N + 2 * SHIFT, N), frame],
        flops=3 * 10**9,
        bytes_accessed=3 * 10**6,
    )(spots, counts, proj, previous, core, probe, measured, tables)
    *outgoing, total = call(
        edge_kernel,
        [VMEM] * 9,
        [message] * (angles - 1) + [field],
        [patch, frame, padded],
        aliases={5: angles - 1},
    )(spots, counts, previous, cross, trans, inner, probe, measured, tables)
    own = call(own_kernel, [VMEM] * 2, [message], [padded])(total, outgoing[-1])[0]
    received = exchange([own, *outgoing])
    early = list(range(angles - 1))
    sums = call(
        functools.partial(slab_kernel, angles, early, False),
        [VMEM] * angles,
        [((2, 2, tile, N), f32)],
        flops=10**9,
        bytes_accessed=10**6,
    )(shifts, *received[:-1])[0]
    grad_delta, grad_beta = call(
        functools.partial(slab_kernel, angles, [angles - 1], True), [VMEM] * 3, [(slab, f32)] * 2
    )(shifts, received[-1], sums)
    return grad_delta.reshape(tile, 2, N), grad_beta.reshape(tile, 2, N)


def solution(mesh):
    placed = (
        P("rows", None, "ang"),
        P("rows", None, "ang"),
        P(),
        P(),
        P("ang", "rows", None, None),
        P("ang", "rows", None),
        P("ang", "rows"),
    )
    return jax.shard_map(
        on_device,
        mesh=mesh,
        in_specs=placed,
        out_specs=(P("rows", None, "ang"), P("rows", None, "ang")),
        check_vma=False,
    )
```

```python
import functools
import math

import jax
import jax.numpy as jnp
import ml_dtypes
import numpy as np
from jax import lax
from jax.experimental import pallas as pl
from jax.experimental.pallas import tpu as pltpu
from jax.sharding import PartitionSpec as P

N = 128
SHIFT = 8
AMP_FLOOR = 0.1
PACK_ROWS = 40
EDGE_ROWS = 8

f32, bf16, i32 = jnp.float32, jnp.bfloat16, jnp.int32
VMEM = pl.BlockSpec(memory_space=pltpu.VMEM)
SMEM = pl.BlockSpec(memory_space=pltpu.SMEM)
HBM = pl.BlockSpec(memory_space=pltpu.HBM)


def fourier_tables():
    counter = np.arange(N)
    angle = (counter[:, None] * counter[None, :] % N) * (2.0 * math.pi / N)
    re, im = np.cos(angle) / math.sqrt(N), -np.sin(angle) / math.sqrt(N)
    right = np.block([[re, im], [-im, re]])
    tables = []
    for table in (right, right.T):
        high = table.astype(ml_dtypes.bfloat16)
        tables += [high, (table - high.astype(np.float64)).astype(ml_dtypes.bfloat16)]
    return np.stack(tables)


def lane_iota(rows):
    return lax.broadcasted_iota(i32, (rows, N), 1)


def roll_lanes(value, by):
    return pltpu.roll(value, by, 1)


def roll_left(value, by):
    return pltpu.roll(value, lax.rem(N - by, N), 1)


def groups_of(rows):
    return [(g, start, min(PACK_ROWS, rows - start)) for g, start in enumerate(range(0, rows, PACK_ROWS))]


def packed_message(main, margins, scratch):
    rows = main.shape[0]
    scratch[0:rows, :] = margins
    packed = None
    for g, start, _ in groups_of(rows):
        part = scratch[start : start + PACK_ROWS, :]
        part = roll_lanes(part, 16 * g) if g else part
        packed = part if packed is None else packed + part
    return jnp.concatenate([main, packed], 0).astype(bf16)


def margins_of(message, rows):
    packed = message[rows:, :]
    parts = []
    for g, _, size in groups_of(rows):
        part = roll_lanes(packed, N - 16 * g) if g else packed
        parts.append(part[:size])
    return jnp.concatenate(parts, 0)


def window_message(shift_of, slab_delta, slab_beta, scratch):
    tile = slab_delta.shape[0] // 2
    lane = lane_iota(tile)
    mains, margins = [], []
    for ref in (slab_delta, slab_beta):
        main = margin = None
        for z in range(2):
            s = shift_of(z)
            rolled = pltpu.roll(ref[pl.ds(z, tile, stride=2), :], lax.rem(N - s, N), 1)
            source = lane + s
            inside = (source >= 0) & (source < N)
            kept, out_of = jnp.where(inside, rolled, 0.0), jnp.where(inside, 0.0, rolled)
            main = kept if z == 0 else main + kept
            margin = out_of if z == 0 else margin + out_of
        mains.append(main)
        margins.append(margin)
    scratch[2 * tile :, :] = jnp.zeros((scratch.shape[0] - 2 * tile, N), f32)
    return packed_message(jnp.concatenate(mains, 0), jnp.concatenate(margins, 0), scratch)


def first_kernel(
    angles, shifts_in, spots_in, delta, beta, measured_in,
    slab_delta, slab_beta, shifts, out, slot, scalar_shifts, scalar_spots, scratch, sems,
):
    copies = [
        pltpu.make_async_copy(source, target, sems.at[k])
        for k, (source, target) in enumerate(
            [
                (shifts_in, scalar_shifts),
                (spots_in, scalar_spots),
                (delta, slab_delta),
                (beta, slab_beta),
                (measured_in.at[0], slot.at[0:N]),
            ]
        )
    ]
    for copy in copies:
        copy.start()
    me = lax.axis_index("ang")
    for copy in copies[:2]:
        copy.wait()
    for d in range(angles):
        angle = lax.rem(me + d, angles)
        for z in range(2):
            shifts[2 * d + z : 2 * d + z + 1, :] = jnp.full((1, N), scalar_shifts[z, angle], i32)
    slot[N : N + 8, :] = jnp.full((8, N), scalar_spots[0, 0], i32).astype(f32)
    slot[N + 8 :, :] = jnp.full((8, N), scalar_spots[1, 0], i32).astype(f32)
    following = lax.rem(me + 1, angles)
    for copy in copies[2:]:
        copy.wait()
    out[...] = window_message(lambda z: scalar_shifts[z, following], slab_delta, slab_beta, scratch)


def window_kernel(shifts, slab_delta, slab_beta, _, *refs):
    outs, slot, scratch = refs[:-2], refs[-2], refs[-1]
    slot[N:, :] = slot[N:, :] + 0.0
    for k, out in enumerate(outs):
        d = k + 2
        out[...] = window_message(lambda z: shifts[2 * d + z, 0], slab_delta, slab_beta, scratch)


def load_kernel(
    counts_in, shifts, slab_delta, slab_beta, _, spots_in, probe_in, measured_in,
    own, counts, spots, probe, measured, scratch, sems,
):
    copies = [
        pltpu.make_async_copy(source, target, sems.at[k])
        for k, (source, target) in enumerate([(spots_in, spots), (probe_in, probe), (measured_in, measured)])
    ]
    for copy in copies:
        copy.start()
    own[...] = window_message(lambda z: shifts[z, 0], slab_delta, slab_beta, scratch)
    counts[...] = jnp.full(counts.shape, counts_in[0, 0], i32)
    for copy in copies:
        copy.wait()


def slot_position(slot):
    return slot[N, 0].astype(i32), slot[N + 8, 0].astype(i32)


def block_of(column, blocks):
    first, offset = column // N, lax.rem(column, N)
    return first, jnp.minimum(first + 1, blocks - 1), offset


def is_even():
    return lax.rem(lax.axis_index("rows"), 2) == 0


def unpack(message, block, proj, margins):
    tile = proj.shape[2]
    message = message.astype(f32)
    proj[0, block] = message[:tile]
    proj[1, block] = message[tile : 2 * tile]
    margins[block] = margins_of(message, 2 * tile)


def add_margins(proj, margins, block, before=None, after=None):
    tile = proj.shape[2]
    lane = lane_iota(tile)
    for c in range(2):
        part = slice(c * tile, (c + 1) * tile)
        value = proj[c, block]
        if before is not None:
            value += jnp.where(lane < SHIFT, margins[before, part], 0.0)
        if after is not None:
            value += jnp.where(lane >= N - SHIFT, margins[after, part], 0.0)
        proj[c, block] = value


def unpack_kernel(*refs):
    received, (proj, margins) = refs[:-2], refs[-2:]
    count = proj.shape[1]
    me = lax.axis_index("ang")
    blocks = [lax.rem(me + (count - d), count) for d in range(count)]
    for block, ref in zip(blocks, received):
        unpack(ref[...], block, proj, margins)
    for d in range(count - 1):
        before = blocks[d + 1] if d < count - 2 else None
        after = blocks[d - 1] if d > 0 else None
        add_margins(proj, margins, blocks[d], before, after)


def assemble_kernel(spots, slot, message, proj_in, margins_in, core, cross, proj, margins):
    blocks = proj.shape[1]
    me = lax.axis_index("ang")
    last, following = lax.rem(me + 1, blocks), lax.rem(me + 2, blocks)
    _, previous = slot_position(slot)
    own = spots[1, 0]
    even = is_even()
    places = [
        (out, upper, block_of(jnp.where(upper, own, previous), blocks))
        for out, upper in ((core, even), (cross, jnp.logical_not(even)))
    ]
    unpack(message[...], last, proj, margins)
    add_margins(proj, margins, last, me, following)
    add_margins(proj, margins, me, None, last)
    add_margins(proj, margins, following, last, None)
    lane = lane_iota(N)
    for out, upper, (first, second, offset) in places:
        rows = pl.ds(pl.multiple_of(jnp.where(upper, EDGE_ROWS, 0), 8), N)
        pair = patch_of(proj, lane, offset, first, second, rows)
        out[...] = jnp.concatenate(pair, 0).astype(bf16)


def transmit(phase, absorb):
    turns = jnp.round(phase * (1.0 / math.pi))
    r = (phase - turns * 3.140625) - turns * 9.67653589793e-4
    z = r * r
    sine = r + r * z * (-1.66666597e-1 + z * (8.33307858e-3 + z * (-1.98106050e-4 + z * 2.60541672e-6)))
    cosine = 1.0 + z * (
        -0.5 + z * (4.16666418e-2 + z * (-1.38883968e-3 + z * (2.47596343e-5 - z * 2.60512e-7)))
    )
    damping = jnp.exp(-absorb)
    damping = jnp.where((turns.astype(i32) & 1) == 1, -damping, damping)
    return damping * cosine, damping * sine


def split(value):
    high = value.astype(bf16)
    return high, (value - high.astype(f32)).astype(bf16)


def dot(a, b):
    return jnp.dot(a, b, preferred_element_type=f32)


def times_right(value, high, low):
    vh, vl = split(value)
    return dot(vh, high) + (dot(vl, high) + dot(vh, low))


def times_left(high, low, value):
    vh, vl = split(value)
    n = value.shape[1]
    both = dot(high, jnp.concatenate([vh, vl], 1))
    return both[:, :n] + (both[:, n:] + dot(low, vh))


def scan_gradients(patches, measured, weights, probe, tables):
    probe_re, probe_im = probe[0], probe[1]
    right_high, right_low, left_high, left_low = (tables[t] for t in range(4))
    rows = [
        jnp.concatenate([probe_re * re - probe_im * im, probe_re * im + probe_im * re], 1)
        for re, im in patches
    ]
    half = times_right(jnp.concatenate(rows, 0), right_high, right_low)
    count = len(patches)
    stacked = jnp.concatenate(
        [
            jnp.concatenate([half[j * N : (j + 1) * N, part * N : (part + 1) * N] for j in range(count)], 1)
            for part in range(2)
        ],
        0,
    )
    far = times_left(left_high, left_low, stacked)
    far_re, far_im = far[:N], far[N:]
    squared = far_re * far_re + far_im * far_im
    inverse = lax.rsqrt(jnp.maximum(squared, AMP_FLOOR * AMP_FLOOR))
    amplitude = jnp.concatenate([m for m in measured], 1)
    factor = 1.0 - amplitude * inverse
    factor = jnp.concatenate(
        [factor[:, j * N : (j + 1) * N] * weights[j] for j in range(count)], 1
    )
    residual = jnp.concatenate([far_re * factor, far_im * factor], 0)
    half = times_left(right_high, right_low, residual)
    rows = [
        jnp.concatenate([half[:N, j * N : (j + 1) * N], half[N:, j * N : (j + 1) * N]], 1)
        for j in range(count)
    ]
    back = times_right(jnp.concatenate(rows, 0), left_high, left_low)
    grads = []
    for j in range(count):
        re, im = back[j * N : (j + 1) * N, :N], back[j * N : (j + 1) * N, N:]
        grads.append((probe_re * re + probe_im * im, probe_re * im - probe_im * re))
    return grads


def patch_of(values, lane, offset, first, second, rows):
    pair = []
    for c in range(2):
        left = roll_left(values[c, first, rows, :], offset)
        right = roll_left(values[c, second, rows, :], offset)
        pair.append(jnp.where(lane < N - offset, left, right))
    return pair


def chain_back(patch, grad):
    (tr, ti), (gr, gi) = patch, grad
    return tr * gi - ti * gr, -(tr * gr + ti * gi)


def add_patch(total, c, rows, value, lane, offset, first, second):
    placed = roll_lanes(value, offset)
    total[c, first, rows, :] += jnp.where(lane >= offset, placed, 0.0)
    total[c, second, rows, :] += jnp.where(lane < offset, placed, 0.0)


def edge_patch(is_own, spots, slot, halo, trans, patch):
    blocks, tile = trans.shape[1], trans.shape[2]
    prev_row, prev_column = slot_position(slot)
    columns = block_of(jnp.where(is_own, spots[1, 0], prev_column), blocks)
    start = jnp.where(is_own, spots[0, 0], jnp.maximum(prev_row, EDGE_ROWS))
    first, second, offset = columns
    here = pl.ds(pl.multiple_of(jnp.where(is_own, 0, tile), 8), tile)
    there = pl.ds(pl.multiple_of(jnp.where(is_own, tile, EDGE_ROWS), 8), N)
    last = lax.axis_index("rows") == lax.axis_size("rows") - 1
    value = jnp.where(is_own & last, 0.0, halo[...].astype(f32))
    outside = transmit(value[:N], value[N:])
    inside = patch_of(trans, lane_iota(tile), offset, first, second, slice(None))
    for c in range(2):
        patch[c, here, :] = inside[c]
        patch[c, there, :] = outside[c]
    pair = [patch[c, pl.ds(start, N), :] for c in range(2)]
    return pair, columns, jnp.where(is_own, start, start - tile)


def edge_weight(is_own, counts, slot):
    prev_row, _ = slot_position(slot)
    reaches = (prev_row > EDGE_ROWS) & (lax.axis_index("rows") > 0)
    return jnp.where(jnp.where(is_own, counts[0, 0] > 0, reaches), 1.0, 0.0).astype(f32)


def add_edge(total, chained, columns, place, frame):
    tile = total.shape[2]
    first, second, offset = columns
    for c in range(2):
        frame[c, 0:tile, :] = jnp.zeros((tile, N), f32)
        frame[c, tile : tile + N, :] = chained[c]
        frame[c, tile + N :, :] = jnp.zeros((tile, N), f32)
        rows = frame[c, pl.ds(tile - place, tile), :]
        add_patch(total, c, slice(None), rows, lane_iota(tile), offset, first, second)


def inner_kernel(spots, counts, proj, slot0, core, probe, measured, tables, trans, grad, patch, frame, edge_frame):
    blocks, tile = proj.shape[1], proj.shape[2]
    slots = measured.shape[0]
    inner = [
        (jnp.minimum(spots[0, slot], EDGE_ROWS), *block_of(spots[1, slot], blocks)) for slot in range(1, slots)
    ]
    for block in range(blocks):
        re, im = transmit(proj[0, block], proj[1, block])
        trans[0, block] = re
        trans[1, block] = im
    grad[...] = jnp.zeros(grad.shape, f32)
    frame[0:SHIFT, :] = jnp.zeros((SHIFT, N), f32)
    frame[SHIFT + N :, :] = jnp.zeros((SHIFT, N), f32)
    lane = lane_iota(N)
    is_own = is_even()
    pair, columns, place = edge_patch(is_own, spots, slot0, core, trans, patch)
    patches, weights = [pair], [edge_weight(is_own, counts, slot0)]
    patterns = [jnp.where(is_own, measured[0], slot0[0:N, :])]
    for slot in range(1, slots):
        row, first, second, offset = inner[slot - 1]
        patches.append(patch_of(trans, lane, offset, first, second, pl.ds(row, N)))
        weights.append(jnp.where(slot < counts[0, 0], 1.0, 0.0).astype(f32))
        patterns.append(measured[slot])
    grads = scan_gradients(patches, patterns, weights, probe, tables)
    add_edge(grad, chain_back(patches[0], grads[0]), columns, place, edge_frame)
    lane = lane_iota(tile)
    for slot in range(1, slots):
        row, first, second, offset = inner[slot - 1]
        chained = chain_back(patches[slot], grads[slot])
        for c in range(2):
            frame[SHIFT : SHIFT + N, :] = chained[c]
            add_patch(grad, c, slice(None), frame[pl.ds(SHIFT - row, tile), :], lane, offset, first, second)


def gradient_message(block, total, scratch):
    blocks, tile = total.shape[1], total.shape[2]
    scratch[2 * tile :, :] = jnp.zeros((scratch.shape[0] - 2 * tile, N), f32)
    lane = lane_iota(tile)
    before, after = lax.rem(block + (blocks - 1), blocks), lax.rem(block + 1, blocks)
    mains, margins = [], []
    for c in range(2):
        mains.append(total[c, block])
        margin = jnp.where(lane < SHIFT, total[c, after], 0.0)
        margins.append(jnp.where(lane >= N - SHIFT, total[c, before], margin))
    return packed_message(jnp.concatenate(mains, 0), jnp.concatenate(margins, 0), scratch)


def edge_kernel(spots, counts, slot0, cross, trans, _, probe, measured, tables, *refs):
    out, total, patch, frame, scratch = refs
    blocks = trans.shape[1]
    is_own = jnp.logical_not(is_even())
    weight = edge_weight(is_own, counts, slot0)
    pair, columns, place = edge_patch(is_own, spots, slot0, cross, trans, patch)
    pattern = jnp.where(is_own, measured[0], slot0[0:N, :])
    grads = scan_gradients([pair], [pattern], [weight], probe, tables)
    add_edge(total, chain_back(pair, grads[0]), columns, place, frame)
    following = lax.rem(lax.axis_index("ang") + 1, blocks)
    out[...] = gradient_message(following, total, scratch)


def cut_kernel(total, *refs):
    outs, scratch = refs[:-1], refs[-1]
    blocks = total.shape[1]
    me = lax.axis_index("ang")
    for k, out in enumerate(outs):
        out[...] = gradient_message(lax.rem(me + k + 2, blocks), total, scratch)


def own_kernel(total, _, out, scratch):
    out[...] = gradient_message(lax.axis_index("ang"), total, scratch)


def slab_kernel(angles, steps, last, shifts, *refs):
    refs, outs = (refs[:-2], refs[-2:]) if last else (refs[:-1], refs[-1:])
    received, before = refs[: len(steps)], refs[len(steps) :]
    tile = (received[0].shape[0] - PACK_ROWS) // 2
    lane = lane_iota(tile)
    sums = [[before[0][c, z] if before else None for z in range(2)] for c in range(2)]
    for d, ref in zip(steps, received):
        message = ref[...].astype(f32)
        margins = margins_of(message, 2 * tile)
        for z in range(2):
            s = shifts[2 * ((angles - d) % angles) + z, 0]
            target = lane + s
            inside = (target >= 0) & (target < N)
            for c in range(2):
                part = slice(c * tile, (c + 1) * tile)
                value = jnp.where(inside, message[part], margins[part])
                value = pltpu.roll(value, lax.rem(s + N, N), 1)
                sums[c][z] = value if sums[c][z] is None else sums[c][z] + value
    for c in range(2):
        for z in range(2):
            if last:
                outs[c][pl.ds(z, tile, stride=2), :] = sums[c][z]
            else:
                outs[0][c, z] = sums[c][z]


def call(kernel, ins, outs, scratch=(), flops=0, bytes_accessed=0, aliases=()):
    scratch = [pltpu.VMEM(item, f32) if isinstance(item, tuple) else item for item in scratch]
    return pl.pallas_call(
        kernel,
        in_specs=ins,
        out_specs=[VMEM] * len(outs),
        out_shape=[jax.ShapeDtypeStruct(shape, dtype) for shape, dtype in outs],
        scratch_shapes=scratch,
        input_output_aliases=dict(aliases),
        compiler_params=pltpu.CompilerParams(vmem_limit_bytes=32 * 1024 * 1024),
        cost_estimate=pl.CostEstimate(flops=flops, bytes_accessed=bytes_accessed, transcendentals=0),
    )


def exchange(messages):
    count = lax.axis_size("ang")
    received = [messages[0]]
    for d in range(1, count):
        received.append(lax.ppermute(messages[d], "ang", [(i, (i + d) % count) for i in range(count)]))
    return received


def on_rows(value, target):
    count = lax.axis_size("rows")
    return lax.ppermute(value, "rows", [(i, target(i) % count) for i in range(count)])


def across_chips(value):
    rows, angles = lax.axis_size("rows"), lax.axis_size("ang")
    pairs = []
    for i in range(rows):
        for a in range(angles):
            if i not in (0, rows - 1):
                target = (i + 1 if i % 2 else i - 1, a)
            elif angles % 2:
                target = (rows - 1 - i, a)
            else:
                target = (i, a ^ 1)
            pairs.append((i * angles + a, target[0] * angles + target[1]))
    return lax.ppermute(value, ("rows", "ang"), pairs)


def on_device(delta_obj, beta_obj, layer_shifts, illumination_field, amplitudes, positions, scan_counts):
    tile = delta_obj.shape[0]
    angles = lax.axis_size("ang")
    message = ((2 * tile + PACK_ROWS, N), bf16)
    padded = (len(groups_of(2 * tile)) * PACK_ROWS, N)
    field = ((2, angles, tile, N), f32)
    slab = (2 * tile, N)
    halo = ((2 * N, N), bf16)
    tables = jnp.asarray(fourier_tables())

    in_hbm = functools.partial(pltpu.with_memory_space_constraint, memory_space=pltpu.HBM)
    shifts, spots, probe, measured = (
        in_hbm(value) for value in (layer_shifts.T, positions[0].T, illumination_field, amplitudes[0])
    )
    slab_delta, slab_beta, shifts, following, slot = call(
        functools.partial(first_kernel, angles),
        [HBM] * 5,
        [(slab, f32), (slab, f32), ((2 * angles, N), i32), message, ((N + 16, N), f32)],
        [pltpu.SMEM(shifts.shape, i32), pltpu.SMEM(spots.shape, i32), padded, pltpu.SemaphoreType.DMA((5,))],
    )(shifts, spots, in_hbm(delta_obj.reshape(slab)), in_hbm(beta_obj.reshape(slab)), measured)
    *others, slot = call(
        window_kernel, [VMEM] * 4, [message] * (angles - 2) + [((N + 16, N), f32)], [padded], aliases={3: angles - 2}
    )(shifts, slab_delta, slab_beta, slot)
    own, counts, spots, probe, measured = call(
        load_kernel,
        [SMEM] + [VMEM] * 4 + [HBM] * 3,
        [message, ((8, N), i32)] + [(value.shape, value.dtype) for value in (spots, probe, measured)],
        [padded, pltpu.SemaphoreType.DMA((3,))],
        flops=10**9,
        bytes_accessed=10**6,
    )(scan_counts, shifts, slab_delta, slab_beta, others[-1], spots, probe, measured)
    windows = [own, following, *others]
    received = exchange(windows)
    previous = on_rows(slot, lambda i: i + 1)
    rows = ((angles, 2 * tile, N), f32)
    partly = call(
        unpack_kernel,
        [VMEM] * (angles - 1),
        [field, rows],
        flops=10**9,
        bytes_accessed=10**6,
    )(*received[:-1])
    core, cross, proj, _ = call(
        assemble_kernel, [VMEM] * 5, [halo, halo, field, rows], aliases={3: 2, 4: 3}
    )(spots, previous, received[-1], *partly)
    core = on_rows(core, lambda i: i ^ 1)
    cross = across_chips(cross)
    patch, frame = (2, 2 * tile, N), (2, 2 * tile + N, N)
    trans, inner = call(
        inner_kernel,
        [VMEM] * 8,
        [field, field],
        [patch, (N + 2 * SHIFT, N), frame],
        flops=3 * 10**9,
        bytes_accessed=3 * 10**6,
    )(spots, counts, proj, previous, core, probe, measured, tables)
    following, total = call(
        edge_kernel,
        [VMEM] * 9,
        [message, field],
        [patch, frame, padded],
        aliases={5: 1},
    )(spots, counts, previous, cross, trans, inner, probe, measured, tables)
    outgoing = [following, *call(cut_kernel, [VMEM], [message] * (angles - 2), [padded])(total)]
    own = call(own_kernel, [VMEM] * 2, [message], [padded])(total, outgoing[-1])[0]
    received = exchange([own, *outgoing])
    early = list(range(angles - 1))
    sums = call(
        functools.partial(slab_kernel, angles, early, False),
        [VMEM] * angles,
        [((2, 2, tile, N), f32)],
        flops=10**9,
        bytes_accessed=10**6,
    )(shifts, *received[:-1])[0]
    grad_delta, grad_beta = call(
        functools.partial(slab_kernel, angles, [angles - 1], True), [VMEM] * 3, [(slab, f32)] * 2
    )(shifts, received[-1], sums)
    return grad_delta.reshape(tile, 2, N), grad_beta.reshape(tile, 2, N)


def solution(mesh):
    placed = (
        P("rows", None, "ang"),
        P("rows", None, "ang"),
        P(),
        P(),
        P("ang", "rows", None, None),
        P("ang", "rows", None),
        P("ang", "rows"),
    )
    return jax.shard_map(
        on_device,
        mesh=mesh,
        in_specs=placed,
        out_specs=(P("rows", None, "ang"), P("rows", None, "ang")),
        check_vma=False,
    )
```
